128 devices in a mesh: frame: 8 (over x_hi, y), pos: 16 (over x_lo, z, core).
Axes of the slice: x: 4 (x_hi: 2, x_lo: 2; x = x_hi * 2 + x_lo), y: 4, z: 4, core: 2. Of those that a mesh axis runs over, the one named last changes fastest.
Arguments:
- inputs: bfloat16 [16, 1536, 1152], P('frame', 'pos'), may hold values from -6 to 6
- cotangent: bfloat16 [16, 1536, 1152], P('frame', 'pos'), may hold values from -6 to 6
- space_projection: bfloat16 [3456, 1152], replicated, may hold values from -2 to 2
- space_output: bfloat16 [1152, 1152], replicated, may hold values from -0.1875 to 0.1875
- time_projection: bfloat16 [3456, 1152], replicated, may hold values from -2 to 2
- time_output: bfloat16 [1152, 1152], replicated, may hold values from -0.1875 to 0.1875
Outputs:
- input_grad: bfloat16 [16, 1536, 1152], P('frame', 'pos')
- space_output_grad: float32 [1152, 1152], P(('frame', 'pos'))
- time_output_grad: float32 [1152, 1152], P(('frame', 'pos'))
The draws below stay inside these ranges and needn't reach their ends.
All inputs are finite; a program needn't handle non-finite values.
Results may differ from the reference program's by a relative error of at most 0.027.
Values may be sent and summed in bfloat16 or wider, within the bound.
A program may use at most 192 MiB of HBM per device.

```python
import jax
import jax.numpy as jnp
from jax import lax

D = 1152
HEADS = 16
HD = 72
FRAMES = 16
PLACES = 1536


def projection_rows(key):
    first, second, third = jax.random.split(key, 3)
    spread = D ** (-0.5)
    queries = jnp.clip(jax.random.normal(first, (D, D), jnp.float32), -4.0, 4.0) * spread
    others = jnp.clip(jax.random.normal(second, (D, D), jnp.float32), -4.0, 4.0) * spread
    values = jnp.clip(jax.random.normal(third, (D, D), jnp.float32), -4.0, 4.0) * spread
    key_rows = others
    return jnp.concatenate([queries, key_rows, values], axis=0)


def draw_space_projection(key, part):
    key = jax.random.fold_in(key, 11)
    return projection_rows(key).astype(jnp.bfloat16)


def draw_time_projection(key, part):
    key = jax.random.fold_in(key, 23)
    return projection_rows(key).astype(jnp.bfloat16)


def raised(values, own_key, source, target, parts, factor):
    def block_of(axis_at):
        return (jnp.arange(values.shape[axis_at]) // (values.shape[axis_at] // parts)).reshape((-1,) + (1,) * (values.ndim - 1 - axis_at))

    one_side = jax.random.permutation(own_key, parts)[block_of(target)]
    far = (block_of(target) + parts // 2) % parts
    return jnp.where((block_of(source) == one_side) | (block_of(source) == far), factor * values, values)


def shard_levels(own_key, dims, shards, least, top_value):
    factor_of = 1.0
    for position, blocks in shards:
        heights = jax.random.uniform(jax.random.fold_in(jax.random.fold_in(own_key, 6), position), (blocks,), jnp.float32, least / len(shards), top_value / len(shards))
        factor_of = factor_of * jnp.repeat(jnp.exp(heights), dims[position] // blocks).reshape((-1,) + (1,) * (len(dims) - 1 - position))
    return factor_of


def normal_values(own_key, extent, width, most, cuts=(), dtype=jnp.bfloat16):
    values = width * jax.random.normal(own_key, extent, jnp.float32)
    if cuts:
        values = values * shard_levels(own_key, extent, cuts, -0.22, 0.18)
    return jnp.clip(values, -most, most).astype(dtype)


def noise_with(own_key, dims, scale, bound, cuts, heavy, held_as=jnp.bfloat16):
    values = scale * jax.random.normal(own_key, dims, jnp.float32)
    if cuts:
        values = values * shard_levels(own_key, dims, cuts, -0.22, 0.18)
    return jnp.clip(raised(values, jax.random.fold_in(own_key, 3), *heavy), -bound, bound).astype(held_as)


def setup_inputs(seed: int = 0) -> dict:
    seeds = jax.random.split(jax.random.key(seed), 7)
    inputs = normal_values(seeds[0], (FRAMES, PLACES, D), 1.0, 6.0, ((0, 8), (1, 16)))
    cotangent = noise_with(seeds[1], (FRAMES, PLACES, D), 1.0, 6.0, ((0, 8), (1, 16)), (1, 2, 16, 2.0))
    space_projection = draw_space_projection(jax.random.fold_in(seeds[6], 71), 0)
    space_output = normal_values(seeds[3], (D, D), D ** -0.5, 0.1875)
    time_projection = draw_time_projection(jax.random.fold_in(seeds[6], 71), 0)
    time_output = normal_values(seeds[5], (D, D), D ** -0.5, 0.1875)
    return dict(inputs=inputs, cotangent=cotangent, space_projection=space_projection, space_output=space_output, time_projection=time_projection, time_output=time_output)


EPS = 1e-06
HIGH = lax.Precision.HIGHEST

def as_float(array):
    return array.astype(jnp.float32)

def normalize(tokens):
    values = as_float(tokens)
    center = values - lax.optimization_barrier(jnp.mean(values, axis=-1, keepdims=True))
    inv_std = lax.rsqrt(lax.optimization_barrier(jnp.mean(center * center, axis=-1, keepdims=True)) + EPS)
    return (center * inv_std, inv_std)

def norm_back(grad_hat, normed, inv_std):
    mean_grad = lax.optimization_barrier(jnp.mean(grad_hat, axis=-1, keepdims=True))
    mean_proj = lax.optimization_barrier(jnp.mean(grad_hat * normed, axis=-1, keepdims=True))
    return inv_std * (grad_hat - mean_grad - normed * mean_proj)

def project_in(hidden, weight):
    weight_three = weight.reshape(3, D, D)
    result = jnp.einsum('fsi,coi->cfso', as_float(hidden), as_float(weight_three), precision=HIGH)
    return result.astype(jnp.bfloat16)

def project_back(gradients, weight):
    weight_three = weight.reshape(3, D, D)
    return jnp.einsum('cfso,coi->fsi', as_float(gradients), as_float(weight_three), precision=HIGH)

def split_heads(array):
    return array.reshape(array.shape[0], array.shape[1], HEADS, HD)

def layouts(seq_first):
    token_form = 'lbhe' if seq_first else 'blhe'
    return (token_form, token_form.replace('l', 'm'))

def softmax_scores(queries, key_vectors, seq_first):
    token_form, key_form = layouts(seq_first)
    scores = jnp.einsum(token_form + ',' + key_form + '->bhlm', as_float(queries), as_float(key_vectors), precision=HIGH)
    return jax.nn.softmax(scores * HD ** (-0.5), axis=-1)

def attend(queries, key_vectors, values, seq_first):
    token_form, key_form = layouts(seq_first)
    probability = softmax_scores(queries, key_vectors, seq_first)
    weights = as_float(probability.astype(jnp.bfloat16))
    mixed = jnp.einsum('bhlm,' + key_form + '->' + token_form, weights, as_float(values), precision=HIGH)
    return mixed.astype(jnp.bfloat16)

def attend_back(queries, key_vectors, values, grad_mixed, seq_first):
    token_form, key_form = layouts(seq_first)
    probability = softmax_scores(queries, key_vectors, seq_first)
    weights = as_float(probability.astype(jnp.bfloat16))
    grad_probs = jnp.einsum(token_form + ',' + key_form + '->bhlm', as_float(grad_mixed), as_float(values), precision=HIGH)
    grad_values = jnp.einsum('bhlm,' + token_form + '->' + key_form, weights, as_float(grad_mixed), precision=HIGH).astype(jnp.bfloat16)
    centered = grad_probs - lax.optimization_barrier(jnp.sum(probability * grad_probs, axis=-1, keepdims=True))
    grad_scores = as_float((probability * centered * HD ** (-0.5)).astype(jnp.bfloat16))
    grad_queries = jnp.einsum('bhlm,' + key_form + '->' + token_form, grad_scores, as_float(key_vectors), precision=HIGH).astype(jnp.bfloat16)
    grad_keys = jnp.einsum('bhlm,' + token_form + '->' + key_form, grad_scores, as_float(queries), precision=HIGH).astype(jnp.bfloat16)
    return jnp.stack([grad_queries, grad_keys, grad_values])

def space_forward(group):
    return attend(group[0][None], group[1][None], group[2][None], False)[0]

def space_backward(group):
    return attend_back(group[0][None], group[1][None], group[2][None], group[3][None], False)[:, 0]

def reference(inputs, cotangent, space_projection, space_output, time_projection, time_output):
    shape = inputs.shape
    space_hat, space_inv = normalize(inputs)
    space_qkv = project_in(space_hat.astype(jnp.bfloat16), space_projection)
    space_parts = (split_heads(space_qkv[0]), split_heads(space_qkv[1]), split_heads(space_qkv[2]))
    space_mixed = lax.map(space_forward, space_parts).reshape(shape)
    space_proj = jnp.einsum('fsi,oi->fso', as_float(space_mixed), as_float(space_output), precision=HIGH)
    stream = (as_float(inputs) + space_proj).astype(jnp.bfloat16)
    time_hat, time_inv = normalize(stream)
    time_qkv = project_in(time_hat.astype(jnp.bfloat16), time_projection)
    time_parts = (split_heads(time_qkv[0]), split_heads(time_qkv[1]), split_heads(time_qkv[2]))
    time_mixed = attend(time_parts[0], time_parts[1], time_parts[2], True).reshape(shape)
    time_output_grad = jnp.einsum('fso,fsi->oi', as_float(cotangent), as_float(time_mixed), precision=HIGH)
    time_back = jnp.einsum('fso,oi->fsi', as_float(cotangent), as_float(time_output), precision=HIGH).astype(jnp.bfloat16)
    time_qkv_grad = attend_back(time_parts[0], time_parts[1], time_parts[2], split_heads(time_back), True)
    time_qkv_grad = time_qkv_grad.reshape(3, shape[0], shape[1], shape[2])
    upstream = (as_float(cotangent) + norm_back(project_back(time_qkv_grad, time_projection), time_hat, time_inv)).astype(jnp.bfloat16)
    space_output_grad = jnp.einsum('fso,fsi->oi', as_float(upstream), as_float(space_mixed), precision=HIGH)
    space_back = jnp.einsum('fso,oi->fsi', as_float(upstream), as_float(space_output), precision=HIGH).astype(jnp.bfloat16)
    space_qkv_grad = lax.map(space_backward, space_parts + (split_heads(space_back),))
    space_qkv_grad = jnp.moveaxis(space_qkv_grad, 1, 0).reshape(3, shape[0], shape[1], shape[2])
    input_grad = (as_float(upstream) + norm_back(project_back(space_qkv_grad, space_projection), space_hat, space_inv)).astype(jnp.bfloat16)
    return (input_grad, space_output_grad, time_output_grad)
```

```python
import jax
import jax.numpy as jnp
from jax import lax
from jax.sharding import PartitionSpec as P

HEADS = 16


EPS = 1e-06


def normalize(tokens):
    values = tokens.astype(jnp.float32)
    center = values - jnp.mean(values, axis=-1, keepdims=True)
    inv_std = lax.rsqrt(jnp.mean(center * center, axis=-1, keepdims=True) + EPS)
    return (center * inv_std, inv_std)


def norm_back(grad_hat, normed, inv_std):
    mean_grad = jnp.mean(grad_hat, axis=-1, keepdims=True)
    mean_proj = jnp.mean(grad_hat * normed, axis=-1, keepdims=True)
    return inv_std * (grad_hat - mean_grad - normed * mean_proj)


def project_in(hidden, weight):
    model_width = weight.shape[1]
    weight_three = weight.reshape(3, model_width, model_width)
    result = jnp.einsum("fsi,coi->cfso", hidden, weight_three, preferred_element_type=jnp.float32)
    return result.astype(jnp.bfloat16)


def project_back(gradients, weight):
    model_width = weight.shape[1]
    weight_three = weight.reshape(3, model_width, model_width)
    return jnp.einsum("cfso,coi->fsi", gradients, weight_three, preferred_element_type=jnp.float32)


def layouts(seq_first):
    token_form = "lbhe" if seq_first else "blhe"
    return (token_form, token_form.replace("l", "m"))


def attend(queries, key_vectors, values, seq_first):
    token_form, key_form = layouts(seq_first)
    score_scale = queries.shape[-1] ** (-0.5)
    scores = jnp.einsum(
        token_form + "," + key_form + "->bhlm",
        queries,
        key_vectors,
        preferred_element_type=jnp.float32,
    )
    probability = jax.nn.softmax(scores * score_scale, axis=-1)
    mixed = jnp.einsum(
        "bhlm," + key_form + "->" + token_form,
        probability.astype(jnp.bfloat16),
        values,
        preferred_element_type=jnp.float32,
    )
    return (mixed.astype(jnp.bfloat16), probability)


def attend_back(queries, key_vectors, values, probability, grad_mixed, seq_first):
    token_form, key_form = layouts(seq_first)
    score_scale = queries.shape[-1] ** (-0.5)
    weights = probability.astype(jnp.bfloat16)
    grad_probs = jnp.einsum(
        token_form + "," + key_form + "->bhlm",
        grad_mixed,
        values,
        preferred_element_type=jnp.float32,
    )
    grad_values = jnp.einsum(
        "bhlm," + token_form + "->" + key_form,
        weights,
        grad_mixed,
        preferred_element_type=jnp.float32,
    ).astype(jnp.bfloat16)
    centered = grad_probs - jnp.sum(probability * grad_probs, axis=-1, keepdims=True)
    grad_scores = (probability * centered * score_scale).astype(jnp.bfloat16)
    grad_queries = jnp.einsum(
        "bhlm," + key_form + "->" + token_form,
        grad_scores,
        key_vectors,
        preferred_element_type=jnp.float32,
    ).astype(jnp.bfloat16)
    grad_keys = jnp.einsum(
        "bhlm," + token_form + "->" + key_form,
        grad_scores,
        queries,
        preferred_element_type=jnp.float32,
    ).astype(jnp.bfloat16)
    return jnp.stack([grad_queries, grad_keys, grad_values])


def space_heads(stacked):
    return lax.all_to_all(stacked, "pos", split_axis=3, concat_axis=2, tiled=True)


def space_rows(stacked):
    return lax.all_to_all(stacked, "pos", split_axis=2, concat_axis=3, tiled=True)


def to_time(rows):
    return lax.all_to_all(rows, "frame", split_axis=1, concat_axis=0, tiled=True)


def to_rows(tokens):
    return lax.all_to_all(tokens, "frame", split_axis=0, concat_axis=1, tiled=True)


def time_mask(frames, places):
    place = jnp.arange(frames * places) % places
    return place[:, None] == place[None, :]


def scatter_sum(partial):
    devices = lax.axis_size("frame") * lax.axis_size("pos")
    rows, width = partial.shape
    flat = partial.reshape(devices, rows * width // devices // 128, 128)
    out = lax.psum_scatter(flat, ("frame", "pos"), scatter_dimension=0, tiled=False)
    return out.reshape(rows // devices, width)


def shards(inputs, cotangent, space_projection, space_output, time_projection, time_output):
    frames_here, places_here, model_width = inputs.shape
    head_size = model_width // HEADS
    scale = head_size ** (-0.5)
    cot_time = to_time(cotangent)
    space_hat, space_inv = normalize(inputs)
    space_qkv = project_in(space_hat.astype(jnp.bfloat16), space_projection)
    space_split = space_heads(space_qkv)
    all_places = space_split.shape[2]
    local_heads = space_split.shape[3] // head_size
    space_parts = space_split.reshape(3, frames_here, all_places, local_heads, head_size)
    space_mixed, space_probs = attend(space_parts[0], space_parts[1], space_parts[2], False)
    space_mixed_rows = space_rows(
        space_mixed.reshape(1, frames_here, all_places, local_heads * head_size)
    )[0]
    space_proj = jnp.einsum(
        "fsi,oi->fso", space_mixed_rows, space_output, preferred_element_type=jnp.float32
    )
    stream_rows = (inputs.astype(jnp.float32) + space_proj).astype(jnp.bfloat16)
    stream = to_time(stream_rows)
    frames, places, _ = stream.shape
    tokens = frames * places
    time_hat, time_inv = normalize(stream.reshape(tokens, model_width))
    qkv = jnp.einsum(
        "ti,oi->to",
        time_hat.astype(jnp.bfloat16),
        time_projection,
        preferred_element_type=jnp.float32,
    ).astype(jnp.bfloat16)
    q, k, v = (
        qkv[:, c * model_width : (c + 1) * model_width].reshape(tokens, HEADS, head_size)
        for c in range(3)
    )
    mask = time_mask(frames, places)
    scores = jnp.einsum("the,she->hts", q, k, preferred_element_type=jnp.float32) * scale
    probs = jax.nn.softmax(jnp.where(mask, scores, -jnp.inf), axis=-1)
    weights = probs.astype(jnp.bfloat16)
    time_mixed = jnp.einsum("hts,she->the", weights, v, preferred_element_type=jnp.float32)
    time_mixed = time_mixed.astype(jnp.bfloat16).reshape(tokens, model_width)
    cot = cot_time.reshape(tokens, model_width)
    time_grad_part = jnp.einsum("to,ti->oi", cot, time_mixed, preferred_element_type=jnp.float32)
    time_sum = scatter_sum(time_grad_part)
    back = jnp.einsum("to,oi->ti", cot, time_output, preferred_element_type=jnp.float32)
    back = back.astype(jnp.bfloat16).reshape(tokens, HEADS, head_size)
    grad_probs = jnp.einsum("the,she->hts", back, v, preferred_element_type=jnp.float32)
    grad_v = jnp.einsum("hts,the->she", weights, back, preferred_element_type=jnp.float32)
    centered = grad_probs - jnp.sum(probs * grad_probs, axis=-1, keepdims=True)
    grad_scores = (probs * centered * scale).astype(jnp.bfloat16)
    grad_q = jnp.einsum("hts,she->the", grad_scores, k, preferred_element_type=jnp.float32)
    grad_k = jnp.einsum("hts,the->she", grad_scores, q, preferred_element_type=jnp.float32)
    grads = jnp.concatenate(
        [g.astype(jnp.bfloat16).reshape(tokens, model_width) for g in (grad_q, grad_k, grad_v)],
        axis=1,
    )
    grad_hat = jnp.einsum("to,oi->ti", grads, time_projection, preferred_element_type=jnp.float32)
    upstream_time = cot.astype(jnp.float32) + norm_back(grad_hat, time_hat, time_inv)
    upstream_time = upstream_time.astype(jnp.bfloat16)
    upstream = to_rows(upstream_time.reshape(frames, places, model_width))
    space_grad_part = jnp.einsum(
        "fso,fsi->oi", upstream, space_mixed_rows, preferred_element_type=jnp.float32
    )
    space_sum = scatter_sum(space_grad_part)
    space_back = jnp.einsum(
        "fso,oi->fsi", upstream, space_output, preferred_element_type=jnp.float32
    ).astype(jnp.bfloat16)
    space_back_split = space_heads(space_back[None]).reshape(
        frames_here, all_places, local_heads, head_size
    )
    space_qkv_grad = attend_back(
        space_parts[0], space_parts[1], space_parts[2], space_probs, space_back_split, False
    )
    space_qkv_rows = space_rows(
        space_qkv_grad.reshape(3, frames_here, all_places, local_heads * head_size)
    )
    space_branch = norm_back(project_back(space_qkv_rows, space_projection), space_hat, space_inv)
    input_grad = (upstream.astype(jnp.float32) + space_branch).astype(jnp.bfloat16)
    return (input_grad, space_sum, time_sum)


def solution(mesh):
    return jax.shard_map(
        shards,
        mesh=mesh,
        in_specs=(P("frame", "pos", None), P("frame", "pos", None), P(), P(), P(), P()),
        out_specs=(P("frame", "pos", None), P(("frame", "pos"), None), P(("frame", "pos"), None)),
        check_vma=False,
    )
```

```python
import jax
import jax.numpy as jnp
import numpy as np
from jax import lax
from jax.experimental import pallas as pl
from jax.experimental.pallas import tpu as pltpu
from jax.sharding import PartitionSpec as P

HEADS = 16
EPS = 1e-06
BF = jnp.bfloat16
F32 = jnp.float32
D = 1152
HD = 72
NP = 16
NF = 8
FR = 2
PL = 96
TOK = FR * PL
ALL = NP * PL
TP = PL // NF
SLAB = 32
TT = NF * SLAB
GR = D // NF
SCALE = HD ** (-0.5)
LOG2E = 1.4426950408889634
QT = 384
BT = 256
KC = 256
LIMIT = 60 * 1024 * 1024


def dot(a, b, ca, cb):
    return lax.dot_general(a, b, (((ca,), (cb,)), ((), ())), preferred_element_type=F32)


def normalize(tokens):
    values = tokens.astype(F32)
    center = values - jnp.mean(values, axis=-1, keepdims=True)
    inv_std = lax.rsqrt(jnp.mean(center * center, axis=-1, keepdims=True) + EPS)
    return center * inv_std, inv_std


def norm_back(grad_hat, normed, inv_std):
    mean_grad = jnp.mean(grad_hat, axis=-1, keepdims=True)
    mean_proj = jnp.mean(grad_hat * normed, axis=-1, keepdims=True)
    return inv_std * (grad_hat - mean_grad - normed * mean_proj)


def greet(barrier, p, f, pos, frame):
    if pos:

        @pl.loop(1, NP)
        def _(s):
            pl.semaphore_signal(barrier, inc=1, device_id={"pos": lax.rem(p + s, NP)})

    if frame:

        @pl.loop(1, NF)
        def _(s):
            pl.semaphore_signal(barrier, inc=1, device_id={"frame": lax.rem(f + s, NF)})


def send(src, dst, send_sem, recv_sem, axis, dest):
    return pltpu.make_async_remote_copy(
        src_ref=src, dst_ref=dst, send_sem=send_sem, recv_sem=recv_sem, device_id={axis: dest}
    )


def space_forward_kernel(
    x, cot, perm, w_hbm, so_hbm,
    qkv_out, stat_out, att_out, mixed_out, stream_out, cot_out,
    w, so, hat, qsend, qkv, kbuf, qbuf, vt, sbuf, pbuf, osend, orecv, stream, fsend, frecv, csend, crecv,
    wsem, sosem, qss, qrs, oss, ors, fss, frs, css, crs, outsem,
):
    p = lax.axis_index("pos")
    f = lax.axis_index("frame")
    par = lax.rem(p, 2)
    half = p // 2
    barrier = pltpu.get_barrier_semaphore()
    greet(barrier, p, f, True, True)

    def w_copy(i, c):
        pair = lax.rem(half + i, 8)
        rows = pl.ds(pl.multiple_of(c * D + pair * 144, 16), 144)
        return pltpu.make_async_copy(w_hbm.at[rows], w.at[i, pl.ds(c * 144, 144)], wsem.at[i, c])

    for i in range(8):
        for c in range(3):
            w_copy(i, c).start()
    so_copy = pltpu.make_async_copy(so_hbm, so, sosem)
    so_copy.start()
    hat[...] = normalize(x[...])[0].astype(BF)
    pl.semaphore_wait(barrier, NP - 1 + NF - 1)

    def peer(s, sign):
        pair = lax.rem(half + sign * (s // 2) + 8, 8)
        return 2 * pair + lax.rem(par + s, 2)

    def q_copy(fr, s):
        return send(qsend.at[s, fr], qkv.at[fr, p], qss.at[fr, s], qrs.at[fr, s], "pos", peer(s, 1))

    @pl.loop(0, 8)
    def _(i):
        for c in range(3):
            w_copy(i, c).wait()
        r = dot(hat[...], w[i], 1, 1)
        pad = jnp.zeros((TOK, 256 - 3 * HD), F32)
        for e in range(2):
            part = [r[:, c * 144 + e * HD : c * 144 + e * HD + HD] for c in range(3)]
            val = jnp.concatenate(part + [pad], axis=1).astype(BF)
            qsend[2 * i + lax.rem(par + e, 2)] = val.reshape(FR, PL, 256)

        @pl.when(i > 0)
        def _():
            q_copy(0, 2 * i).start()

        q_copy(0, 2 * i + 1).start()

    @pl.loop(1, NP)
    def _(s):
        q_copy(1, s).start()

    qkv[:, pl.ds(p, 1)] = qsend[0][:, None]

    def c_copy(s):
        to = lax.rem(f + s, NF)
        return send(csend.at[to], crecv.at[f], css.at[s], crs.at[s], "frame", to)

    csend[...] = dot(perm[...], cot[...], 1, 0).astype(BF).reshape(NF, SLAB, D)

    @pl.loop(1, NF)
    def _(s):
        c_copy(s).start()

    crecv[pl.ds(f, 1)] = csend[pl.ds(f, 1)]

    def o_copy(fr, s):
        to = lax.rem(p + s, NP)
        return send(osend.at[fr, to], orecv.at[fr, p], oss.at[fr, s], ors.at[fr, s], "pos", to)

    outs = []
    for fr in range(FR):

        @pl.loop(1, NP)
        def _(s):
            q_copy(fr, s).wait_recv()

        out = pltpu.make_async_copy(qkv.at[fr], qkv_out.at[fr], outsem.at[fr])
        out.start()
        outs.append(out)
        rows = qkv[fr].reshape(ALL, 256)
        lane = lax.broadcasted_iota(jnp.int32, (1, 128), 1)
        keep = (lane < HD).astype(F32).astype(BF)
        zeros = jnp.zeros((ALL, 128 - HD), BF)
        qbuf[...] = rows[:, :128] * keep
        kbuf[...] = rows[:, HD : HD + 128]
        vt[...] = jnp.concatenate([rows[:, 2 * HD : 3 * HD], zeros], axis=1).T

        @pl.loop(0, ALL // QT)
        def _(t):
            tile = lax.rem(p // 4 + t, ALL // QT)
            at = pl.ds(pl.multiple_of(tile * QT, QT), QT)
            q = qbuf[at]
            top = jnp.full((8, QT), -jnp.inf, F32)
            for k in range(0, ALL, KC):
                s = dot(kbuf[k : k + KC], q, 1, 1)
                sbuf[k : k + KC] = s
                top = jnp.maximum(top, jnp.max(s.reshape(KC // 8, 8, QT), axis=0))
            top = jnp.max(top, axis=0, keepdims=True) * (SCALE * LOG2E)
            total = jnp.zeros((8, QT), F32)
            for k in range(0, ALL, KC):
                e = jnp.exp2(sbuf[k : k + KC] * (SCALE * LOG2E) - top)
                total = total + jnp.sum(e.reshape(KC // 8, 8, QT), axis=0)
                pbuf[k : k + KC] = e.astype(BF)
            total = jnp.sum(total, axis=0, keepdims=True)
            o = dot(vt[...], pbuf[...], 1, 0) * (1.0 / total)
            stat_out[fr, :, at] = jnp.broadcast_to(top + jnp.log(total) * LOG2E, (8, QT))
            att_out[fr, :, at] = o
            osend[fr, pl.ds(tile * 4, 4)] = o.T.astype(BF).reshape(4, PL, 128)
            for j in range(4):
                to = tile * 4 + j

                @pl.when(to != p)
                def _():
                    o_copy(fr, lax.rem(to - p + NP, NP)).start()

        orecv[fr, pl.ds(p, 1)] = osend[fr, pl.ds(p, 1)]

    so_copy.wait()
    for fr in range(FR):

        @pl.loop(1, NP)
        def _(s):
            o_copy(fr, s).wait_recv()

        mixed = jnp.concatenate([orecv[fr, h][:, :HD].astype(F32) for h in range(HEADS)], axis=1)
        mixed = mixed.astype(BF)
        part = slice(fr * PL, (fr + 1) * PL)
        mixed_out[part] = mixed
        stream[part] = (x[part].astype(F32) + dot(mixed, so[...], 1, 1)).astype(BF)

    def f_copy(s):
        to = lax.rem(f + s, NF)
        return send(fsend.at[to], frecv.at[f], fss.at[s], frs.at[s], "frame", to)

    fsend[...] = dot(perm[...], stream[...], 1, 0).astype(BF).reshape(NF, SLAB, D)

    @pl.loop(1, NF)
    def _(s):
        f_copy(s).start()

    frecv[pl.ds(f, 1)] = fsend[pl.ds(f, 1)]

    @pl.loop(1, NF)
    def _(s):
        c_copy(s).wait_recv()

    cot_out[...] = crecv[...]

    @pl.loop(1, NP)
    def _(s):
        for fr in range(FR):
            q_copy(fr, s).wait_send()
            o_copy(fr, s).wait_send()

    for out in outs:
        out.wait()

    @pl.loop(1, NF)
    def _(s):
        f_copy(s).wait_recv()

    stream_out[...] = frecv[...]

    @pl.loop(1, NF)
    def _(s):
        c_copy(s).wait_send()
        f_copy(s).wait_send()


def vmem():
    return pl.BlockSpec(memory_space=pltpu.VMEM)


def anywhere():
    return pl.BlockSpec(memory_space=pl.ANY)


DMA = pltpu.SemaphoreType.DMA


def params(collective_id):
    return pltpu.CompilerParams(
        collective_id=collective_id, has_side_effects=True, vmem_limit_bytes=LIMIT
    )


def space_forward(x, cot, perm, w, so):
    V = pltpu.VMEM
    sds = jax.ShapeDtypeStruct
    return pl.pallas_call(
        space_forward_kernel,
        out_shape=(
            sds((FR, NP, PL, 256), BF),
            sds((FR, 8, ALL), F32),
            sds((FR, 128, ALL), F32),
            sds((TOK, D), BF),
            sds((NF, SLAB, D), BF),
            sds((NF, SLAB, D), BF),
        ),
        in_specs=[vmem(), vmem(), vmem(), anywhere(), anywhere()],
        out_specs=(anywhere(), vmem(), vmem(), vmem(), vmem(), vmem()),
        scratch_shapes=[
            V((8, 432, D), BF), V((D, D), BF), V((TOK, D), BF), V((NP, FR, PL, 256), BF),
            V((FR, NP, PL, 256), BF), V((ALL, 128), BF), V((ALL, 128), BF), V((128, ALL), BF),
            V((ALL, QT), F32), V((ALL, QT), BF),
            V((FR, NP, PL, 128), BF), V((FR, NP, PL, 128), BF), V((TOK, D), BF),
            V((NF, SLAB, D), BF), V((NF, SLAB, D), BF), V((NF, SLAB, D), BF), V((NF, SLAB, D), BF),
            DMA((8, 3)), DMA, DMA((FR, NP)), DMA((FR, NP)), DMA((FR, NP)), DMA((FR, NP)),
            DMA((NF,)), DMA((NF,)), DMA((NF,)), DMA((NF,)), DMA((FR,)),
        ],
        compiler_params=params(1),
    )(x, cot, perm, w, so)


def time_kernel(
    stream, cot, mask, unperm, w_hbm, to_hbm,
    up_out, grad_out,
    w, wo, hat, qkv, back, mixed, dqkv, usend, urecv,
    wsem, tosem, uss, urs,
):
    p = lax.axis_index("pos")
    f = lax.axis_index("frame")
    barrier = pltpu.get_barrier_semaphore()
    greet(barrier, p, f, False, True)
    to_copy = pltpu.make_async_copy(to_hbm, wo, tosem)
    to_copy.start()
    w_copies = [pltpu.make_async_copy(w_hbm.at[pl.ds(c * D, D)], w.at[c], wsem.at[c]) for c in range(3)]
    for c in w_copies:
        c.start()
    normed, inv = normalize(stream[...])
    hat[...] = normed
    normed = normed.astype(BF)
    to_copy.wait()
    back[...] = dot(cot[...], wo[...], 1, 0).astype(BF)
    for c in range(3):
        w_copies[c].wait()
        qkv[c] = dot(normed, w[c], 1, 1).astype(BF)
    mixed[...] = jnp.zeros_like(mixed)
    dqkv[...] = jnp.zeros_like(dqkv)
    for h in range(HEADS):
        off = (h * HD) % 128
        start = h * HD - off
        width = 128 if off + HD <= 128 else 256
        win = slice(start, start + width)
        lane = lax.broadcasted_iota(jnp.int32, (1, width), 1)
        keep = ((lane >= off) & (lane < off + HD)).astype(F32).astype(BF)
        q, k, v, b = qkv[0, :, win], qkv[1, :, win], qkv[2, :, win], back[:, win]
        qm, km, vm, bm = q * keep, k * keep, v * keep, b * keep
        s = dot(qm, k, 1, 1) * SCALE + mask[...]
        e = jnp.exp(s - jnp.max(s, axis=1, keepdims=True))
        prob = e * (1.0 / jnp.sum(e, axis=1, keepdims=True))
        pb = prob.astype(BF)
        mixed[:, win] += dot(pb, vm, 1, 0)
        gp = dot(bm, v, 1, 1)
        gs = prob * (gp - jnp.sum(prob * gp, axis=1, keepdims=True)) * SCALE
        gs = gs.astype(BF)
        dqkv[0, :, win] += dot(gs, km, 1, 0)
        dqkv[1, :, win] += dot(gs, qm, 0, 0)
        dqkv[2, :, win] += dot(pb, bm, 0, 0)
    grad_hat = dot(dqkv[0].astype(BF), w[0], 1, 0)
    for c in range(1, 3):
        grad_hat += dot(dqkv[c].astype(BF), w[c], 1, 0)
    up = cot[...].astype(F32) + norm_back(grad_hat, hat[...], inv)
    usend[...] = up.astype(BF).reshape(NF, SLAB, D)
    pl.semaphore_wait(barrier, NF - 1)

    def u_copy(s):
        to = lax.rem(f + s, NF)
        return send(usend.at[to], urecv.at[f], uss.at[s], urs.at[s], "frame", to)

    @pl.loop(1, NF)
    def _(s):
        u_copy(s).start()

    urecv[pl.ds(f, 1)] = usend[pl.ds(f, 1)]
    mb = mixed[...].astype(BF)
    for r in range(0, D, 128):
        grad_out[r : r + 128] = dot(cot[:, r : r + 128], mb, 0, 0).astype(BF)

    @pl.loop(1, NF)
    def _(s):
        u_copy(s).wait()

    up_out[...] = dot(unperm[...], urecv[...].reshape(TT, D), 1, 0).astype(BF)


def time_block(stream, cot, mask, unperm, w, wo):
    V = pltpu.VMEM
    sds = jax.ShapeDtypeStruct
    return pl.pallas_call(
        time_kernel,
        out_shape=(sds((TOK, D), BF), sds((D, D), BF)),
        in_specs=[vmem(), vmem(), vmem(), vmem(), anywhere(), anywhere()],
        out_specs=(vmem(), vmem()),
        scratch_shapes=[
            V((3, D, D), BF), V((D, D), BF), V((TT, D), F32), V((3, TT, D), BF), V((TT, D), BF),
            V((TT, D), F32), V((3, TT, D), F32), V((NF, SLAB, D), BF), V((NF, SLAB, D), BF),
            DMA((3,)), DMA, DMA((NF,)), DMA((NF,)),
        ],
        compiler_params=params(2),
    )(stream, cot, mask, unperm, w, wo)


def space_backward_kernel(
    x, up, mixed, spread, stat, att, qkv_hbm, gt_hbm, w_hbm, so_hbm,
    grad_out, gs_out, gt_out,
    w, so, qkv, bsend, brecv, gpart, grecv, hsend, hrecv, qbuf, kbuf, vbuf, kt, pbuf, sbuf,
    dq, dk, dv, rsend, rrecv,
    wsem, sosem, qsem, gsem, bss, brs, gss, grs, hss, hrs, rss, rrs,
):
    p = lax.axis_index("pos")
    f = lax.axis_index("frame")
    barrier = pltpu.get_barrier_semaphore()
    greet(barrier, p, f, True, True)
    so_copy = pltpu.make_async_copy(so_hbm, so, sosem)
    so_copy.start()
    qkv_copy = pltpu.make_async_copy(qkv_hbm, qkv, qsem)
    qkv_copy.start()
    gt_copy = pltpu.make_async_copy(gt_hbm, gpart.at[0], gsem)
    gt_copy.start()
    w_copy = pltpu.make_async_copy(w_hbm, w, wsem)
    w_copy.start()
    so_copy.wait()
    back = dot(up[...], so[...], 1, 0)
    pad = jnp.zeros((TOK, 128 - HD), F32)
    for h in range(HEADS):
        val = jnp.concatenate([back[:, h * HD : (h + 1) * HD], pad], axis=1).astype(BF)
        bsend[:, h] = val.reshape(FR, PL, 128)
    pl.semaphore_wait(barrier, NP - 1 + NF - 1)

    def b_copy(fr, s):
        to = lax.rem(p + s, NP)
        return send(bsend.at[fr, to], brecv.at[fr, p], bss.at[fr, s], brs.at[fr, s], "pos", to)

    for fr in range(FR):

        @pl.loop(1, NP)
        def _(s):
            b_copy(fr, s).start()

    brecv[:, pl.ds(p, 1)] = bsend[:, pl.ds(p, 1)]

    def g_copy(g, s):
        to = lax.rem(f + s, NF)
        rows = pl.ds(pl.multiple_of(to * GR, 16), GR)
        return send(gpart.at[g, rows], grecv.at[g, f], gss.at[g, s], grs.at[g, s], "frame", to)

    gt_copy.wait()

    @pl.loop(1, NF)
    def _(s):
        g_copy(0, s).start()

    for r in range(0, D, 128):
        gpart[1, r : r + 128] = dot(up[:, r : r + 128], mixed[...], 0, 0).astype(BF)

    @pl.loop(1, NF)
    def _(s):
        g_copy(1, s).start()

    for g in range(2):
        grecv[g, pl.ds(f, 1)] = gpart[g, pl.ds(pl.multiple_of(f * GR, 16), GR)][None]

    def r_copy(fr, s):
        to = lax.rem(p + s, NP)
        return send(rsend.at[fr, to], rrecv.at[fr, p], rss.at[fr, s], rrs.at[fr, s], "pos", to)

    qkv_copy.wait()
    lane = lax.broadcasted_iota(jnp.int32, (1, 128), 1)
    keep = (lane < HD).astype(F32).astype(BF)
    for fr in range(FR):
        rows = qkv[fr].reshape(ALL, 256)
        zeros = jnp.zeros((ALL, 128 - HD), BF)
        qbuf[...] = rows[:, :128] * keep
        k = rows[:, HD : HD + 128] * keep
        kbuf[...] = k
        kt[...] = k.T
        vbuf[...] = jnp.concatenate([rows[:, 2 * HD : 3 * HD], zeros], axis=1)
        dk[...] = jnp.zeros_like(dk)
        dv[...] = jnp.zeros_like(dv)

        @pl.loop(1, NP)
        def _(s):
            b_copy(fr, s).wait_recv()

        @pl.loop(0, ALL // BT)
        def _(t):
            at = pl.ds(pl.multiple_of(t * BT, BT), BT)
            q = qbuf[at]
            b = brecv.reshape(FR, ALL, 128)[fr, at]
            total = jnp.sum(b.astype(F32).T * att[fr, :, at], axis=0, keepdims=True)
            lse = stat[fr, 0:1, at]
            for k in range(0, ALL, KC):
                s = dot(kbuf[k : k + KC], q, 1, 1)
                gp = dot(vbuf[k : k + KC], b, 1, 1)
                prob = jnp.exp2(s * (SCALE * LOG2E) - lse)
                pbuf[k : k + KC] = prob.astype(BF)
                sbuf[k : k + KC] = (prob * (gp - total)).astype(BF)
            dv[...] += dot(pbuf[...], b, 1, 0)
            dk[...] += dot(sbuf[...], q, 1, 0)
            dq[at] = dot(kt[...], sbuf[...], 1, 0).T

        val = jnp.concatenate(
            [
                dq[:, :HD] * SCALE,
                dk[:, :HD] * SCALE,
                dv[:, :HD],
                jnp.zeros((ALL, 256 - 3 * HD), F32),
            ],
            axis=1,
        )
        rsend[fr] = val.astype(BF).reshape(NP, PL, 256)

        @pl.loop(1, NP)
        def _(s):
            r_copy(fr, s).start()

        rrecv[fr, pl.ds(p, 1)] = rsend[fr, pl.ds(p, 1)]

    def h_copy(g, s):
        to = lax.rem(p + s, NP)
        return send(hsend.at[g, to], hrecv.at[g, p], hss.at[g, s], hrs.at[g, s], "pos", to)

    for g in range(2):

        @pl.loop(1, NF)
        def _(s):
            g_copy(g, s).wait_recv()

        total = grecv[g, 0].astype(F32)
        for s in range(1, NF):
            total += grecv[g, s].astype(F32)
        hsend[g] = dot(spread[...], total.astype(BF), 1, 0).astype(BF).reshape(NP, 16, D)

        @pl.loop(1, NP)
        def _(s):
            h_copy(g, s).start()

        hrecv[g, pl.ds(p, 1)] = hsend[g, pl.ds(p, 1)]

    w_copy.wait()
    for fr in range(FR):

        @pl.loop(1, NP)
        def _(s):
            r_copy(fr, s).wait_recv()

        got = [rrecv[fr, h].astype(F32) for h in range(HEADS)]
        grad_hat = jnp.zeros((PL, D), F32)
        for c in range(3):
            part = jnp.concatenate([v[:, c * HD : (c + 1) * HD] for v in got], axis=1)
            grad_hat += dot(part.astype(BF), w[c * D : (c + 1) * D], 1, 0)
        here = slice(fr * PL, (fr + 1) * PL)
        normed, inv = normalize(x[here])
        grad_out[here] = (up[here].astype(F32) + norm_back(grad_hat, normed, inv)).astype(BF)

    for g, out in ((0, gt_out), (1, gs_out)):

        @pl.loop(1, NP)
        def _(s):
            h_copy(g, s).wait_recv()

        total = hrecv[g, 0].astype(F32)
        for s in range(1, NP):
            total += hrecv[g, s].astype(F32)
        out[...] = total

    @pl.loop(1, NP)
    def _(s):
        for fr in range(FR):
            b_copy(fr, s).wait_send()
            r_copy(fr, s).wait_send()
        for g in range(2):
            h_copy(g, s).wait_send()

    @pl.loop(1, NF)
    def _(s):
        for g in range(2):
            g_copy(g, s).wait_send()


def space_backward(x, up, mixed, spread, stat, att, qkv, gt, w, so):
    V = pltpu.VMEM
    sds = jax.ShapeDtypeStruct
    return pl.pallas_call(
        space_backward_kernel,
        out_shape=(sds((TOK, D), BF), sds((16, D), F32), sds((16, D), F32)),
        in_specs=[vmem()] * 6 + [anywhere()] * 4,
        out_specs=(vmem(), vmem(), vmem()),
        scratch_shapes=[
            V((3 * D, D), BF), V((D, D), BF), V((FR, NP, PL, 256), BF),
            V((FR, NP, PL, 128), BF), V((FR, NP, PL, 128), BF),
            V((2, D, D), BF), V((2, NF, GR, D), BF), V((2, NP, 16, D), BF), V((2, NP, 16, D), BF),
            V((ALL, 128), BF), V((ALL, 128), BF), V((ALL, 128), BF), V((128, ALL), BF),
            V((ALL, BT), BF), V((ALL, BT), BF),
            V((ALL, 128), F32), V((ALL, 128), F32), V((ALL, 128), F32),
            V((FR, NP, PL, 256), BF), V((FR, NP, PL, 256), BF),
            DMA, DMA, DMA, DMA, DMA((FR, NP)), DMA((FR, NP)), DMA((2, NF)), DMA((2, NF)),
            DMA((2, NP)), DMA((2, NP)), DMA((FR, NP)), DMA((FR, NP)),
        ],
        compiler_params=params(3),
    )(x, up, mixed, spread, stat, att, qkv, gt, w, so)


def tables():
    row = np.arange(TT)
    slab, inner = row // SLAB, row % SLAB
    real = inner < FR * TP
    col = (inner // TP) * PL + slab * TP + inner % TP
    perm = (real[:, None] & (col[:, None] == np.arange(TOK)[None])).astype(np.float32)
    place = np.where(real, inner % TP, -1)
    mask = np.where(place[:, None] == place[None], 0.0, -1e30).astype(np.float32)
    row = np.arange(NP * 16)
    spread = (row % 16 < GR // NP)[:, None] & (
        ((row // 16) * (GR // NP) + row % 16)[:, None] == np.arange(GR)[None]
    )
    return jnp.asarray(perm, BF), jnp.asarray(perm.T, BF), jnp.asarray(mask), jnp.asarray(spread, BF)


def shards(inputs, cotangent, space_projection, space_output, time_projection, time_output):
    perm, unperm, mask, spread = tables()
    x = inputs.reshape(TOK, D)
    cot = cotangent.reshape(TOK, D)
    qkv, stat, att, mixed, stream_t, cot_t = space_forward(x, cot, perm, space_projection, space_output)
    up, gt = time_block(
        stream_t.reshape(TT, D), cot_t.reshape(TT, D), mask, unperm, time_projection, time_output
    )
    grad, gs, gt = space_backward(
        x, up, mixed, spread, stat, att, qkv, gt, space_projection, space_output
    )
    rows = GR // NP
    return grad.reshape(FR, PL, D), gs[:rows], gt[:rows]


def solution(mesh):
    return jax.shard_map(
        shards,
        mesh=mesh,
        in_specs=(P("frame", "pos", None), P("frame", "pos", None), P(), P(), P(), P()),
        out_specs=(P("frame", "pos", None), P(("frame", "pos"), None), P(("frame", "pos"), None)),
        check_vma=False,
    )
```

```python
import jax
import jax.numpy as jnp
import numpy as np
from jax import lax
from jax.experimental import pallas as pl
from jax.experimental.pallas import tpu as pltpu
from jax.sharding import PartitionSpec as P

HEADS = 16
EPS = 1e-06
BF = jnp.bfloat16
F32 = jnp.float32
D = 1152
HD = 72
NP = 16
NF = 8
FR = 2
PL = 96
TOK = FR * PL
ALL = NP * PL
TP = PL // NF
SLAB = 32
TT = NF * SLAB
GR = D // NF // NP
NK = NP // 2
GS = 80
GH = NF * GS
GRP = PL // 3
SCALE = HD ** (-0.5)
LOG2E = 1.4426950408889634
QT = 384
BT = 256
KC = 256
LIMIT = 60 * 1024 * 1024


def dot(a, b, ca, cb):
    return lax.dot_general(a, b, (((ca,), (cb,)), ((), ())), preferred_element_type=F32)


def normalize(tokens):
    values = tokens.astype(F32)
    center = values - jnp.mean(values, axis=-1, keepdims=True)
    inv_std = lax.rsqrt(jnp.mean(center * center, axis=-1, keepdims=True) + EPS)
    return center * inv_std, inv_std


def norm_back(grad_hat, normed, inv_std):
    mean_grad = jnp.mean(grad_hat, axis=-1, keepdims=True)
    mean_proj = jnp.mean(grad_hat * normed, axis=-1, keepdims=True)
    return inv_std * (grad_hat - mean_grad - normed * mean_proj)


def pack(parts):
    shape = parts[0].shape[:-1] + (256 - 3 * HD,)
    return jnp.concatenate(list(parts) + [jnp.zeros(shape, F32)], axis=-1).astype(BF)


def lanes(value, g):
    return value[..., g * HD : (g + 1) * HD]


def greet(barrier, p, f, pos, frame):
    if pos:

        @pl.loop(1, NP)
        def _(s):
            pl.semaphore_signal(barrier, inc=1, device_id={"pos": lax.rem(p + s, NP)})

    if frame:

        @pl.loop(1, NF)
        def _(s):
            pl.semaphore_signal(barrier, inc=1, device_id={"frame": lax.rem(f + s, NF)})


def send(src, dst, send_sem, recv_sem, axis, dest):
    return pltpu.make_async_remote_copy(
        src_ref=src, dst_ref=dst, send_sem=send_sem, recv_sem=recv_sem, device_id={axis: dest}
    )


def space_forward_kernel(
    x, cot, perm, w_hbm, so_hbm,
    qkv_out, stat_out, att_out, mixed_out, stream_out, cot_out,
    w, so, hat, qsend, qkv, kbuf, qbuf, vt, sbuf, pbuf, osend, orecv, stream, fsend, frecv, csend, crecv,
    wsem, sosem, qss, qrs, oss, ors, fss, frs, css, crs, outsem,
):
    p = lax.axis_index("pos")
    f = lax.axis_index("frame")
    par = lax.rem(p, 2)
    half = p // 2
    barrier = pltpu.get_barrier_semaphore()
    greet(barrier, p, f, True, True)

    def w_copy(i, c):
        pair = lax.rem(half + i, 8)
        rows = pl.ds(pl.multiple_of(c * D + pair * 144, 16), 144)
        return pltpu.make_async_copy(w_hbm.at[rows], w.at[i, pl.ds(c * 144, 144)], wsem.at[i, c])

    for i in range(8):
        for c in range(3):
            w_copy(i, c).start()
    so_copy = pltpu.make_async_copy(so_hbm, so, sosem)
    so_copy.start()
    hat[...] = normalize(x[...])[0].astype(BF)
    pl.semaphore_wait(barrier, NP - 1 + NF - 1)

    def peer(s, sign):
        pair = lax.rem(half + sign * (s // 2) + 8, 8)
        return 2 * pair + lax.rem(par + s, 2)

    def q_copy(fr, s):
        return send(qsend.at[s, fr], qkv.at[fr, p], qss.at[fr, s], qrs.at[fr, s], "pos", peer(s, 1))

    @pl.loop(0, 8)
    def _(i):
        for c in range(3):
            w_copy(i, c).wait()
        r = dot(hat[...], w[i], 1, 1)
        pad = jnp.zeros((TOK, 256 - 3 * HD), F32)
        for e in range(2):
            part = [r[:, c * 144 + e * HD : c * 144 + e * HD + HD] for c in range(3)]
            val = jnp.concatenate(part + [pad], axis=1).astype(BF)
            qsend[2 * i + lax.rem(par + e, 2)] = val.reshape(FR, PL, 256)

        @pl.when(i > 0)
        def _():
            q_copy(0, 2 * i).start()

        q_copy(0, 2 * i + 1).start()

    @pl.loop(1, NP)
    def _(s):
        q_copy(1, s).start()

    qkv[:, pl.ds(p, 1)] = qsend[0][:, None]

    def c_copy(s):
        to = lax.rem(f + s, NF)
        return send(csend.at[to], crecv.at[f], css.at[s], crs.at[s], "frame", to)

    csend[...] = dot(perm[...], cot[...], 1, 0).astype(BF).reshape(NF, SLAB, D)

    @pl.loop(1, NF)
    def _(s):
        c_copy(s).start()

    crecv[pl.ds(f, 1)] = csend[pl.ds(f, 1)]

    def o_copy(fr, s):
        to = lax.rem(p + s, NP)
        return send(osend.at[fr, to], orecv.at[fr, p], oss.at[fr, s], ors.at[fr, s], "pos", to)

    outs = []
    for fr in range(FR):

        @pl.loop(1, NP)
        def _(s):
            q_copy(fr, s).wait_recv()

        out = pltpu.make_async_copy(qkv.at[fr], qkv_out.at[fr], outsem.at[fr])
        out.start()
        outs.append(out)
        rows = qkv[fr].reshape(ALL, 256)
        lane = lax.broadcasted_iota(jnp.int32, (1, 128), 1)
        keep = (lane < HD).astype(F32).astype(BF)
        zeros = jnp.zeros((ALL, 128 - HD), BF)
        qbuf[...] = rows[:, :128] * keep
        kbuf[...] = rows[:, HD : HD + 128]
        vt[...] = jnp.concatenate([rows[:, 2 * HD : 3 * HD], zeros], axis=1).T

        @pl.loop(0, ALL // QT)
        def _(t):
            tile = lax.rem(p // 4 + t, ALL // QT)
            at = pl.ds(pl.multiple_of(tile * QT, QT), QT)
            q = qbuf[at]
            top = jnp.full((8, QT), -jnp.inf, F32)
            for k in range(0, ALL, KC):
                s = dot(kbuf[k : k + KC], q, 1, 1)
                sbuf[k : k + KC] = s
                top = jnp.maximum(top, jnp.max(s.reshape(KC // 8, 8, QT), axis=0))
            top = jnp.max(top, axis=0, keepdims=True) * (SCALE * LOG2E)
            total = jnp.zeros((8, QT), F32)
            for k in range(0, ALL, KC):
                e = jnp.exp2(sbuf[k : k + KC] * (SCALE * LOG2E) - top)
                total = total + jnp.sum(e.reshape(KC // 8, 8, QT), axis=0)
                pbuf[k : k + KC] = e.astype(BF)
            total = jnp.sum(total, axis=0, keepdims=True)
            o = dot(vt[...], pbuf[...], 1, 0) * (1.0 / total)
            stat_out[fr, :, at] = jnp.broadcast_to(top + jnp.log(total) * LOG2E, (8, QT))
            att_out[fr, :, at] = o
            turned = o.T.reshape(4, 3, GRP, 128)
            osend[fr, pl.ds(tile * 4, 4)] = pack([turned[:, g, :, :HD] for g in range(3)])
            for j in range(4):
                to = tile * 4 + j

                @pl.when(to != p)
                def _():
                    o_copy(fr, lax.rem(to - p + NP, NP)).start()

        orecv[fr, pl.ds(p, 1)] = osend[fr, pl.ds(p, 1)]

    so_copy.wait()
    for fr in range(FR):

        @pl.loop(1, NP)
        def _(s):
            o_copy(fr, s).wait_recv()

        got = [orecv[fr, h].astype(F32) for h in range(HEADS)]
        mixed = jnp.concatenate(
            [jnp.concatenate([lanes(v, g) for v in got], axis=1) for g in range(3)], axis=0
        ).astype(BF)
        part = slice(fr * PL, (fr + 1) * PL)
        mixed_out[part] = mixed
        stream[part] = (x[part].astype(F32) + dot(mixed, so[...], 1, 1)).astype(BF)

    def f_copy(s):
        to = lax.rem(f + s, NF)
        return send(fsend.at[to], frecv.at[f], fss.at[s], frs.at[s], "frame", to)

    fsend[...] = dot(perm[...], stream[...], 1, 0).astype(BF).reshape(NF, SLAB, D)

    @pl.loop(1, NF)
    def _(s):
        f_copy(s).start()

    frecv[pl.ds(f, 1)] = fsend[pl.ds(f, 1)]

    @pl.loop(1, NF)
    def _(s):
        c_copy(s).wait_recv()

    cot_out[...] = crecv[...]

    @pl.loop(1, NP)
    def _(s):
        for fr in range(FR):
            q_copy(fr, s).wait_send()
            o_copy(fr, s).wait_send()

    for out in outs:
        out.wait()

    @pl.loop(1, NF)
    def _(s):
        f_copy(s).wait_recv()

    stream_out[...] = frecv[...]

    @pl.loop(1, NF)
    def _(s):
        c_copy(s).wait_send()
        f_copy(s).wait_send()


def vmem():
    return pl.BlockSpec(memory_space=pltpu.VMEM)


def anywhere():
    return pl.BlockSpec(memory_space=pl.ANY)


DMA = pltpu.SemaphoreType.DMA


def params(collective_id):
    return pltpu.CompilerParams(
        collective_id=collective_id, has_side_effects=True, vmem_limit_bytes=LIMIT
    )


def space_forward(x, cot, perm, w, so):
    V = pltpu.VMEM
    sds = jax.ShapeDtypeStruct
    return pl.pallas_call(
        space_forward_kernel,
        out_shape=(
            sds((FR, NP, PL, 256), BF),
            sds((FR, 8, ALL), F32),
            sds((FR, 128, ALL), F32),
            sds((TOK, D), BF),
            sds((NF, SLAB, D), BF),
            sds((NF, SLAB, D), BF),
        ),
        in_specs=[vmem(), vmem(), vmem(), anywhere(), anywhere()],
        out_specs=(anywhere(), vmem(), vmem(), vmem(), vmem(), vmem()),
        scratch_shapes=[
            V((8, 432, D), BF), V((D, D), BF), V((TOK, D), BF), V((NP, FR, PL, 256), BF),
            V((FR, NP, PL, 256), BF), V((ALL, 128), BF), V((ALL, 128), BF), V((128, ALL), BF),
            V((ALL, QT), F32), V((ALL, QT), BF),
            V((FR, NP, GRP, 256), BF), V((FR, NP, GRP, 256), BF), V((TOK, D), BF),
            V((NF, SLAB, D), BF), V((NF, SLAB, D), BF), V((NF, SLAB, D), BF), V((NF, SLAB, D), BF),
            DMA((8, 3)), DMA, DMA((FR, NP)), DMA((FR, NP)), DMA((FR, NP)), DMA((FR, NP)),
            DMA((NF,)), DMA((NF,)), DMA((NF,)), DMA((NF,)), DMA((FR,)),
        ],
        compiler_params=params(1),
    )(x, cot, perm, w, so)


def time_kernel(
    stream, cot, mask, unperm, order_hbm, w_hbm, to_hbm,
    up_out, grad_out,
    w, wo, order, hat, qkv, back, mixed, probs, dqkv, usend, urecv, asend, arecv, msend, mrecv,
    wsem, tosem, ordsem, uss, urs, mss, mrs,
):
    p = lax.axis_index("pos")
    f = lax.axis_index("frame")
    par = lax.rem(p, 2)
    mate = p + 1 - 2 * par
    barrier = pltpu.get_barrier_semaphore()
    greet(barrier, p, f, False, True)
    pl.semaphore_signal(barrier, inc=1, device_id={"pos": mate})
    order_copy = pltpu.make_async_copy(order_hbm, order, ordsem)
    to_copy = pltpu.make_async_copy(to_hbm, wo, tosem)
    to_copy.start()
    w_copies = [pltpu.make_async_copy(w_hbm.at[pl.ds(c * D, D)], w.at[c], wsem.at[c]) for c in range(3)]
    for c in w_copies:
        c.start()
    order_copy.start()
    normed, inv = normalize(stream[...])
    hat[...] = normed
    normed = normed.astype(BF)
    to_copy.wait()
    back[...] = dot(cot[...], wo[...], 1, 0).astype(BF)
    for c in range(3):
        w_copies[c].wait()
        qkv[c] = dot(normed, w[c], 1, 1).astype(BF)
    order_copy.wait()
    for e in range(2):
        asend[e] = dot(cot[...], order[e], 1, 0).astype(BF)
    mixed[...] = jnp.zeros_like(mixed)
    dqkv[...] = jnp.zeros_like(dqkv)

    def window(h):
        off = (h * HD) % 128
        start = h * HD - off
        width = 128 if off + HD <= 128 else 256
        lane = lax.broadcasted_iota(jnp.int32, (1, width), 1)
        keep = ((lane >= off) & (lane < off + HD)).astype(F32).astype(BF)
        return slice(start, start + width), keep

    for h in range(HEADS):
        win, keep = window(h)
        s = dot(qkv[0, :, win] * keep, qkv[1, :, win], 1, 1) * SCALE + mask[...]
        e = jnp.exp(s - jnp.max(s, axis=1, keepdims=True))
        prob = e * (1.0 / jnp.sum(e, axis=1, keepdims=True))
        probs[h] = prob
        mixed[:, win] += dot(prob.astype(BF), qkv[2, :, win] * keep, 1, 0)
    msend[...] = mixed[...].astype(BF)
    pl.semaphore_wait(barrier, NF)
    a_copy = send(asend.at[1 - par], arecv, mss.at[0], mrs.at[0], "pos", mate)
    m_copy = send(msend, mrecv, mss.at[1], mrs.at[1], "pos", mate)
    a_copy.start()
    m_copy.start()
    for h in range(HEADS):
        win, keep = window(h)
        k, q = qkv[1, :, win] * keep, qkv[0, :, win] * keep
        b = back[:, win] * keep
        prob = probs[h]
        gp = dot(b, qkv[2, :, win], 1, 1)
        gs = prob * (gp - jnp.sum(prob * gp, axis=1, keepdims=True)) * SCALE
        gs = gs.astype(BF)
        dqkv[0, :, win] += dot(gs, k, 1, 0)
        dqkv[1, :, win] += dot(gs, q, 0, 0)
        dqkv[2, :, win] += dot(prob.astype(BF), b, 0, 0)
    grad_hat = dot(dqkv[0].astype(BF), w[0], 1, 0)
    for c in range(1, 3):
        grad_hat += dot(dqkv[c].astype(BF), w[c], 1, 0)
    up = cot[...].astype(F32) + norm_back(grad_hat, hat[...], inv)
    usend[...] = up.astype(BF).reshape(NF, SLAB, D)

    def u_copy(s):
        to = lax.rem(f + s, NF)
        return send(usend.at[to], urecv.at[f], uss.at[s], urs.at[s], "frame", to)

    @pl.loop(1, NF)
    def _(s):
        u_copy(s).start()

    urecv[pl.ds(f, 1)] = usend[pl.ds(f, 1)]
    a_copy.wait()
    m_copy.wait()
    mine = asend.at[par]
    for r in range(0, GH, 128):
        part = dot(mine[:, r : r + 128], msend[...], 0, 0)
        part += dot(arecv[:, r : r + 128], mrecv[...], 0, 0)
        grad_out[r : r + 128] = part.astype(BF)

    @pl.loop(1, NF)
    def _(s):
        u_copy(s).wait()

    up_out[...] = dot(unperm[...], urecv[...].reshape(TT, D), 1, 0).astype(BF)


def time_block(stream, cot, mask, unperm, order, w, wo):
    V = pltpu.VMEM
    sds = jax.ShapeDtypeStruct
    return pl.pallas_call(
        time_kernel,
        out_shape=(sds((TOK, D), BF), sds((GH, D), BF)),
        in_specs=[vmem(), vmem(), vmem(), vmem(), anywhere(), anywhere(), anywhere()],
        out_specs=(vmem(), vmem()),
        scratch_shapes=[
            V((3, D, D), BF), V((D, D), BF), V((2, D, GH), BF), V((TT, D), F32), V((3, TT, D), BF),
            V((TT, D), BF), V((TT, D), F32), V((HEADS, TT, TT), F32), V((3, TT, D), F32),
            V((NF, SLAB, D), BF), V((NF, SLAB, D), BF),
            V((2, TT, GH), BF), V((TT, GH), BF), V((TT, D), BF), V((TT, D), BF),
            DMA((3,)), DMA, DMA, DMA((NF,)), DMA((NF,)), DMA((2,)), DMA((2,)),
        ],
        compiler_params=params(2),
    )(stream, cot, mask, unperm, order, w, wo)


def space_backward_kernel(
    x, up, mixed, spread, stat, att, order_hbm, qkv_hbm, gt_hbm, w_hbm, so_hbm,
    grad_out, sums_out,
    w, so, order, qkv, bsend, brecv, gpart, grecv, hsend, hrecv, asend, arecv, mrecv,
    qbuf, kbuf, vbuf, bbuf, kt, pbuf, sbuf, dq, dk, dv, rsend, rrecv,
    wsem, sosem, ordsem, qsem, gsem, bss, brs, gss, grs, hss, hrs, rss, rrs, mss, mrs,
):
    p = lax.axis_index("pos")
    f = lax.axis_index("frame")
    barrier = pltpu.get_barrier_semaphore()
    par = lax.rem(p, 2)
    chip = p // 2
    mate = p + 1 - 2 * par
    greet(barrier, p, f, True, True)
    so_copy = pltpu.make_async_copy(so_hbm, so, sosem)
    so_copy.start()
    order_copy = pltpu.make_async_copy(order_hbm, order, ordsem)
    order_copy.start()
    qkv_copy = pltpu.make_async_copy(qkv_hbm, qkv, qsem)
    qkv_copy.start()
    gt_copy = pltpu.make_async_copy(gt_hbm, gpart.at[0], gsem)
    gt_copy.start()
    w_copy = pltpu.make_async_copy(w_hbm, w, wsem)
    w_copy.start()
    so_copy.wait()
    back = dot(up[...], so[...], 1, 0)
    back = back.reshape(FR, 3, GRP, D)
    for h in range(HEADS):
        bsend[:, h] = pack([lanes(back[:, g], h) for g in range(3)])
    pl.semaphore_wait(barrier, NP - 1 + NF - 1)

    def b_copy(fr, s):
        to = lax.rem(p + s, NP)
        return send(bsend.at[fr, to], brecv.at[fr, p], bss.at[fr, s], brs.at[fr, s], "pos", to)

    for fr in range(FR):

        @pl.loop(1, NP)
        def _(s):
            b_copy(fr, s).start()

    brecv[:, pl.ds(p, 1)] = bsend[:, pl.ds(p, 1)]

    def g_copy(g, s):
        to = lax.rem(f + s, NF)
        rows = pl.ds(pl.multiple_of(to * GS, 16), GS)
        return send(gpart.at[g, rows], grecv.at[g, f], gss.at[g, s], grs.at[g, s], "frame", to)

    m_copy = send(mixed, mrecv, mss.at[1], mrs.at[1], "pos", mate)
    m_copy.start()
    gt_copy.wait()

    @pl.loop(1, NF)
    def _(s):
        g_copy(0, s).start()

    order_copy.wait()
    for e in range(2):
        asend[e] = dot(up[...], order[e], 1, 0).astype(BF)
    a_copy = send(asend.at[1 - par], arecv, mss.at[0], mrs.at[0], "pos", mate)
    a_copy.start()
    a_copy.wait()
    m_copy.wait()
    mine = asend.at[par]
    for r in range(0, GH, 128):
        part = dot(mine[:, r : r + 128], mixed[...], 0, 0)
        part += dot(arecv[:, r : r + 128], mrecv[...], 0, 0)
        gpart[1, r : r + 128] = part.astype(BF)

    @pl.loop(1, NF)
    def _(s):
        g_copy(1, s).start()

    for g in range(2):
        grecv[g, pl.ds(f, 1)] = gpart[g, pl.ds(pl.multiple_of(f * GS, 16), GS)][None]

    def r_copy(fr, s):
        to = lax.rem(p + s, NP)
        return send(rsend.at[fr, to], rrecv.at[fr, p], rss.at[fr, s], rrs.at[fr, s], "pos", to)

    qkv_copy.wait()
    lane = lax.broadcasted_iota(jnp.int32, (1, 128), 1)
    keep = (lane < HD).astype(F32).astype(BF)
    for fr in range(FR):
        rows = qkv[fr].reshape(ALL, 256)
        zeros = jnp.zeros((ALL, 128 - HD), BF)
        qbuf[...] = rows[:, :128] * keep
        k = rows[:, HD : HD + 128] * keep
        kbuf[...] = k
        kt[...] = k.T
        vbuf[...] = jnp.concatenate([rows[:, 2 * HD : 3 * HD], zeros], axis=1)
        dk[...] = jnp.zeros_like(dk)
        dv[...] = jnp.zeros_like(dv)

        @pl.loop(1, NP)
        def _(s):
            b_copy(fr, s).wait_recv()

        got = brecv[fr]
        zeros = jnp.zeros((NP, GRP, 128 - HD), BF)
        for g in range(3):
            bbuf[:, g * GRP : (g + 1) * GRP] = jnp.concatenate([lanes(got, g), zeros], axis=-1)

        @pl.loop(0, ALL // BT)
        def _(t):
            at = pl.ds(pl.multiple_of(t * BT, BT), BT)
            q = qbuf[at]
            b = bbuf.reshape(ALL, 128)[at]
            total = jnp.sum(b.astype(F32).T * att[fr, :, at], axis=0, keepdims=True)
            lse = stat[fr, 0:1, at]
            for k in range(0, ALL, KC):
                s = dot(kbuf[k : k + KC], q, 1, 1)
                gp = dot(vbuf[k : k + KC], b, 1, 1)
                prob = jnp.exp2(s * (SCALE * LOG2E) - lse)
                pbuf[k : k + KC] = prob.astype(BF)
                sbuf[k : k + KC] = (prob * (gp - total)).astype(BF)
            dv[...] += dot(pbuf[...], b, 1, 0)
            dk[...] += dot(sbuf[...], q, 1, 0)
            dq[at] = dot(kt[...], sbuf[...], 1, 0).T

        val = jnp.concatenate(
            [
                dq[:, :HD] * SCALE,
                dk[:, :HD] * SCALE,
                dv[:, :HD],
                jnp.zeros((ALL, 256 - 3 * HD), F32),
            ],
            axis=1,
        )
        rsend[fr] = val.astype(BF).reshape(NP, PL, 256)

        @pl.loop(1, NP)
        def _(s):
            r_copy(fr, s).start()

        rrecv[fr, pl.ds(p, 1)] = rsend[fr, pl.ds(p, 1)]

    def h_copy(g, s):
        to = lax.rem(chip + s, NK)
        return send(
            hsend.at[g, to], hrecv.at[g, chip], hss.at[g, s], hrs.at[g, s], "pos", 2 * to + par
        )

    for g in range(2):

        @pl.loop(1, NF)
        def _(s):
            g_copy(g, s).wait_recv()

        total = grecv[g, 0].astype(F32)
        for s in range(1, NF):
            total += grecv[g, s].astype(F32)
        hsend[g] = dot(spread[...], total.astype(BF), 1, 0).astype(BF).reshape(NK, 16, D)

        @pl.loop(1, NK)
        def _(s):
            h_copy(g, s).start()

        hrecv[g, pl.ds(chip, 1)] = hsend[g, pl.ds(chip, 1)]

    w_copy.wait()
    for fr in range(FR):

        @pl.loop(1, NP)
        def _(s):
            r_copy(fr, s).wait_recv()

        got = [rrecv[fr, h].astype(F32) for h in range(HEADS)]
        grad_hat = jnp.zeros((PL, D), F32)
        for c in range(3):
            part = jnp.concatenate([v[:, c * HD : (c + 1) * HD] for v in got], axis=1)
            grad_hat += dot(part.astype(BF), w[c * D : (c + 1) * D], 1, 0)
        here = slice(fr * PL, (fr + 1) * PL)
        normed, inv = normalize(x[here])
        grad_out[here] = (up[here].astype(F32) + norm_back(grad_hat, normed, inv)).astype(BF)

    for g in range(2):

        @pl.loop(1, NK)
        def _(s):
            h_copy(g, s).wait_recv()

        total = hrecv[g, 0].astype(F32)
        for s in range(1, NK):
            total += hrecv[g, s].astype(F32)
        sums_out[g] = total

    @pl.loop(1, NP)
    def _(s):
        for fr in range(FR):
            b_copy(fr, s).wait_send()
            r_copy(fr, s).wait_send()

    @pl.loop(1, NF)
    def _(s):
        for g in range(2):
            g_copy(g, s).wait_send()

    @pl.loop(1, NK)
    def _(s):
        for g in range(2):
            h_copy(g, s).wait_send()


def space_backward(x, up, mixed, spread, stat, att, order, qkv, gt, w, so):
    V = pltpu.VMEM
    sds = jax.ShapeDtypeStruct
    return pl.pallas_call(
        space_backward_kernel,
        out_shape=(sds((TOK, D), BF), sds((2, 16, D), F32)),
        in_specs=[vmem()] * 6 + [anywhere()] * 5,
        out_specs=(vmem(), vmem()),
        scratch_shapes=[
            V((3 * D, D), BF), V((D, D), BF), V((2, D, GH), BF), V((FR, NP, PL, 256), BF),
            V((FR, NP, GRP, 256), BF), V((FR, NP, GRP, 256), BF),
            V((2, GH, D), BF), V((2, NF, GS, D), BF), V((2, NK, 16, D), BF), V((2, NK, 16, D), BF),
            V((2, TOK, GH), BF), V((TOK, GH), BF), V((TOK, D), BF),
            V((ALL, 128), BF), V((ALL, 128), BF), V((ALL, 128), BF), V((NP, PL, 128), BF),
            V((128, ALL), BF),
            V((ALL, BT), BF), V((ALL, BT), BF),
            V((ALL, 128), F32), V((ALL, 128), F32), V((ALL, 128), F32),
            V((FR, NP, PL, 256), BF), V((FR, NP, PL, 256), BF),
            DMA, DMA, DMA, DMA, DMA, DMA((FR, NP)), DMA((FR, NP)), DMA((2, NF)), DMA((2, NF)),
            DMA((2, NK)), DMA((2, NK)), DMA((FR, NP)), DMA((FR, NP)), DMA((2,)), DMA((2,)),
        ],
        compiler_params=params(3),
    )(x, up, mixed, spread, stat, att, order, qkv, gt, w, so)


def finish_kernel(grad, sums, grad_out, gs_out, gt_out, sem):
    copy = pltpu.make_async_copy(grad, grad_out, sem)
    copy.start()
    gt_out[...] = sums[0, :GR]
    gs_out[...] = sums[1, :GR]
    copy.wait()


def finish(grad, sums):
    sds = jax.ShapeDtypeStruct
    return pl.pallas_call(
        finish_kernel,
        out_shape=(sds((TOK, D), BF), sds((GR, D), F32), sds((GR, D), F32)),
        in_specs=[anywhere(), vmem()],
        out_specs=(anywhere(), vmem(), vmem()),
        scratch_shapes=[DMA],
    )(grad, sums)


def tables():
    row = np.arange(TT)
    slab, inner = row // SLAB, row % SLAB
    real = inner < FR * TP
    col = (inner // TP) * PL + slab * TP + inner % TP
    perm = (real[:, None] & (col[:, None] == np.arange(TOK)[None])).astype(np.float32)
    place = np.where(real, inner % TP, -1)
    mask = np.where(place[:, None] == place[None], 0.0, -1e30).astype(np.float32)
    row = np.arange(NK * 16)
    spread = (row % 16 < GR)[:, None] & (((row // 16) * GR + row % 16)[:, None] == np.arange(GS)[None])
    col = np.arange(2 * GH)
    core, slab, inner = col // GH, col % GH // GS, col % GS
    source = (slab * NP + 2 * (inner // GR) + core) * GR + inner % GR
    order = (inner < NK * GR)[None] & (np.arange(D)[:, None] == source[None])
    order = order.reshape(D, 2, GH).transpose(1, 0, 2)
    return [jnp.asarray(t.astype(np.float32), BF) for t in (perm, perm.T, spread, order)] + [
        jnp.asarray(mask)
    ]


def shards(inputs, cotangent, space_projection, space_output, time_projection, time_output):
    perm, unperm, spread, order, mask = tables()
    x = inputs.reshape(TOK, D)
    cot = cotangent.reshape(TOK, D)
    qkv, stat, att, mixed, stream_t, cot_t = space_forward(x, cot, perm, space_projection, space_output)
    up, gt = time_block(
        stream_t.reshape(TT, D), cot_t.reshape(TT, D), mask, unperm, order, time_projection, time_output
    )
    grad, sums = space_backward(
        x, up, mixed, spread, stat, att, order, qkv, gt, space_projection, space_output
    )
    grad, gs, gt = finish(grad, sums)
    return grad.reshape(FR, PL, D), gs, gt


def solution(mesh):
    return jax.shard_map(
        shards,
        mesh=mesh,
        in_specs=(P("frame", "pos", None), P("frame", "pos", None), P(), P(), P(), P()),
        out_specs=(P("frame", "pos", None), P(("frame", "pos"), None), P(("frame", "pos"), None)),
        check_vma=False,
    )
```

```python
import jax
import jax.numpy as jnp
import numpy as np
from jax import lax
from jax.experimental import pallas as pl
from jax.experimental.pallas import tpu as pltpu
from jax.sharding import PartitionSpec as P

HEADS = 16
EPS = 1e-06
BF = jnp.bfloat16
F32 = jnp.float32
D = 1152
HD = 72
NP = 16
NF = 8
FR = 2
PL = 96
TOK = FR * PL
ALL = NP * PL
TP = PL // NF
SLAB = 32
TT = NF * SLAB
GR = D // NF // NP
NK = NP // 2
GS = 80
GH = NF * GS
GRP = PL // 3
SCALE = HD ** (-0.5)
LOG2E = 1.4426950408889634
QT = 384
BT = 256
KC = 256
LIMIT = 60 * 1024 * 1024


def dot(a, b, ca, cb):
    return lax.dot_general(a, b, (((ca,), (cb,)), ((), ())), preferred_element_type=F32)


def normalize(tokens):
    values = tokens.astype(F32)
    center = values - jnp.mean(values, axis=-1, keepdims=True)
    inv_std = lax.rsqrt(jnp.mean(center * center, axis=-1, keepdims=True) + EPS)
    return center * inv_std, inv_std


def norm_back(grad_hat, normed, inv_std):
    mean_grad = jnp.mean(grad_hat, axis=-1, keepdims=True)
    mean_proj = jnp.mean(grad_hat * normed, axis=-1, keepdims=True)
    return inv_std * (grad_hat - mean_grad - normed * mean_proj)


def pos_peer(p, s, sign):
    v = 7 - (s // 2 + 7) % 8
    x, z = lax.rem(p // 8 + v // 4, 2), lax.rem(lax.rem(p // 2, 4) + sign * (v % 4) + 4, 4)
    return 8 * x + 2 * z + lax.rem(lax.rem(p, 2) + s % 2, 2)


def pack(parts):
    shape = parts[0].shape[:-1] + (256 - 3 * HD,)
    return jnp.concatenate(list(parts) + [jnp.zeros(shape, F32)], axis=-1).astype(BF)


def lanes(value, g):
    return value[..., g * HD : (g + 1) * HD]


def greet(barrier, p, f, pos, frame):
    if pos:

        @pl.loop(1, NP)
        def _(s):
            pl.semaphore_signal(barrier, inc=1, device_id={"pos": lax.rem(p + s, NP)})

    if frame:

        @pl.loop(1, NF)
        def _(s):
            pl.semaphore_signal(barrier, inc=1, device_id={"frame": lax.rem(f + s, NF)})


def send(src, dst, send_sem, recv_sem, axis, dest):
    return pltpu.make_async_remote_copy(
        src_ref=src, dst_ref=dst, send_sem=send_sem, recv_sem=recv_sem, device_id={axis: dest}
    )


def space_forward_kernel(
    x, cot, perm, w_hbm, so_hbm,
    qkv_out, stat_out, att_out, mixed_out, stream_out, cot_out,
    w, so, hat, qsend, qkv, kbuf, qbuf, vt, sbuf, pbuf, osend, orecv, stream, fsend, frecv, csend, crecv,
    wsem, sosem, qss, qrs, oss, ors, fss, frs, css, crs, outsem,
):
    p = lax.axis_index("pos")
    f = lax.axis_index("frame")
    par = lax.rem(p, 2)
    barrier = pltpu.get_barrier_semaphore()
    greet(barrier, p, f, True, True)

    def w_copy(i, c):
        pair = pos_peer(p, 2 * i, 1) // 2
        rows = pl.ds(pl.multiple_of(c * D + pair * 144, 16), 144)
        return pltpu.make_async_copy(w_hbm.at[rows], w.at[i, pl.ds(c * 144, 144)], wsem.at[i, c])

    for i in range(8):
        for c in range(3):
            w_copy(i, c).start()
    so_copy = pltpu.make_async_copy(so_hbm, so, sosem)
    so_copy.start()
    hat[...] = normalize(x[...])[0].astype(BF)
    pl.semaphore_wait(barrier, NP - 1 + NF - 1)

    def q_copy(fr, s):
        return send(qsend.at[s, fr], qkv.at[fr, p], qss.at[fr, s], qrs.at[fr, s], "pos", pos_peer(p, s, 1))

    @pl.loop(0, 8)
    def _(i):
        for c in range(3):
            w_copy(i, c).wait()
        r = dot(hat[...], w[i], 1, 1)
        pad = jnp.zeros((TOK, 256 - 3 * HD), F32)
        for e in range(2):
            part = [r[:, c * 144 + e * HD : c * 144 + e * HD + HD] for c in range(3)]
            val = jnp.concatenate(part + [pad], axis=1).astype(BF)
            qsend[2 * i + lax.rem(par + e, 2)] = val.reshape(FR, PL, 256)

        @pl.when(i > 0)
        def _():
            q_copy(0, 2 * i).start()

        q_copy(0, 2 * i + 1).start()

    @pl.loop(1, NP)
    def _(s):
        q_copy(1, s).start()

    qkv[:, pl.ds(p, 1)] = qsend[0][:, None]

    def c_copy(s):
        to = lax.rem(f + s, NF)
        return send(csend.at[to], crecv.at[f], css.at[s], crs.at[s], "frame", to)

    csend[...] = dot(perm[...], cot[...], 1, 0).astype(BF).reshape(NF, SLAB, D)

    @pl.loop(1, NF)
    def _(s):
        c_copy(s).start()

    crecv[pl.ds(f, 1)] = csend[pl.ds(f, 1)]

    def o_copy(fr, s):
        to = lax.rem(p + s, NP)
        return send(osend.at[fr, to], orecv.at[fr, p], oss.at[fr, s], ors.at[fr, s], "pos", to)

    outs = []
    for fr in range(FR):

        @pl.loop(1, NP)
        def _(s):
            q_copy(fr, s).wait_recv()

        out = pltpu.make_async_copy(qkv.at[fr], qkv_out.at[fr], outsem.at[fr])
        out.start()
        outs.append(out)
        rows = qkv[fr].reshape(ALL, 256)
        lane = lax.broadcasted_iota(jnp.int32, (1, 128), 1)
        keep = (lane < HD).astype(F32).astype(BF)
        zeros = jnp.zeros((ALL, 128 - HD), BF)
        qbuf[...] = rows[:, :128] * keep
        kbuf[...] = rows[:, HD : HD + 128]
        vt[...] = jnp.concatenate([rows[:, 2 * HD : 3 * HD], zeros], axis=1).T

        @pl.loop(0, ALL // QT)
        def _(t):
            tile = lax.rem(p // 4 + t, ALL // QT)
            at = pl.ds(pl.multiple_of(tile * QT, QT), QT)
            q = qbuf[at]
            top = jnp.full((8, QT), -jnp.inf, F32)
            for k in range(0, ALL, KC):
                s = dot(kbuf[k : k + KC], q, 1, 1)
                sbuf[k : k + KC] = s
                top = jnp.maximum(top, jnp.max(s.reshape(KC // 8, 8, QT), axis=0))
            top = jnp.max(top, axis=0, keepdims=True) * (SCALE * LOG2E)
            total = jnp.zeros((8, QT), F32)
            for k in range(0, ALL, KC):
                e = jnp.exp2(sbuf[k : k + KC] * (SCALE * LOG2E) - top)
                total = total + jnp.sum(e.reshape(KC // 8, 8, QT), axis=0)
                pbuf[k : k + KC] = e.astype(BF)
            total = jnp.sum(total, axis=0, keepdims=True)
            o = dot(vt[...], pbuf[...], 1, 0) * (1.0 / total)
            stat_out[fr, :, at] = jnp.broadcast_to(top + jnp.log(total) * LOG2E, (8, QT))
            att_out[fr, :, at] = o
            turned = o.T.reshape(4, 3, GRP, 128)
            osend[fr, pl.ds(tile * 4, 4)] = pack([turned[:, g, :, :HD] for g in range(3)])
            for j in range(4):
                to = tile * 4 + j

                @pl.when(to != p)
                def _():
                    o_copy(fr, lax.rem(to - p + NP, NP)).start()

        orecv[fr, pl.ds(p, 1)] = osend[fr, pl.ds(p, 1)]

    so_copy.wait()
    for fr in range(FR):

        @pl.loop(1, NP)
        def _(s):
            o_copy(fr, s).wait_recv()

        got = [orecv[fr, h].astype(F32) for h in range(HEADS)]
        mixed = jnp.concatenate(
            [jnp.concatenate([lanes(v, g) for v in got], axis=1) for g in range(3)], axis=0
        ).astype(BF)
        part = slice(fr * PL, (fr + 1) * PL)
        mixed_out[part] = mixed
        stream[part] = (x[part].astype(F32) + dot(mixed, so[...], 1, 1)).astype(BF)

    def f_copy(s):
        to = lax.rem(f + s, NF)
        return send(fsend.at[to], frecv.at[f], fss.at[s], frs.at[s], "frame", to)

    fsend[...] = dot(perm[...], stream[...], 1, 0).astype(BF).reshape(NF, SLAB, D)

    @pl.loop(1, NF)
    def _(s):
        f_copy(s).start()

    frecv[pl.ds(f, 1)] = fsend[pl.ds(f, 1)]

    @pl.loop(1, NF)
    def _(s):
        c_copy(s).wait_recv()

    cot_out[...] = crecv[...]

    @pl.loop(1, NP)
    def _(s):
        for fr in range(FR):
            q_copy(fr, s).wait_send()
            o_copy(fr, s).wait_send()

    for out in outs:
        out.wait()

    @pl.loop(1, NF)
    def _(s):
        f_copy(s).wait_recv()

    stream_out[...] = frecv[...]

    @pl.loop(1, NF)
    def _(s):
        c_copy(s).wait_send()
        f_copy(s).wait_send()


def vmem():
    return pl.BlockSpec(memory_space=pltpu.VMEM)


def anywhere():
    return pl.BlockSpec(memory_space=pl.ANY)


DMA = pltpu.SemaphoreType.DMA


def params(collective_id):
    return pltpu.CompilerParams(
        collective_id=collective_id, has_side_effects=True, vmem_limit_bytes=LIMIT
    )


def space_forward(x, cot, perm, w, so):
    V = pltpu.VMEM
    sds = jax.ShapeDtypeStruct
    return pl.pallas_call(
        space_forward_kernel,
        out_shape=(
            sds((FR, NP, PL, 256), BF),
            sds((FR, 8, ALL), F32),
            sds((FR, 128, ALL), F32),
            sds((TOK, D), BF),
            sds((NF, SLAB, D), BF),
            sds((NF, SLAB, D), BF),
        ),
        in_specs=[vmem(), vmem(), vmem(), anywhere(), anywhere()],
        out_specs=(anywhere(), vmem(), vmem(), vmem(), vmem(), vmem()),
        scratch_shapes=[
            V((8, 432, D), BF), V((D, D), BF), V((TOK, D), BF), V((NP, FR, PL, 256), BF),
            V((FR, NP, PL, 256), BF), V((ALL, 128), BF), V((ALL, 128), BF), V((128, ALL), BF),
            V((ALL, QT), F32), V((ALL, QT), BF),
            V((FR, NP, GRP, 256), BF), V((FR, NP, GRP, 256), BF), V((TOK, D), BF),
            V((NF, SLAB, D), BF), V((NF, SLAB, D), BF), V((NF, SLAB, D), BF), V((NF, SLAB, D), BF),
            DMA((8, 3)), DMA, DMA((FR, NP)), DMA((FR, NP)), DMA((FR, NP)), DMA((FR, NP)),
            DMA((NF,)), DMA((NF,)), DMA((NF,)), DMA((NF,)), DMA((FR,)),
        ],
        compiler_params=params(1),
    )(x, cot, perm, w, so)


def rest_kernel(
    stream, cot, mask, unperm, spread, x, mixed, stat, att,
    order_hbm, tw_hbm, to_hbm, qkv_hbm, w_hbm, so_hbm,
    grad_out, sums_out,
    w, wo, so, order, hat, tqkv, back, tmixed, probs, dqkv, usend, urecv, up,
    tasend, tarecv, tmsend, tmrecv, asend, arecv, mrecv,
    qkv, bsend, brecv, gpart, grecv, hsend, hrecv,
    qbuf, kbuf, vbuf, bbuf, kt, pbuf, sbuf, dq, dk, dv, rsend, rrecv,
    wsem, tosem, sosem, ordsem, qsem, uss, urs, mss, mrs, bss, brs, gss, grs, hss, hrs, rss, rrs,
):
    p = lax.axis_index("pos")
    f = lax.axis_index("frame")
    par = lax.rem(p, 2)
    chip = p // 2
    mate = p + 1 - 2 * par
    barrier = pltpu.get_barrier_semaphore()
    greet(barrier, p, f, True, True)
    to_copy = pltpu.make_async_copy(to_hbm, wo, tosem)
    to_copy.start()
    tw_copies = [
        pltpu.make_async_copy(tw_hbm.at[pl.ds(c * D, D)], w.at[c], wsem.at[c]) for c in range(3)
    ]
    for c in tw_copies:
        c.start()
    order_copy = pltpu.make_async_copy(order_hbm, order, ordsem)
    order_copy.start()
    so_copy = pltpu.make_async_copy(so_hbm, so, sosem)
    so_copy.start()
    qkv_copy = pltpu.make_async_copy(qkv_hbm, qkv, qsem)
    qkv_copy.start()

    normed, inv = normalize(stream[...])
    hat[...] = normed
    normed = normed.astype(BF)
    to_copy.wait()
    back[...] = dot(cot[...], wo[...], 1, 0).astype(BF)
    for c in range(3):
        tw_copies[c].wait()
        tqkv[c] = dot(normed, w[c], 1, 1).astype(BF)
    order_copy.wait()
    for e in range(2):
        tasend[e] = dot(cot[...], order[e], 1, 0).astype(BF)
    tmixed[...] = jnp.zeros_like(tmixed)
    dqkv[...] = jnp.zeros_like(dqkv)

    def window(h):
        off = (h * HD) % 128
        start = h * HD - off
        width = 128 if off + HD <= 128 else 256
        lane = lax.broadcasted_iota(jnp.int32, (1, width), 1)
        keep = ((lane >= off) & (lane < off + HD)).astype(F32).astype(BF)
        return slice(start, start + width), keep

    for h in range(HEADS):
        win, keep = window(h)
        s = dot(tqkv[0, :, win] * keep, tqkv[1, :, win], 1, 1) * SCALE + mask[...]
        e = jnp.exp(s - jnp.max(s, axis=1, keepdims=True))
        prob = e * (1.0 / jnp.sum(e, axis=1, keepdims=True))
        probs[h] = prob
        tmixed[:, win] += dot(prob.astype(BF), tqkv[2, :, win] * keep, 1, 0)
    tmsend[...] = tmixed[...].astype(BF)
    pl.semaphore_wait(barrier, NP - 1 + NF - 1)
    ta_copy = send(tasend.at[1 - par], tarecv, mss.at[0], mrs.at[0], "pos", mate)
    tm_copy = send(tmsend, tmrecv, mss.at[1], mrs.at[1], "pos", mate)
    m_copy = send(mixed, mrecv, mss.at[2], mrs.at[2], "pos", mate)
    ta_copy.start()
    tm_copy.start()
    m_copy.start()
    for h in range(HEADS):
        win, keep = window(h)
        k, q = tqkv[1, :, win] * keep, tqkv[0, :, win] * keep
        b = back[:, win] * keep
        prob = probs[h]
        gp = dot(b, tqkv[2, :, win], 1, 1)
        gs = prob * (gp - jnp.sum(prob * gp, axis=1, keepdims=True)) * SCALE
        gs = gs.astype(BF)
        dqkv[0, :, win] += dot(gs, k, 1, 0)
        dqkv[1, :, win] += dot(gs, q, 0, 0)
        dqkv[2, :, win] += dot(prob.astype(BF), b, 0, 0)
    grad_hat = dot(dqkv[0].astype(BF), w[0], 1, 0)
    for c in range(1, 3):
        grad_hat += dot(dqkv[c].astype(BF), w[c], 1, 0)
    turned = cot[...].astype(F32) + norm_back(grad_hat, hat[...], inv)
    usend[...] = turned.astype(BF).reshape(NF, SLAB, D)

    def u_copy(s):
        to = lax.rem(f + s, NF)
        return send(usend.at[to], urecv.at[f], uss.at[s], urs.at[s], "frame", to)

    @pl.loop(1, NF)
    def _(s):
        u_copy(s).start()

    urecv[pl.ds(f, 1)] = usend[pl.ds(f, 1)]

    w_copies = [
        pltpu.make_async_copy(w_hbm.at[pl.ds(c * D, D)], w.at[c], wsem.at[c]) for c in range(3)
    ]
    for c in w_copies:
        c.start()

    def g_copy(g, s):
        to = lax.rem(f + s, NF)
        rows = pl.ds(pl.multiple_of(to * GS, 16), GS)
        return send(gpart.at[g, rows], grecv.at[g, f], gss.at[g, s], grs.at[g, s], "frame", to)

    def gradient(g, mine, left, theirs, right):
        for r in range(0, GH, 128):
            part = dot(mine[:, r : r + 128], left[...], 0, 0)
            part += dot(theirs[:, r : r + 128], right[...], 0, 0)
            gpart[g, r : r + 128] = part.astype(BF)

        @pl.loop(1, NF)
        def _(s):
            g_copy(g, s).start()

        grecv[g, pl.ds(f, 1)] = gpart[g, pl.ds(pl.multiple_of(f * GS, 16), GS)][None]

    ta_copy.wait()
    tm_copy.wait()
    gradient(0, tasend.at[par], tmsend, tarecv, tmrecv)

    qkv_copy.wait()
    so_copy.wait()
    lane = lax.broadcasted_iota(jnp.int32, (1, 128), 1)
    keep = (lane < HD).astype(F32).astype(BF)
    zeros = jnp.zeros((ALL, 128 - HD), BF)
    for fr in range(FR):
        rows = qkv[fr].reshape(ALL, 256)
        qbuf[fr] = rows[:, :128] * keep
        k = rows[:, HD : HD + 128] * keep
        kbuf[fr] = k
        kt[fr] = k.T
        vbuf[fr] = jnp.concatenate([rows[:, 2 * HD : 3 * HD], zeros], axis=1)

    @pl.loop(1, NF)
    def _(s):
        u_copy(s).wait_recv()

    up[...] = dot(unperm[...], urecv[...].reshape(TT, D), 1, 0).astype(BF)

    sback = dot(up[...], so[...], 1, 0).reshape(FR, 3, GRP, D)
    for h in range(HEADS):
        bsend[:, h] = pack([lanes(sback[:, g], h) for g in range(3)])

    def b_copy(fr, s):
        to, dst = pos_peer(p, s, 1), p
        return send(bsend.at[fr, to], brecv.at[fr, dst], bss.at[fr, s], brs.at[fr, s], "pos", to)

    for fr in range(FR):

        @pl.loop(1, NP)
        def _(s):
            b_copy(fr, s).start()

    brecv[:, pl.ds(p, 1)] = bsend[:, pl.ds(p, 1)]
    for e in range(2):
        asend[e] = dot(up[...], order[e], 1, 0).astype(BF)
    a_copy = send(asend.at[1 - par], arecv, mss.at[3], mrs.at[3], "pos", mate)
    a_copy.start()
    a_copy.wait()
    m_copy.wait()
    gradient(1, asend.at[par], mixed, arecv, mrecv)

    def r_copy(fr, s):
        to = pos_peer(p, s, 1)
        return send(rsend.at[fr, to], rrecv.at[fr, p], rss.at[fr, s], rrs.at[fr, s], "pos", to)

    def h_copy(g, s):
        to = lax.rem(chip + s, NK)
        return send(
            hsend.at[g, to], hrecv.at[g, chip], hss.at[g, s], hrs.at[g, s], "pos", 2 * to + par
        )

    for fr in range(FR):
        dk[...] = jnp.zeros_like(dk)
        dv[...] = jnp.zeros_like(dv)

        @pl.loop(1, NP)
        def _(s):
            b_copy(fr, s).wait_recv()

        got = brecv[fr]
        zeros = jnp.zeros((NP, GRP, 128 - HD), BF)
        for g in range(3):
            bbuf[:, g * GRP : (g + 1) * GRP] = jnp.concatenate([lanes(got, g), zeros], axis=-1)

        @pl.loop(0, ALL // BT)
        def _(t):
            at = pl.ds(pl.multiple_of(t * BT, BT), BT)
            q = qbuf[fr, at]
            b = bbuf.reshape(ALL, 128)[at]
            total = jnp.sum(b.astype(F32).T * att[fr, :, at], axis=0, keepdims=True)
            lse = stat[fr, 0:1, at]
            for k in range(0, ALL, KC):
                s = dot(kbuf[fr, k : k + KC], q, 1, 1)
                gp = dot(vbuf[fr, k : k + KC], b, 1, 1)
                prob = jnp.exp2(s * (SCALE * LOG2E) - lse)
                pbuf[k : k + KC] = prob.astype(BF)
                sbuf[k : k + KC] = (prob * (gp - total)).astype(BF)
            dv[...] += dot(pbuf[...], b, 1, 0)
            dk[...] += dot(sbuf[...], q, 1, 0)
            dq[at] = dot(kt[fr], sbuf[...], 1, 0).T

        val = pack([dq[:, :HD] * SCALE, dk[:, :HD] * SCALE, dv[:, :HD]])
        rsend[fr] = val.reshape(NP, PL, 256)

        @pl.loop(1, NP)
        def _(s):
            r_copy(fr, s).start()

        rrecv[fr, pl.ds(p, 1)] = rsend[fr, pl.ds(p, 1)]

    def spread_out(g):
        @pl.loop(1, NF)
        def _(s):
            g_copy(g, s).wait_recv()

        total = grecv[g, 0].astype(F32)
        for s in range(1, NF):
            total += grecv[g, s].astype(F32)
        hsend[g] = dot(spread[...], total.astype(BF), 1, 0).astype(BF).reshape(NK, 16, D)

        @pl.loop(1, NK)
        def _(s):
            h_copy(g, s).start()

        hrecv[g, pl.ds(chip, 1)] = hsend[g, pl.ds(chip, 1)]

    def finish_rows(fr):
        @pl.loop(1, NP)
        def _(s):
            r_copy(fr, s).wait_recv()

        got = [rrecv[fr, h].astype(F32) for h in range(HEADS)]
        grad_hat = jnp.zeros((PL, D), F32)
        for c in range(3):
            part = jnp.concatenate([lanes(v, c) for v in got], axis=1)
            grad_hat += dot(part.astype(BF), w[c], 1, 0)
        here = slice(fr * PL, (fr + 1) * PL)
        normed, inv = normalize(x[here])
        grad_out[here] = (up[here].astype(F32) + norm_back(grad_hat, normed, inv)).astype(BF)

    spread_out(0)
    for c in w_copies:
        c.wait()
    finish_rows(0)
    spread_out(1)
    finish_rows(1)
    for g in range(2):

        @pl.loop(1, NK)
        def _(s):
            h_copy(g, s).wait_recv()

        total = hrecv[g, 0].astype(F32)
        for s in range(1, NK):
            total += hrecv[g, s].astype(F32)
        sums_out[g] = total

    @pl.loop(1, NP)
    def _(s):
        for fr in range(FR):
            b_copy(fr, s).wait_send()
            r_copy(fr, s).wait_send()

    @pl.loop(1, NF)
    def _(s):
        u_copy(s).wait_send()
        for g in range(2):
            g_copy(g, s).wait_send()

    @pl.loop(1, NK)
    def _(s):
        for g in range(2):
            h_copy(g, s).wait_send()


def rest(stream, cot, mask, unperm, spread, x, mixed, stat, att, order, tw, wo, qkv, w, so):
    V = pltpu.VMEM
    sds = jax.ShapeDtypeStruct
    return pl.pallas_call(
        rest_kernel,
        out_shape=(sds((TOK, D), BF), sds((2, 16, D), F32)),
        in_specs=[vmem()] * 9 + [anywhere()] * 6,
        out_specs=(vmem(), vmem()),
        scratch_shapes=[
            V((3, D, D), BF), V((D, D), BF), V((D, D), BF), V((2, D, GH), BF), V((TT, D), F32),
            V((3, TT, D), BF), V((TT, D), BF), V((TT, D), F32), V((HEADS, TT, TT), F32),
            V((3, TT, D), F32), V((NF, SLAB, D), BF), V((NF, SLAB, D), BF), V((TOK, D), BF),
            V((2, TT, GH), BF), V((TT, GH), BF), V((TT, D), BF), V((TT, D), BF),
            V((2, TOK, GH), BF), V((TOK, GH), BF), V((TOK, D), BF),
            V((FR, NP, PL, 256), BF), V((FR, NP, GRP, 256), BF), V((FR, NP, GRP, 256), BF),
            V((2, GH, D), BF), V((2, NF, GS, D), BF), V((2, NK, 16, D), BF), V((2, NK, 16, D), BF),
            V((FR, ALL, 128), BF), V((FR, ALL, 128), BF), V((FR, ALL, 128), BF),
            V((NP, PL, 128), BF), V((FR, 128, ALL), BF),
            V((ALL, BT), BF), V((ALL, BT), BF),
            V((ALL, 128), F32), V((ALL, 128), F32), V((ALL, 128), F32),
            V((FR, NP, PL, 256), BF), V((FR, NP, PL, 256), BF),
            DMA((3,)), DMA, DMA, DMA, DMA, DMA((NF,)), DMA((NF,)), DMA((4,)), DMA((4,)),
            DMA((FR, NP)), DMA((FR, NP)), DMA((2, NF)), DMA((2, NF)),
            DMA((2, NK)), DMA((2, NK)), DMA((FR, NP)), DMA((FR, NP)),
        ],
        compiler_params=params(2),
    )(stream, cot, mask, unperm, spread, x, mixed, stat, att, order, tw, wo, qkv, w, so)


def finish_kernel(grad, sums, grad_out, gs_out, gt_out):
    grad_out[...] = grad[...]
    gt_out[...] = sums[0, :GR]
    gs_out[...] = sums[1, :GR]


def finish(grad, sums):
    sds = jax.ShapeDtypeStruct
    return pl.pallas_call(
        finish_kernel,
        out_shape=(sds((TOK, D), BF), sds((GR, D), F32), sds((GR, D), F32)),
        in_specs=[vmem(), vmem()],
        out_specs=(vmem(), vmem(), vmem()),
    )(grad, sums)


def tables():
    row = np.arange(TT)
    slab, inner = row // SLAB, row % SLAB
    real = inner < FR * TP
    col = (inner // TP) * PL + slab * TP + inner % TP
    perm = (real[:, None] & (col[:, None] == np.arange(TOK)[None])).astype(np.float32)
    place = np.where(real, inner % TP, -1)
    mask = np.where(place[:, None] == place[None], 0.0, -1e30).astype(np.float32)
    row = np.arange(NK * 16)
    spread = (row % 16 < GR)[:, None] & (((row // 16) * GR + row % 16)[:, None] == np.arange(GS)[None])
    col = np.arange(2 * GH)
    core, slab, inner = col // GH, col % GH // GS, col % GS
    source = (slab * NP + 2 * (inner // GR) + core) * GR + inner % GR
    order = (inner < NK * GR)[None] & (np.arange(D)[:, None] == source[None])
    order = order.reshape(D, 2, GH).transpose(1, 0, 2)
    return [jnp.asarray(t.astype(np.float32), BF) for t in (perm, perm.T, spread, order)] + [
        jnp.asarray(mask)
    ]


def shards(inputs, cotangent, space_projection, space_output, time_projection, time_output):
    perm, unperm, spread, order, mask = tables()
    x = inputs.reshape(TOK, D)
    cot = cotangent.reshape(TOK, D)
    qkv, stat, att, mixed, stream_t, cot_t = space_forward(x, cot, perm, space_projection, space_output)
    grad, sums = rest(
        stream_t.reshape(TT, D), cot_t.reshape(TT, D), mask, unperm, spread, x, mixed, stat, att,
        order, time_projection, time_output, qkv, space_projection, space_output,
    )
    grad, gs, gt = finish(grad, sums)
    return grad.reshape(FR, PL, D), gs, gt


def solution(mesh):
    return jax.shard_map(
        shards,
        mesh=mesh,
        in_specs=(P("frame", "pos", None), P("frame", "pos", None), P(), P(), P(), P()),
        out_specs=(P("frame", "pos", None), P(("frame", "pos"), None), P(("frame", "pos"), None)),
        check_vma=False,
    )
```

```python
import jax
import jax.numpy as jnp
import numpy as np
from jax import lax
from jax.experimental import pallas as pl
from jax.experimental.pallas import tpu as pltpu
from jax.sharding import PartitionSpec as P

HEADS = 16
EPS = 1e-06
BF = jnp.bfloat16
F32 = jnp.float32
D = 1152
HD = 72
NP = 16
NF = 8
FR = 2
PL = 96
TOK = FR * PL
ALL = NP * PL
TP = PL // NF
SLAB = 32
TT = NF * SLAB
GR = D // NF // NP
NK = NP // 2
GS = 80
GH = NF * GS
GRP = PL // 3
SCALE = HD ** (-0.5)
LOG2E = 1.4426950408889634
QT = 384
BT = 256
KC = 256
LIMIT = 60 * 1024 * 1024


def dot(a, b, ca, cb):
    return lax.dot_general(a, b, (((ca,), (cb,)), ((), ())), preferred_element_type=F32)


def normalize(tokens):
    values = tokens.astype(F32)
    center = values - jnp.mean(values, axis=-1, keepdims=True)
    inv_std = lax.rsqrt(jnp.mean(center * center, axis=-1, keepdims=True) + EPS)
    return center * inv_std, inv_std


def norm_back(grad_hat, normed, inv_std):
    mean_grad = jnp.mean(grad_hat, axis=-1, keepdims=True)
    mean_proj = jnp.mean(grad_hat * normed, axis=-1, keepdims=True)
    return inv_std * (grad_hat - mean_grad - normed * mean_proj)


def pos_peer(p, s, sign):
    v = 7 - (s // 2 + 7) % 8
    x, z = lax.rem(p // 8 + v // 4, 2), lax.rem(lax.rem(p // 2, 4) + sign * (v % 4) + 4, 4)
    return 8 * x + 2 * z + lax.rem(lax.rem(p, 2) + s % 2, 2)


def pack(parts):
    shape = parts[0].shape[:-1] + (256 - 3 * HD,)
    return jnp.concatenate(list(parts) + [jnp.zeros(shape, F32)], axis=-1).astype(BF)


def lanes(value, g):
    return value[..., g * HD : (g + 1) * HD]


def greet(barrier, p, f, pos, frame):
    if pos:

        @pl.loop(1, NP)
        def _(s):
            pl.semaphore_signal(barrier, inc=1, device_id={"pos": lax.rem(p + s, NP)})

    if frame:

        @pl.loop(1, NF)
        def _(s):
            pl.semaphore_signal(barrier, inc=1, device_id={"frame": lax.rem(f + s, NF)})


def send(src, dst, send_sem, recv_sem, axis, dest):
    return pltpu.make_async_remote_copy(
        src_ref=src, dst_ref=dst, send_sem=send_sem, recv_sem=recv_sem, device_id={axis: dest}
    )


def space_forward_kernel(
    x, cot, perm, w_hbm, so_hbm,
    qkv_out, stat_out, att_out, mixed_out, stream_out, cot_out,
    w, so, hat, qsend, qkv, kbuf, qbuf, vt, sbuf, pbuf, osend, orecv, stream, fsend, frecv, csend, crecv,
    wsem, sosem, qss, qrs, oss, ors, fss, frs, css, crs, outsem,
):
    p = lax.axis_index("pos")
    f = lax.axis_index("frame")
    par = lax.rem(p, 2)
    barrier = pltpu.get_barrier_semaphore()
    greet(barrier, p, f, True, True)

    def w_copy(i, c):
        pair = pos_peer(p, 2 * i, 1) // 2
        rows = pl.ds(pl.multiple_of(c * D + pair * 144, 16), 144)
        return pltpu.make_async_copy(w_hbm.at[rows], w.at[i, pl.ds(c * 144, 144)], wsem.at[i, c])

    for i in range(8):
        for c in range(3):
            w_copy(i, c).start()
    so_copy = pltpu.make_async_copy(so_hbm, so, sosem)
    so_copy.start()
    hat[...] = normalize(x[...])[0].astype(BF)
    pl.semaphore_wait(barrier, NP - 1 + NF - 1)

    def q_copy(fr, s):
        return send(qsend.at[s, fr], qkv.at[fr, p], qss.at[fr, s], qrs.at[fr, s], "pos", pos_peer(p, s, 1))

    @pl.loop(0, 8)
    def _(i):
        for c in range(3):
            w_copy(i, c).wait()
        r = dot(hat[...], w[i], 1, 1)
        pad = jnp.zeros((TOK, 256 - 3 * HD), F32)
        for e in range(2):
            part = [r[:, c * 144 + e * HD : c * 144 + e * HD + HD] for c in range(3)]
            val = jnp.concatenate(part + [pad], axis=1).astype(BF)
            qsend[2 * i + lax.rem(par + e, 2)] = val.reshape(FR, PL, 256)

        @pl.when(i > 0)
        def _():
            q_copy(0, 2 * i).start()

        q_copy(0, 2 * i + 1).start()

    @pl.loop(1, NP)
    def _(s):
        q_copy(1, s).start()

    qkv[:, pl.ds(p, 1)] = qsend[0][:, None]

    def c_copy(s):
        to = lax.rem(f + s, NF)
        return send(csend.at[to], crecv.at[f], css.at[s], crs.at[s], "frame", to)

    csend[...] = dot(perm[...], cot[...], 1, 0).astype(BF).reshape(NF, SLAB, D)

    @pl.loop(1, NF)
    def _(s):
        c_copy(s).start()

    crecv[pl.ds(f, 1)] = csend[pl.ds(f, 1)]

    def o_copy(fr, s):
        to = lax.rem(p + s, NP)
        return send(osend.at[fr, to], orecv.at[fr, p], oss.at[fr, s], ors.at[fr, s], "pos", to)

    outs = []
    for fr in range(FR):

        @pl.loop(1, NP)
        def _(s):
            q_copy(fr, s).wait_recv()

        out = pltpu.make_async_copy(qkv.at[fr], qkv_out.at[fr], outsem.at[fr])
        out.start()
        outs.append(out)
        rows = qkv[fr].reshape(ALL, 256)
        lane = lax.broadcasted_iota(jnp.int32, (1, 128), 1)
        keep = (lane < HD).astype(F32).astype(BF)
        zeros = jnp.zeros((ALL, 128 - HD), BF)
        qbuf[...] = rows[:, :128] * keep
        kbuf[...] = rows[:, HD : HD + 128]
        vt[...] = jnp.concatenate([rows[:, 2 * HD : 3 * HD], zeros], axis=1).T

        @pl.loop(0, ALL // QT)
        def _(t):
            tile = lax.rem(p // 4 + t, ALL // QT)
            at = pl.ds(pl.multiple_of(tile * QT, QT), QT)
            q = qbuf[at]
            top = jnp.full((8, QT), -jnp.inf, F32)
            for k in range(0, ALL, KC):
                s = dot(kbuf[k : k + KC], q, 1, 1)
                sbuf[k : k + KC] = s
                top = jnp.maximum(top, jnp.max(s.reshape(KC // 8, 8, QT), axis=0))
            top = jnp.max(top, axis=0, keepdims=True) * (SCALE * LOG2E)
            total = jnp.zeros((8, QT), F32)
            for k in range(0, ALL, KC):
                e = jnp.exp2(sbuf[k : k + KC] * (SCALE * LOG2E) - top)
                total = total + jnp.sum(e.reshape(KC // 8, 8, QT), axis=0)
                pbuf[k : k + KC] = e.astype(BF)
            total = jnp.sum(total, axis=0, keepdims=True)
            o = dot(vt[...], pbuf[...], 1, 0) * (1.0 / total)
            stat_out[fr, :, at] = jnp.broadcast_to(top + jnp.log(total) * LOG2E, (8, QT))
            att_out[fr, :, at] = o
            turned = o.T.reshape(4, 3, GRP, 128)
            osend[fr, pl.ds(tile * 4, 4)] = pack([turned[:, g, :, :HD] for g in range(3)])
            for j in range(4):
                to = tile * 4 + j

                @pl.when(to != p)
                def _():
                    o_copy(fr, lax.rem(to - p + NP, NP)).start()

        orecv[fr, pl.ds(p, 1)] = osend[fr, pl.ds(p, 1)]

    so_copy.wait()
    for fr in range(FR):

        @pl.loop(1, NP)
        def _(s):
            o_copy(fr, s).wait_recv()

        got = [orecv[fr, h].astype(F32) for h in range(HEADS)]
        mixed = jnp.concatenate(
            [jnp.concatenate([lanes(v, g) for v in got], axis=1) for g in range(3)], axis=0
        ).astype(BF)
        part = slice(fr * PL, (fr + 1) * PL)
        mixed_out[part] = mixed
        stream[part] = (x[part].astype(F32) + dot(mixed, so[...], 1, 1)).astype(BF)

    def f_copy(s):
        to = lax.rem(f + s, NF)
        return send(fsend.at[to], frecv.at[f], fss.at[s], frs.at[s], "frame", to)

    fsend[...] = dot(perm[...], stream[...], 1, 0).astype(BF).reshape(NF, SLAB, D)

    @pl.loop(1, NF)
    def _(s):
        f_copy(s).start()

    frecv[pl.ds(f, 1)] = fsend[pl.ds(f, 1)]

    @pl.loop(1, NF)
    def _(s):
        c_copy(s).wait_recv()

    cot_out[...] = crecv[...]

    @pl.loop(1, NP)
    def _(s):
        for fr in range(FR):
            q_copy(fr, s).wait_send()
            o_copy(fr, s).wait_send()

    for out in outs:
        out.wait()

    @pl.loop(1, NF)
    def _(s):
        f_copy(s).wait_recv()

    stream_out[...] = frecv[...]

    @pl.loop(1, NF)
    def _(s):
        c_copy(s).wait_send()
        f_copy(s).wait_send()


def vmem():
    return pl.BlockSpec(memory_space=pltpu.VMEM)


def anywhere():
    return pl.BlockSpec(memory_space=pl.ANY)


DMA = pltpu.SemaphoreType.DMA


def params(collective_id):
    return pltpu.CompilerParams(
        collective_id=collective_id, has_side_effects=True, vmem_limit_bytes=LIMIT
    )


def space_forward(x, cot, perm, w, so):
    V = pltpu.VMEM
    sds = jax.ShapeDtypeStruct
    return pl.pallas_call(
        space_forward_kernel,
        out_shape=(
            sds((FR, NP, PL, 256), BF),
            sds((FR, 8, ALL), F32),
            sds((FR, 128, ALL), F32),
            sds((TOK, D), BF),
            sds((NF, SLAB, D), BF),
            sds((NF, SLAB, D), BF),
        ),
        in_specs=[vmem(), vmem(), vmem(), anywhere(), anywhere()],
        out_specs=(anywhere(), vmem(), vmem(), vmem(), vmem(), vmem()),
        scratch_shapes=[
            V((8, 432, D), BF), V((D, D), BF), V((TOK, D), BF), V((NP, FR, PL, 256), BF),
            V((FR, NP, PL, 256), BF), V((ALL, 128), BF), V((ALL, 128), BF), V((128, ALL), BF),
            V((ALL, QT), F32), V((ALL, QT), BF),
            V((FR, NP, GRP, 256), BF), V((FR, NP, GRP, 256), BF), V((TOK, D), BF),
            V((NF, SLAB, D), BF), V((NF, SLAB, D), BF), V((NF, SLAB, D), BF), V((NF, SLAB, D), BF),
            DMA((8, 3)), DMA, DMA((FR, NP)), DMA((FR, NP)), DMA((FR, NP)), DMA((FR, NP)),
            DMA((NF,)), DMA((NF,)), DMA((NF,)), DMA((NF,)), DMA((FR,)),
        ],
        compiler_params=params(1),
    )(x, cot, perm, w, so)


def rest_kernel(
    stream, cot, mask, unperm, spread, x, mixed, stat, att,
    order_hbm, tw_hbm, to_hbm, qkv_hbm, w_hbm, so_hbm,
    grad_out, sums_out,
    w, wo, so, order, hat, tqkv, back, tmixed, probs, dqkv, usend, urecv, up,
    tasend, tarecv, tmsend, tmrecv, asend, arecv, mrecv,
    qkv, bsend, brecv, gpart, grecv, xsend, xrecv, hsend, hrecv,
    qbuf, kbuf, vbuf, bbuf, kt, pbuf, sbuf, dq, dk, dv, rsend, rrecv,
    wsem, tosem, sosem, ordsem, qsem, uss, urs, mss, mrs, bss, brs, gss, grs, xss, xrs, hss, hrs, rss, rrs,
):
    p = lax.axis_index("pos")
    f = lax.axis_index("frame")
    par = lax.rem(p, 2)
    chip = p // 2
    y, half = lax.rem(f, 4), f // 4
    mate = p + 1 - 2 * par
    barrier = pltpu.get_barrier_semaphore()
    greet(barrier, p, f, True, True)
    to_copy = pltpu.make_async_copy(to_hbm, wo, tosem)
    to_copy.start()
    tw_copies = [
        pltpu.make_async_copy(tw_hbm.at[pl.ds(c * D, D)], w.at[c], wsem.at[c]) for c in range(3)
    ]
    for c in tw_copies:
        c.start()
    order_copy = pltpu.make_async_copy(order_hbm, order, ordsem)
    order_copy.start()
    so_copy = pltpu.make_async_copy(so_hbm, so, sosem)
    so_copy.start()
    qkv_copy = pltpu.make_async_copy(qkv_hbm, qkv, qsem)
    qkv_copy.start()

    normed, inv = normalize(stream[...])
    hat[...] = normed
    normed = normed.astype(BF)
    to_copy.wait()
    back[...] = dot(cot[...], wo[...], 1, 0).astype(BF)
    for c in range(3):
        tw_copies[c].wait()
        tqkv[c] = dot(normed, w[c], 1, 1).astype(BF)
    order_copy.wait()
    for e in range(2):
        tasend[e] = dot(cot[...], order[e], 1, 0).astype(BF)
    tmixed[...] = jnp.zeros_like(tmixed)
    dqkv[...] = jnp.zeros_like(dqkv)

    def window(h):
        off = (h * HD) % 128
        start = h * HD - off
        width = 128 if off + HD <= 128 else 256
        lane = lax.broadcasted_iota(jnp.int32, (1, width), 1)
        keep = ((lane >= off) & (lane < off + HD)).astype(F32).astype(BF)
        return slice(start, start + width), keep

    for h in range(HEADS):
        win, keep = window(h)
        s = dot(tqkv[0, :, win] * keep, tqkv[1, :, win], 1, 1) * SCALE + mask[...]
        e = jnp.exp(s - jnp.max(s, axis=1, keepdims=True))
        prob = e * (1.0 / jnp.sum(e, axis=1, keepdims=True))
        probs[h] = prob
        tmixed[:, win] += dot(prob.astype(BF), tqkv[2, :, win] * keep, 1, 0)
    tmsend[...] = tmixed[...].astype(BF)
    pl.semaphore_wait(barrier, NP - 1 + NF - 1)
    ta_copy = send(tasend.at[1 - par], tarecv, mss.at[0], mrs.at[0], "pos", mate)
    tm_copy = send(tmsend, tmrecv, mss.at[1], mrs.at[1], "pos", mate)
    m_copy = send(mixed, mrecv, mss.at[2], mrs.at[2], "pos", mate)
    ta_copy.start()
    tm_copy.start()
    m_copy.start()
    for h in range(HEADS):
        win, keep = window(h)
        k, q = tqkv[1, :, win] * keep, tqkv[0, :, win] * keep
        b = back[:, win] * keep
        prob = probs[h]
        gp = dot(b, tqkv[2, :, win], 1, 1)
        gs = prob * (gp - jnp.sum(prob * gp, axis=1, keepdims=True)) * SCALE
        gs = gs.astype(BF)
        dqkv[0, :, win] += dot(gs, k, 1, 0)
        dqkv[1, :, win] += dot(gs, q, 0, 0)
        dqkv[2, :, win] += dot(prob.astype(BF), b, 0, 0)
    grad_hat = dot(dqkv[0].astype(BF), w[0], 1, 0)
    for c in range(1, 3):
        grad_hat += dot(dqkv[c].astype(BF), w[c], 1, 0)
    turned = cot[...].astype(F32) + norm_back(grad_hat, hat[...], inv)
    usend[...] = turned.astype(BF).reshape(NF, SLAB, D)

    def u_copy(s):
        to = lax.rem(f + s, NF)
        return send(usend.at[to], urecv.at[f], uss.at[s], urs.at[s], "frame", to)

    @pl.loop(1, NF)
    def _(s):
        u_copy(s).start()

    urecv[pl.ds(f, 1)] = usend[pl.ds(f, 1)]

    w_copies = [
        pltpu.make_async_copy(w_hbm.at[pl.ds(c * D, D)], w.at[c], wsem.at[c]) for c in range(3)
    ]
    for c in w_copies:
        c.start()

    def g_copy(g, s):
        to = lax.rem(y + s, 4)
        rows = pl.ds(pl.multiple_of(to * 2 * GS, 16), 2 * GS)
        return send(
            gpart.at[g, rows], grecv.at[g, y], gss.at[g, s], grs.at[g, s], "frame", 4 * half + to
        )

    def gradient(g, mine, left, theirs, right):
        for r in range(0, GH, 128):
            part = dot(mine[:, r : r + 128], left[...], 0, 0)
            part += dot(theirs[:, r : r + 128], right[...], 0, 0)
            gpart[g, r : r + 128] = part.astype(BF)

        @pl.loop(1, 4)
        def _(s):
            g_copy(g, s).start()

        grecv[g, pl.ds(y, 1)] = gpart[g, pl.ds(pl.multiple_of(y * 2 * GS, 16), 2 * GS)][None]

    ta_copy.wait()
    tm_copy.wait()
    gradient(0, tasend.at[par], tmsend, tarecv, tmrecv)

    qkv_copy.wait()
    so_copy.wait()
    lane = lax.broadcasted_iota(jnp.int32, (1, 128), 1)
    keep = (lane < HD).astype(F32).astype(BF)
    zeros = jnp.zeros((ALL, 128 - HD), BF)
    for fr in range(FR):
        rows = qkv[fr].reshape(ALL, 256)
        qbuf[fr] = rows[:, :128] * keep
        k = rows[:, HD : HD + 128] * keep
        kbuf[fr] = k
        kt[fr] = k.T
        vbuf[fr] = jnp.concatenate([rows[:, 2 * HD : 3 * HD], zeros], axis=1)

    @pl.loop(1, NF)
    def _(s):
        u_copy(s).wait_recv()

    up[...] = dot(unperm[...], urecv[...].reshape(TT, D), 1, 0).astype(BF)

    sback = dot(up[...], so[...], 1, 0).reshape(FR, 3, GRP, D)
    for h in range(HEADS):
        bsend[:, h] = pack([lanes(sback[:, g], h) for g in range(3)])

    def b_copy(fr, s):
        to, dst = pos_peer(p, s, 1), p
        return send(bsend.at[fr, to], brecv.at[fr, dst], bss.at[fr, s], brs.at[fr, s], "pos", to)

    for fr in range(FR):

        @pl.loop(1, NP)
        def _(s):
            b_copy(fr, s).start()

    brecv[:, pl.ds(p, 1)] = bsend[:, pl.ds(p, 1)]
    for e in range(2):
        asend[e] = dot(up[...], order[e], 1, 0).astype(BF)
    a_copy = send(asend.at[1 - par], arecv, mss.at[3], mrs.at[3], "pos", mate)
    a_copy.start()
    a_copy.wait()
    m_copy.wait()
    gradient(1, asend.at[par], mixed, arecv, mrecv)

    def r_copy(fr, s):
        to = pos_peer(p, s, 1)
        return send(rsend.at[fr, to], rrecv.at[fr, p], rss.at[fr, s], rrs.at[fr, s], "pos", to)

    def h_copy(g, s):
        to = lax.rem(chip + s, NK)
        return send(
            hsend.at[g, to], hrecv.at[g, chip], hss.at[g, s], hrs.at[g, s], "pos", 2 * to + par
        )

    def x_copy(g):
        to = 4 * (1 - half) + y
        return send(xsend.at[g, 1 - half], xrecv.at[g], xss.at[g], xrs.at[g], "frame", to)

    def fold(g):
        @pl.loop(1, 4)
        def _(s):
            g_copy(g, s).wait_recv()

        total = grecv[g, 0].astype(F32)
        for s in range(1, 4):
            total += grecv[g, s].astype(F32)
        xsend[g] = total.astype(BF).reshape(2, GS, D)
        x_copy(g).start()

    for fr in range(FR):
        dk[...] = jnp.zeros_like(dk)
        dv[...] = jnp.zeros_like(dv)

        @pl.loop(1, NP)
        def _(s):
            b_copy(fr, s).wait_recv()

        got = brecv[fr]
        zeros = jnp.zeros((NP, GRP, 128 - HD), BF)
        for g in range(3):
            bbuf[:, g * GRP : (g + 1) * GRP] = jnp.concatenate([lanes(got, g), zeros], axis=-1)

        @pl.loop(0, ALL // BT)
        def _(t):
            at = pl.ds(pl.multiple_of(t * BT, BT), BT)
            q = qbuf[fr, at]
            b = bbuf.reshape(ALL, 128)[at]
            total = jnp.sum(b.astype(F32).T * att[fr, :, at], axis=0, keepdims=True)
            lse = stat[fr, 0:1, at]
            for k in range(0, ALL, KC):
                s = dot(kbuf[fr, k : k + KC], q, 1, 1)
                gp = dot(vbuf[fr, k : k + KC], b, 1, 1)
                prob = jnp.exp2(s * (SCALE * LOG2E) - lse)
                pbuf[k : k + KC] = prob.astype(BF)
                sbuf[k : k + KC] = (prob * (gp - total)).astype(BF)
            dv[...] += dot(pbuf[...], b, 1, 0)
            dk[...] += dot(sbuf[...], q, 1, 0)
            dq[at] = dot(kt[fr], sbuf[...], 1, 0).T

        val = pack([dq[:, :HD] * SCALE, dk[:, :HD] * SCALE, dv[:, :HD]])
        rsend[fr] = val.reshape(NP, PL, 256)

        @pl.loop(1, NP)
        def _(s):
            r_copy(fr, s).start()

        rrecv[fr, pl.ds(p, 1)] = rsend[fr, pl.ds(p, 1)]
        if fr == 0:
            fold(0)

    def spread_out(g):
        x_copy(g).wait_recv()
        total = xsend[g, half].astype(F32) + xrecv[g].astype(F32)
        hsend[g] = dot(spread[...], total.astype(BF), 1, 0).astype(BF).reshape(NK, 16, D)

        @pl.loop(1, NK)
        def _(s):
            h_copy(g, s).start()

        hrecv[g, pl.ds(chip, 1)] = hsend[g, pl.ds(chip, 1)]

    def finish_rows(fr):
        @pl.loop(1, NP)
        def _(s):
            r_copy(fr, s).wait_recv()

        got = [rrecv[fr, h].astype(F32) for h in range(HEADS)]
        grad_hat = jnp.zeros((PL, D), F32)
        for c in range(3):
            part = jnp.concatenate([lanes(v, c) for v in got], axis=1)
            grad_hat += dot(part.astype(BF), w[c], 1, 0)
        here = slice(fr * PL, (fr + 1) * PL)
        normed, inv = normalize(x[here])
        grad_out[here] = (up[here].astype(F32) + norm_back(grad_hat, normed, inv)).astype(BF)

    spread_out(0)
    for c in w_copies:
        c.wait()
    finish_rows(0)
    fold(1)
    spread_out(1)
    finish_rows(1)
    for g in range(2):

        @pl.loop(1, NK)
        def _(s):
            h_copy(g, s).wait_recv()

        total = hrecv[g, 0].astype(F32)
        for s in range(1, NK):
            total += hrecv[g, s].astype(F32)
        sums_out[g] = total

    @pl.loop(1, NP)
    def _(s):
        for fr in range(FR):
            b_copy(fr, s).wait_send()
            r_copy(fr, s).wait_send()

    @pl.loop(1, NF)
    def _(s):
        u_copy(s).wait_send()

    @pl.loop(1, 4)
    def _(s):
        for g in range(2):
            g_copy(g, s).wait_send()

    for g in range(2):
        x_copy(g).wait_send()

    @pl.loop(1, NK)
    def _(s):
        for g in range(2):
            h_copy(g, s).wait_send()


def rest(stream, cot, mask, unperm, spread, x, mixed, stat, att, order, tw, wo, qkv, w, so):
    V = pltpu.VMEM
    sds = jax.ShapeDtypeStruct
    return pl.pallas_call(
        rest_kernel,
        out_shape=(sds((TOK, D), BF), sds((2, 16, D), F32)),
        in_specs=[vmem()] * 9 + [anywhere()] * 6,
        out_specs=(vmem(), vmem()),
        scratch_shapes=[
            V((3, D, D), BF), V((D, D), BF), V((D, D), BF), V((2, D, GH), BF), V((TT, D), F32),
            V((3, TT, D), BF), V((TT, D), BF), V((TT, D), F32), V((HEADS, TT, TT), F32),
            V((3, TT, D), F32), V((NF, SLAB, D), BF), V((NF, SLAB, D), BF), V((TOK, D), BF),
            V((2, TT, GH), BF), V((TT, GH), BF), V((TT, D), BF), V((TT, D), BF),
            V((2, TOK, GH), BF), V((TOK, GH), BF), V((TOK, D), BF),
            V((FR, NP, PL, 256), BF), V((FR, NP, GRP, 256), BF), V((FR, NP, GRP, 256), BF),
            V((2, GH, D), BF), V((2, 4, 2 * GS, D), BF),
            V((2, 2, GS, D), BF), V((2, GS, D), BF), V((2, NK, 16, D), BF), V((2, NK, 16, D), BF),
            V((FR, ALL, 128), BF), V((FR, ALL, 128), BF), V((FR, ALL, 128), BF),
            V((NP, PL, 128), BF), V((FR, 128, ALL), BF),
            V((ALL, BT), BF), V((ALL, BT), BF),
            V((ALL, 128), F32), V((ALL, 128), F32), V((ALL, 128), F32),
            V((FR, NP, PL, 256), BF), V((FR, NP, PL, 256), BF),
            DMA((3,)), DMA, DMA, DMA, DMA, DMA((NF,)), DMA((NF,)), DMA((4,)), DMA((4,)),
            DMA((FR, NP)), DMA((FR, NP)), DMA((2, 4)), DMA((2, 4)),
            DMA((2,)), DMA((2,)), DMA((2, NK)), DMA((2, NK)), DMA((FR, NP)), DMA((FR, NP)),
        ],
        compiler_params=params(2),
    )(stream, cot, mask, unperm, spread, x, mixed, stat, att, order, tw, wo, qkv, w, so)


def finish_kernel(grad, sums, grad_out, gs_out, gt_out):
    grad_out[...] = grad[...]
    gt_out[...] = sums[0, :GR]
    gs_out[...] = sums[1, :GR]


def finish(grad, sums):
    sds = jax.ShapeDtypeStruct
    return pl.pallas_call(
        finish_kernel,
        out_shape=(sds((TOK, D), BF), sds((GR, D), F32), sds((GR, D), F32)),
        in_specs=[vmem(), vmem()],
        out_specs=(vmem(), vmem(), vmem()),
    )(grad, sums)


def tables():
    row = np.arange(TT)
    slab, inner = row // SLAB, row % SLAB
    real = inner < FR * TP
    col = (inner // TP) * PL + slab * TP + inner % TP
    perm = (real[:, None] & (col[:, None] == np.arange(TOK)[None])).astype(np.float32)
    place = np.where(real, inner % TP, -1)
    mask = np.where(place[:, None] == place[None], 0.0, -1e30).astype(np.float32)
    row = np.arange(NK * 16)
    spread = (row % 16 < GR)[:, None] & (((row // 16) * GR + row % 16)[:, None] == np.arange(GS)[None])
    col = np.arange(2 * GH)
    core, slab, inner = col // GH, col % GH // GS, col % GS
    frame = slab % 2 * 4 + slab // 2
    source = (frame * NP + 2 * (inner // GR) + core) * GR + inner % GR
    order = (inner < NK * GR)[None] & (np.arange(D)[:, None] == source[None])
    order = order.reshape(D, 2, GH).transpose(1, 0, 2)
    return [jnp.asarray(t.astype(np.float32), BF) for t in (perm, perm.T, spread, order)] + [
        jnp.asarray(mask)
    ]


def shards(inputs, cotangent, space_projection, space_output, time_projection, time_output):
    perm, unperm, spread, order, mask = tables()
    x = inputs.reshape(TOK, D)
    cot = cotangent.reshape(TOK, D)
    qkv, stat, att, mixed, stream_t, cot_t = space_forward(x, cot, perm, space_projection, space_output)
    grad, sums = rest(
        stream_t.reshape(TT, D), cot_t.reshape(TT, D), mask, unperm, spread, x, mixed, stat, att,
        order, time_projection, time_output, qkv, space_projection, space_output,
    )
    grad, gs, gt = finish(grad, sums)
    return grad.reshape(FR, PL, D), gs, gt


def solution(mesh):
    return jax.shard_map(
        shards,
        mesh=mesh,
        in_specs=(P("frame", "pos", None), P("frame", "pos", None), P(), P(), P(), P()),
        out_specs=(P("frame", "pos", None), P(("frame", "pos"), None), P(("frame", "pos"), None)),
        check_vma=False,
    )
```

```python
import jax
import jax.numpy as jnp
import numpy as np
from jax import lax
from jax.experimental import pallas as pl
from jax.experimental.pallas import tpu as pltpu
from jax.sharding import PartitionSpec as P

HEADS = 16
EPS = 1e-06
BF = jnp.bfloat16
F32 = jnp.float32
D = 1152
HD = 72
NP = 16
NF = 8
FR = 2
PL = 96
TOK = FR * PL
ALL = NP * PL
TP = PL // NF
SLAB = 32
TT = NF * SLAB
GR = D // NF // NP
NK = NP // 2
GS = 80
GH = NF * GS
GRP = PL // 3
SCALE = HD ** (-0.5)
LOG2E = 1.4426950408889634
QT = 384
BT = 256
KC = 256
LIMIT = 60 * 1024 * 1024


def dot(a, b, ca, cb):
    return lax.dot_general(a, b, (((ca,), (cb,)), ((), ())), preferred_element_type=F32)


def normalize(tokens):
    values = tokens.astype(F32)
    center = values - jnp.mean(values, axis=-1, keepdims=True)
    inv_std = lax.rsqrt(jnp.mean(center * center, axis=-1, keepdims=True) + EPS)
    return center * inv_std, inv_std


def norm_back(grad_hat, normed, inv_std):
    mean_grad = jnp.mean(grad_hat, axis=-1, keepdims=True)
    mean_proj = jnp.mean(grad_hat * normed, axis=-1, keepdims=True)
    return inv_std * (grad_hat - mean_grad - normed * mean_proj)


def pos_peer(p, s, sign):
    v = 7 - (s // 2 + 7) % 8
    x, z = lax.rem(p // 8 + v // 4, 2), lax.rem(lax.rem(p // 2, 4) + sign * (v % 4) + 4, 4)
    return 8 * x + 2 * z + lax.rem(lax.rem(p, 2) + s % 2, 2)


def pack(parts):
    shape = parts[0].shape[:-1] + (256 - 3 * HD,)
    return jnp.concatenate(list(parts) + [jnp.zeros(shape, F32)], axis=-1).astype(BF)


def lanes(value, g):
    return value[..., g * HD : (g + 1) * HD]


def greet(barrier, p, f, pos, frame):
    if pos:

        @pl.loop(1, NP)
        def _(s):
            pl.semaphore_signal(barrier, inc=1, device_id={"pos": lax.rem(p + s, NP)})

    if frame:

        @pl.loop(1, NF)
        def _(s):
            pl.semaphore_signal(barrier, inc=1, device_id={"frame": lax.rem(f + s, NF)})


def send(src, dst, send_sem, recv_sem, axis, dest):
    return pltpu.make_async_remote_copy(
        src_ref=src, dst_ref=dst, send_sem=send_sem, recv_sem=recv_sem, device_id={axis: dest}
    )


def space_forward_kernel(
    x, cot, perm, w_hbm, so_hbm,
    qkv_out, stat_out, att_out, mixed_out, stream_out, cot_out,
    w, so, hat, qsend, qkv, kbuf, qbuf, vt, sbuf, pbuf, osend, orecv, stream, fsend, frecv, csend, crecv,
    wsem, sosem, qss, qrs, oss, ors, fss, frs, css, crs, outsem,
):
    p = lax.axis_index("pos")
    f = lax.axis_index("frame")
    par = lax.rem(p, 2)
    barrier = pltpu.get_barrier_semaphore()
    greet(barrier, p, f, True, True)

    def w_copy(i, c):
        pair = pos_peer(p, 2 * i, 1) // 2
        rows = pl.ds(pl.multiple_of(c * D + pair * 144, 16), 144)
        return pltpu.make_async_copy(w_hbm.at[rows], w.at[i, pl.ds(c * 144, 144)], wsem.at[i, c])

    for i in range(8):
        for c in range(3):
            w_copy(i, c).start()
    so_copy = pltpu.make_async_copy(so_hbm, so, sosem)
    so_copy.start()
    hat[...] = normalize(x[...])[0].astype(BF)
    pl.semaphore_wait(barrier, NP - 1 + NF - 1)

    def q_copy(fr, s):
        return send(qsend.at[s, fr], qkv.at[fr, p], qss.at[fr, s], qrs.at[fr, s], "pos", pos_peer(p, s, 1))

    @pl.loop(0, 8)
    def _(i):
        for c in range(3):
            w_copy(i, c).wait()
        r = dot(hat[...], w[i], 1, 1)
        pad = jnp.zeros((TOK, 256 - 3 * HD), F32)
        for e in range(2):
            part = [r[:, c * 144 + e * HD : c * 144 + e * HD + HD] for c in range(3)]
            val = jnp.concatenate(part + [pad], axis=1).astype(BF)
            qsend[2 * i + lax.rem(par + e, 2)] = val.reshape(FR, PL, 256)

        @pl.when(i > 0)
        def _():
            q_copy(0, 2 * i).start()

        q_copy(0, 2 * i + 1).start()

    @pl.loop(1, NP)
    def _(s):
        q_copy(1, s).start()

    qkv[:, pl.ds(p, 1)] = qsend[0][:, None]

    def c_copy(s):
        to = lax.rem(f + s, NF)
        return send(csend.at[to], crecv.at[f], css.at[s], crs.at[s], "frame", to)

    csend[...] = dot(perm[...], cot[...], 1, 0).astype(BF).reshape(NF, SLAB, D)

    @pl.loop(1, NF)
    def _(s):
        c_copy(s).start()

    crecv[pl.ds(f, 1)] = csend[pl.ds(f, 1)]

    def o_copy(fr, s):
        to = lax.rem(p + s, NP)
        return send(osend.at[fr, to], orecv.at[fr, p], oss.at[fr, s], ors.at[fr, s], "pos", to)

    outs = []
    for fr in range(FR):

        @pl.loop(1, NP)
        def _(s):
            q_copy(fr, s).wait_recv()

        out = pltpu.make_async_copy(qkv.at[fr], qkv_out.at[fr], outsem.at[fr])
        out.start()
        outs.append(out)
        rows = qkv[fr].reshape(ALL, 256)
        lane = lax.broadcasted_iota(jnp.int32, (1, 128), 1)
        keep = (lane < HD).astype(F32).astype(BF)
        zeros = jnp.zeros((ALL, 128 - HD), BF)
        qbuf[...] = rows[:, :128] * keep
        kbuf[...] = rows[:, HD : HD + 128]
        vt[...] = jnp.concatenate([rows[:, 2 * HD : 3 * HD], zeros], axis=1).T

        @pl.loop(0, ALL // QT)
        def _(t):
            tile = lax.rem(p // 4 + t, ALL // QT)
            at = pl.ds(pl.multiple_of(tile * QT, QT), QT)
            q = qbuf[at]
            top = jnp.full((8, QT), -jnp.inf, F32)
            for k in range(0, ALL, KC):
                s = dot(kbuf[k : k + KC], q, 1, 1)
                sbuf[k : k + KC] = s
                top = jnp.maximum(top, jnp.max(s.reshape(KC // 8, 8, QT), axis=0))
            top = jnp.max(top, axis=0, keepdims=True) * (SCALE * LOG2E)
            total = jnp.zeros((8, QT), F32)
            for k in range(0, ALL, KC):
                e = jnp.exp2(sbuf[k : k + KC] * (SCALE * LOG2E) - top)
                total = total + jnp.sum(e.reshape(KC // 8, 8, QT), axis=0)
                pbuf[k : k + KC] = e.astype(BF)
            total = jnp.sum(total, axis=0, keepdims=True)
            o = dot(vt[...], pbuf[...], 1, 0) * (1.0 / total)
            stat_out[fr, :, at] = jnp.broadcast_to(top + jnp.log(total) * LOG2E, (8, QT))
            att_out[fr, :, at] = o
            turned = o.T.reshape(4, 3, GRP, 128)
            osend[fr, pl.ds(tile * 4, 4)] = pack([turned[:, g, :, :HD] for g in range(3)])
            for j in range(4):
                to = tile * 4 + j

                @pl.when(to != p)
                def _():
                    o_copy(fr, lax.rem(to - p + NP, NP)).start()

        orecv[fr, pl.ds(p, 1)] = osend[fr, pl.ds(p, 1)]

    so_copy.wait()
    for fr in range(FR):

        @pl.loop(1, NP)
        def _(s):
            o_copy(fr, s).wait_recv()

        got = [orecv[fr, h].astype(F32) for h in range(HEADS)]
        mixed = jnp.concatenate(
            [jnp.concatenate([lanes(v, g) for v in got], axis=1) for g in range(3)], axis=0
        ).astype(BF)
        part = slice(fr * PL, (fr + 1) * PL)
        mixed_out[part] = mixed
        stream[part] = (x[part].astype(F32) + dot(mixed, so[...], 1, 1)).astype(BF)

    def f_copy(s):
        to = lax.rem(f + s, NF)
        return send(fsend.at[to], frecv.at[f], fss.at[s], frs.at[s], "frame", to)

    fsend[...] = dot(perm[...], stream[...], 1, 0).astype(BF).reshape(NF, SLAB, D)

    @pl.loop(1, NF)
    def _(s):
        f_copy(s).start()

    frecv[pl.ds(f, 1)] = fsend[pl.ds(f, 1)]

    @pl.loop(1, NF)
    def _(s):
        c_copy(s).wait_recv()

    cot_out[...] = crecv[...]

    @pl.loop(1, NP)
    def _(s):
        for fr in range(FR):
            q_copy(fr, s).wait_send()
            o_copy(fr, s).wait_send()

    for out in outs:
        out.wait()

    @pl.loop(1, NF)
    def _(s):
        f_copy(s).wait_recv()

    stream_out[...] = frecv[...]

    @pl.loop(1, NF)
    def _(s):
        c_copy(s).wait_send()
        f_copy(s).wait_send()


def vmem():
    return pl.BlockSpec(memory_space=pltpu.VMEM)


def anywhere():
    return pl.BlockSpec(memory_space=pl.ANY)


DMA = pltpu.SemaphoreType.DMA


def params(collective_id):
    return pltpu.CompilerParams(
        collective_id=collective_id, has_side_effects=True, vmem_limit_bytes=LIMIT
    )


def space_forward(x, cot, perm, w, so):
    V = pltpu.VMEM
    sds = jax.ShapeDtypeStruct
    return pl.pallas_call(
        space_forward_kernel,
        out_shape=(
            sds((FR, NP, PL, 256), BF),
            sds((FR, 8, ALL), F32),
            sds((FR, 128, ALL), F32),
            sds((TOK, D), BF),
            sds((NF, SLAB, D), BF),
            sds((NF, SLAB, D), BF),
        ),
        in_specs=[vmem(), vmem(), vmem(), anywhere(), anywhere()],
        out_specs=(anywhere(), vmem(), vmem(), vmem(), vmem(), vmem()),
        scratch_shapes=[
            V((8, 432, D), BF), V((D, D), BF), V((TOK, D), BF), V((NP, FR, PL, 256), BF),
            V((FR, NP, PL, 256), BF), V((ALL, 128), BF), V((ALL, 128), BF), V((128, ALL), BF),
            V((ALL, QT), F32), V((ALL, QT), BF),
            V((FR, NP, GRP, 256), BF), V((FR, NP, GRP, 256), BF), V((TOK, D), BF),
            V((NF, SLAB, D), BF), V((NF, SLAB, D), BF), V((NF, SLAB, D), BF), V((NF, SLAB, D), BF),
            DMA((8, 3)), DMA, DMA((FR, NP)), DMA((FR, NP)), DMA((FR, NP)), DMA((FR, NP)),
            DMA((NF,)), DMA((NF,)), DMA((NF,)), DMA((NF,)), DMA((FR,)),
        ],
        compiler_params=params(1),
    )(x, cot, perm, w, so)


def rest_kernel(
    stream, cot, mask, unperm, spread, x, mixed, stat, att,
    order_hbm, tw_hbm, to_hbm, qkv_hbm, w_hbm, so_hbm,
    grad_out, sums_out,
    w, wo, so, order, hat, tqkv, back, tmixed, probs, dqkv, usend, urecv, up,
    tasend, tarecv, tmsend, tmrecv, asend, arecv, mrecv,
    qkv, bsend, brecv, gpart, grecv, hsend, hrecv,
    qbuf, kbuf, vbuf, bbuf, kt, pbuf, sbuf, dq, dk, dv, rsend, rrecv,
    wsem, tosem, sosem, ordsem, qsem, uss, urs, mss, mrs, bss, brs, gss, grs, hss, hrs, rss, rrs,
):
    p = lax.axis_index("pos")
    f = lax.axis_index("frame")
    par = lax.rem(p, 2)
    chip = p // 2
    y, half = lax.rem(f, 4), f // 4
    place = NK * half + chip
    mate = p + 1 - 2 * par
    barrier = pltpu.get_barrier_semaphore()
    greet(barrier, p, f, True, True)

    @pl.loop(1, NK)
    def _(s):
        other = {"frame": 4 * (1 - half) + y, "pos": 2 * lax.rem(chip + s, NK) + par}
        pl.semaphore_signal(barrier, inc=1, device_id=other)

    to_copy = pltpu.make_async_copy(to_hbm, wo, tosem)
    to_copy.start()
    tw_copies = [
        pltpu.make_async_copy(tw_hbm.at[pl.ds(c * D, D)], w.at[c], wsem.at[c]) for c in range(3)
    ]
    for c in tw_copies:
        c.start()
    order_copy = pltpu.make_async_copy(order_hbm, order, ordsem)
    order_copy.start()
    so_copy = pltpu.make_async_copy(so_hbm, so, sosem)
    so_copy.start()
    qkv_copy = pltpu.make_async_copy(qkv_hbm, qkv, qsem)
    qkv_copy.start()

    normed, inv = normalize(stream[...])
    hat[...] = normed
    normed = normed.astype(BF)
    to_copy.wait()
    back[...] = dot(cot[...], wo[...], 1, 0).astype(BF)
    for c in range(3):
        tw_copies[c].wait()
        tqkv[c] = dot(normed, w[c], 1, 1).astype(BF)
    order_copy.wait()
    for e in range(2):
        tasend[e] = dot(cot[...], order[e], 1, 0).astype(BF)
    tmixed[...] = jnp.zeros_like(tmixed)
    dqkv[...] = jnp.zeros_like(dqkv)

    def window(h):
        off = (h * HD) % 128
        start = h * HD - off
        width = 128 if off + HD <= 128 else 256
        lane = lax.broadcasted_iota(jnp.int32, (1, width), 1)
        keep = ((lane >= off) & (lane < off + HD)).astype(F32).astype(BF)
        return slice(start, start + width), keep

    for h in range(HEADS):
        win, keep = window(h)
        s = dot(tqkv[0, :, win] * keep, tqkv[1, :, win], 1, 1) * SCALE + mask[...]
        e = jnp.exp(s - jnp.max(s, axis=1, keepdims=True))
        prob = e * (1.0 / jnp.sum(e, axis=1, keepdims=True))
        probs[h] = prob
        tmixed[:, win] += dot(prob.astype(BF), tqkv[2, :, win] * keep, 1, 0)
    tmsend[...] = tmixed[...].astype(BF)
    pl.semaphore_wait(barrier, NP - 1 + NF - 1 + NK - 1)
    ta_copy = send(tasend.at[1 - par], tarecv, mss.at[0], mrs.at[0], "pos", mate)
    tm_copy = send(tmsend, tmrecv, mss.at[1], mrs.at[1], "pos", mate)
    m_copy = send(mixed, mrecv, mss.at[2], mrs.at[2], "pos", mate)
    ta_copy.start()
    tm_copy.start()
    m_copy.start()
    for h in range(HEADS):
        win, keep = window(h)
        k, q = tqkv[1, :, win] * keep, tqkv[0, :, win] * keep
        b = back[:, win] * keep
        prob = probs[h]
        gp = dot(b, tqkv[2, :, win], 1, 1)
        gs = prob * (gp - jnp.sum(prob * gp, axis=1, keepdims=True)) * SCALE
        gs = gs.astype(BF)
        dqkv[0, :, win] += dot(gs, k, 1, 0)
        dqkv[1, :, win] += dot(gs, q, 0, 0)
        dqkv[2, :, win] += dot(prob.astype(BF), b, 0, 0)
    grad_hat = dot(dqkv[0].astype(BF), w[0], 1, 0)
    for c in range(1, 3):
        grad_hat += dot(dqkv[c].astype(BF), w[c], 1, 0)
    turned = cot[...].astype(F32) + norm_back(grad_hat, hat[...], inv)
    usend[...] = turned.astype(BF).reshape(NF, SLAB, D)

    def u_copy(s):
        to = lax.rem(f + s, NF)
        return send(usend.at[to], urecv.at[f], uss.at[s], urs.at[s], "frame", to)

    @pl.loop(1, NF)
    def _(s):
        u_copy(s).start()

    urecv[pl.ds(f, 1)] = usend[pl.ds(f, 1)]

    w_copies = [
        pltpu.make_async_copy(w_hbm.at[pl.ds(c * D, D)], w.at[c], wsem.at[c]) for c in range(3)
    ]
    for c in w_copies:
        c.start()

    def g_copy(g, s):
        to = lax.rem(y + s, 4)
        rows = pl.ds(pl.multiple_of(to * 2 * GS, 16), 2 * GS)
        return send(
            gpart.at[g, rows], grecv.at[g, y], gss.at[g, s], grs.at[g, s], "frame", 4 * half + to
        )

    def gradient(g, mine, left, theirs, right):
        for r in range(0, GH, 128):
            part = dot(mine[:, r : r + 128], left[...], 0, 0)
            part += dot(theirs[:, r : r + 128], right[...], 0, 0)
            gpart[g, r : r + 128] = part.astype(BF)

        @pl.loop(1, 4)
        def _(s):
            g_copy(g, s).start()

        grecv[g, pl.ds(y, 1)] = gpart[g, pl.ds(pl.multiple_of(y * 2 * GS, 16), 2 * GS)][None]

    ta_copy.wait()
    tm_copy.wait()
    gradient(0, tasend.at[par], tmsend, tarecv, tmrecv)

    qkv_copy.wait()
    so_copy.wait()
    lane = lax.broadcasted_iota(jnp.int32, (1, 128), 1)
    keep = (lane < HD).astype(F32).astype(BF)
    zeros = jnp.zeros((ALL, 128 - HD), BF)
    for fr in range(FR):
        rows = qkv[fr].reshape(ALL, 256)
        qbuf[fr] = rows[:, :128] * keep
        k = rows[:, HD : HD + 128] * keep
        kbuf[fr] = k
        kt[fr] = k.T
        vbuf[fr] = jnp.concatenate([rows[:, 2 * HD : 3 * HD], zeros], axis=1)

    @pl.loop(1, NF)
    def _(s):
        u_copy(s).wait_recv()

    up[...] = dot(unperm[...], urecv[...].reshape(TT, D), 1, 0).astype(BF)

    sback = dot(up[...], so[...], 1, 0).reshape(FR, 3, GRP, D)
    for h in range(HEADS):
        bsend[:, h] = pack([lanes(sback[:, g], h) for g in range(3)])

    def b_copy(fr, s):
        to, dst = pos_peer(p, s, 1), p
        return send(bsend.at[fr, to], brecv.at[fr, dst], bss.at[fr, s], brs.at[fr, s], "pos", to)

    for fr in range(FR):

        @pl.loop(1, NP)
        def _(s):
            b_copy(fr, s).start()

    brecv[:, pl.ds(p, 1)] = bsend[:, pl.ds(p, 1)]
    for e in range(2):
        asend[e] = dot(up[...], order[e], 1, 0).astype(BF)
    a_copy = send(asend.at[1 - par], arecv, mss.at[3], mrs.at[3], "pos", mate)
    a_copy.start()
    a_copy.wait()
    m_copy.wait()
    gradient(1, asend.at[par], mixed, arecv, mrecv)

    def r_copy(fr, s):
        to = pos_peer(p, s, 1)
        return send(rsend.at[fr, to], rrecv.at[fr, p], rss.at[fr, s], rrs.at[fr, s], "pos", to)

    def h_copy(g, s):
        to = lax.rem(place + s, NP)
        return pltpu.make_async_remote_copy(
            src_ref=hsend.at[g, to],
            dst_ref=hrecv.at[g, place],
            send_sem=hss.at[g, s],
            recv_sem=hrs.at[g, s],
            device_id={"frame": 4 * (to // NK) + y, "pos": 2 * lax.rem(to, NK) + par},
        )

    def fold(g):
        @pl.loop(1, 4)
        def _(s):
            g_copy(g, s).wait_recv()

        total = grecv[g, 0].astype(F32)
        for s in range(1, 4):
            total += grecv[g, s].astype(F32)
        hsend[g] = dot(spread[...], total.astype(BF), 1, 0).astype(BF).reshape(NP, 16, D)

        @pl.loop(1, NP)
        def _(s):
            h_copy(g, s).start()

        hrecv[g, pl.ds(place, 1)] = hsend[g, pl.ds(place, 1)]

    for fr in range(FR):
        dk[...] = jnp.zeros_like(dk)
        dv[...] = jnp.zeros_like(dv)

        @pl.loop(1, NP)
        def _(s):
            b_copy(fr, s).wait_recv()

        got = brecv[fr]
        zeros = jnp.zeros((NP, GRP, 128 - HD), BF)
        for g in range(3):
            bbuf[:, g * GRP : (g + 1) * GRP] = jnp.concatenate([lanes(got, g), zeros], axis=-1)

        @pl.loop(0, ALL // BT)
        def _(t):
            at = pl.ds(pl.multiple_of(t * BT, BT), BT)
            q = qbuf[fr, at]
            b = bbuf.reshape(ALL, 128)[at]
            total = jnp.sum(b.astype(F32).T * att[fr, :, at], axis=0, keepdims=True)
            lse = stat[fr, 0:1, at]
            for k in range(0, ALL, KC):
                s = dot(kbuf[fr, k : k + KC], q, 1, 1)
                gp = dot(vbuf[fr, k : k + KC], b, 1, 1)
                prob = jnp.exp2(s * (SCALE * LOG2E) - lse)
                pbuf[k : k + KC] = prob.astype(BF)
                sbuf[k : k + KC] = (prob * (gp - total)).astype(BF)
            dv[...] += dot(pbuf[...], b, 1, 0)
            dk[...] += dot(sbuf[...], q, 1, 0)
            dq[at] = dot(kt[fr], sbuf[...], 1, 0).T

        val = pack([dq[:, :HD] * SCALE, dk[:, :HD] * SCALE, dv[:, :HD]])
        rsend[fr] = val.reshape(NP, PL, 256)

        @pl.loop(1, NP)
        def _(s):
            r_copy(fr, s).start()

        rrecv[fr, pl.ds(p, 1)] = rsend[fr, pl.ds(p, 1)]
        if fr == 0:
            fold(0)

    def finish_rows(fr):
        @pl.loop(1, NP)
        def _(s):
            r_copy(fr, s).wait_recv()

        got = [rrecv[fr, h].astype(F32) for h in range(HEADS)]
        grad_hat = jnp.zeros((PL, D), F32)
        for c in range(3):
            part = jnp.concatenate([lanes(v, c) for v in got], axis=1)
            grad_hat += dot(part.astype(BF), w[c], 1, 0)
        here = slice(fr * PL, (fr + 1) * PL)
        normed, inv = normalize(x[here])
        grad_out[here] = (up[here].astype(F32) + norm_back(grad_hat, normed, inv)).astype(BF)

    for c in w_copies:
        c.wait()
    finish_rows(0)
    fold(1)
    finish_rows(1)
    for g in range(2):

        @pl.loop(1, NP)
        def _(s):
            h_copy(g, s).wait_recv()

        total = hrecv[g, 0].astype(F32)
        for s in range(1, NP):
            total += hrecv[g, s].astype(F32)
        sums_out[g] = total

    @pl.loop(1, NP)
    def _(s):
        for fr in range(FR):
            b_copy(fr, s).wait_send()
            r_copy(fr, s).wait_send()
        for g in range(2):
            h_copy(g, s).wait_send()

    @pl.loop(1, NF)
    def _(s):
        u_copy(s).wait_send()

    @pl.loop(1, 4)
    def _(s):
        for g in range(2):
            g_copy(g, s).wait_send()


def rest(stream, cot, mask, unperm, spread, x, mixed, stat, att, order, tw, wo, qkv, w, so):
    V = pltpu.VMEM
    sds = jax.ShapeDtypeStruct
    return pl.pallas_call(
        rest_kernel,
        out_shape=(sds((TOK, D), BF), sds((2, 16, D), F32)),
        in_specs=[vmem()] * 9 + [anywhere()] * 6,
        out_specs=(vmem(), vmem()),
        scratch_shapes=[
            V((3, D, D), BF), V((D, D), BF), V((D, D), BF), V((2, D, GH), BF), V((TT, D), F32),
            V((3, TT, D), BF), V((TT, D), BF), V((TT, D), F32), V((HEADS, TT, TT), F32),
            V((3, TT, D), F32), V((NF, SLAB, D), BF), V((NF, SLAB, D), BF), V((TOK, D), BF),
            V((2, TT, GH), BF), V((TT, GH), BF), V((TT, D), BF), V((TT, D), BF),
            V((2, TOK, GH), BF), V((TOK, GH), BF), V((TOK, D), BF),
            V((FR, NP, PL, 256), BF), V((FR, NP, GRP, 256), BF), V((FR, NP, GRP, 256), BF),
            V((2, GH, D), BF), V((2, 4, 2 * GS, D), BF),
            V((2, NP, 16, D), BF), V((2, NP, 16, D), BF),
            V((FR, ALL, 128), BF), V((FR, ALL, 128), BF), V((FR, ALL, 128), BF),
            V((NP, PL, 128), BF), V((FR, 128, ALL), BF),
            V((ALL, BT), BF), V((ALL, BT), BF),
            V((ALL, 128), F32), V((ALL, 128), F32), V((ALL, 128), F32),
            V((FR, NP, PL, 256), BF), V((FR, NP, PL, 256), BF),
            DMA((3,)), DMA, DMA, DMA, DMA, DMA((NF,)), DMA((NF,)), DMA((4,)), DMA((4,)),
            DMA((FR, NP)), DMA((FR, NP)), DMA((2, 4)), DMA((2, 4)),
            DMA((2, NP)), DMA((2, NP)), DMA((FR, NP)), DMA((FR, NP)),
        ],
        compiler_params=params(2),
    )(stream, cot, mask, unperm, spread, x, mixed, stat, att, order, tw, wo, qkv, w, so)


def finish_kernel(grad, sums, grad_out, gs_out, gt_out):
    grad_out[...] = grad[...]
    gt_out[...] = sums[0, :GR]
    gs_out[...] = sums[1, :GR]


def finish(grad, sums):
    sds = jax.ShapeDtypeStruct
    return pl.pallas_call(
        finish_kernel,
        out_shape=(sds((TOK, D), BF), sds((GR, D), F32), sds((GR, D), F32)),
        in_specs=[vmem(), vmem()],
        out_specs=(vmem(), vmem(), vmem()),
    )(grad, sums)


def tables():
    row = np.arange(TT)
    slab, inner = row // SLAB, row % SLAB
    real = inner < FR * TP
    col = (inner // TP) * PL + slab * TP + inner % TP
    perm = (real[:, None] & (col[:, None] == np.arange(TOK)[None])).astype(np.float32)
    place = np.where(real, inner % TP, -1)
    mask = np.where(place[:, None] == place[None], 0.0, -1e30).astype(np.float32)
    row = np.arange(NP * 16)
    source = row // 16 // NK * GS + row // 16 % NK * GR + row % 16
    spread = (row % 16 < GR)[:, None] & (source[:, None] == np.arange(2 * GS)[None])
    col = np.arange(2 * GH)
    core, slab, inner = col // GH, col % GH // GS, col % GS
    frame = slab % 2 * 4 + slab // 2
    source = (frame * NP + 2 * (inner // GR) + core) * GR + inner % GR
    order = (inner < NK * GR)[None] & (np.arange(D)[:, None] == source[None])
    order = order.reshape(D, 2, GH).transpose(1, 0, 2)
    return [jnp.asarray(t.astype(np.float32), BF) for t in (perm, perm.T, spread, order)] + [
        jnp.asarray(mask)
    ]


def shards(inputs, cotangent, space_projection, space_output, time_projection, time_output):
    perm, unperm, spread, order, mask = tables()
    x = inputs.reshape(TOK, D)
    cot = cotangent.reshape(TOK, D)
    qkv, stat, att, mixed, stream_t, cot_t = space_forward(x, cot, perm, space_projection, space_output)
    grad, sums = rest(
        stream_t.reshape(TT, D), cot_t.reshape(TT, D), mask, unperm, spread, x, mixed, stat, att,
        order, time_projection, time_output, qkv, space_projection, space_output,
    )
    grad, gs, gt = finish(grad, sums)
    return grad.reshape(FR, PL, D), gs, gt


def solution(mesh):
    return jax.shard_map(
        shards,
        mesh=mesh,
        in_specs=(P("frame", "pos", None), P("frame", "pos", None), P(), P(), P(), P()),
        out_specs=(P("frame", "pos", None), P(("frame", "pos"), None), P(("frame", "pos"), None)),
        check_vma=False,
    )
```

```python
import jax
import jax.numpy as jnp
import numpy as np
from jax import lax
from jax.experimental import pallas as pl
from jax.experimental.pallas import tpu as pltpu
from jax.sharding import PartitionSpec as P

HEADS = 16
EPS = 1e-06
BF = jnp.bfloat16
F32 = jnp.float32
D = 1152
HD = 72
NP = 16
NF = 8
FR = 2
PL = 96
TOK = FR * PL
ALL = NP * PL
TP = PL // NF
SLAB = 32
TT = NF * SLAB
GR = D // NF // NP
NK = NP // 2
GS = 80
GH = NF * GS
GRP = PL // 3
SCALE = HD ** (-0.5)
LOG2E = 1.4426950408889634
QT = 384
BT = 256
KC = 256
LIMIT = 60 * 1024 * 1024


def dot(a, b, ca, cb):
    return lax.dot_general(a, b, (((ca,), (cb,)), ((), ())), preferred_element_type=F32)


def normalize(tokens):
    values = tokens.astype(F32)
    center = values - jnp.mean(values, axis=-1, keepdims=True)
    inv_std = lax.rsqrt(jnp.mean(center * center, axis=-1, keepdims=True) + EPS)
    return center * inv_std, inv_std


def norm_back(grad_hat, normed, inv_std):
    mean_grad = jnp.mean(grad_hat, axis=-1, keepdims=True)
    mean_proj = jnp.mean(grad_hat * normed, axis=-1, keepdims=True)
    return inv_std * (grad_hat - mean_grad - normed * mean_proj)


def pos_peer(p, s, sign):
    v = 7 - (s // 2 + 7) % 8
    x, z = lax.rem(p // 8 + v // 4, 2), lax.rem(lax.rem(p // 2, 4) + sign * (v % 4) + 4, 4)
    return 8 * x + 2 * z + lax.rem(lax.rem(p, 2) + s % 2, 2)


def pack(parts):
    shape = parts[0].shape[:-1] + (256 - 3 * HD,)
    return jnp.concatenate(list(parts) + [jnp.zeros(shape, F32)], axis=-1).astype(BF)


def lanes(value, g):
    return value[..., g * HD : (g + 1) * HD]


def greet(barrier, p, f, pos, frame):
    if pos:

        @pl.loop(1, NP)
        def _(s):
            pl.semaphore_signal(barrier, inc=1, device_id={"pos": lax.rem(p + s, NP)})

    if frame:

        @pl.loop(1, NF)
        def _(s):
            pl.semaphore_signal(barrier, inc=1, device_id={"frame": lax.rem(f + s, NF)})


def send(src, dst, send_sem, recv_sem, axis, dest):
    return pltpu.make_async_remote_copy(
        src_ref=src, dst_ref=dst, send_sem=send_sem, recv_sem=recv_sem, device_id={axis: dest}
    )


def space_forward_kernel(
    x, cot, perm, w_hbm, so_hbm, wo_hbm, order_hbm,
    qkv_out, stat_out, att_out, mixed_out, stream_out, cot_out, back_out, split_out,
    w, so, wo, order, hat, qsend, qkv, kbuf, qbuf, vt, sbuf, pbuf, osend, orecv, stream, fsend, frecv, csend, crecv,
    wsem, sosem, wosem, ordsem, qss, qrs, oss, ors, fss, frs, css, crs, outsem,
):
    p = lax.axis_index("pos")
    f = lax.axis_index("frame")
    par = lax.rem(p, 2)
    barrier = pltpu.get_barrier_semaphore()
    greet(barrier, p, f, True, True)

    def w_copy(i, c):
        pair = pos_peer(p, 2 * i, 1) // 2
        rows = pl.ds(pl.multiple_of(c * D + pair * 144, 16), 144)
        return pltpu.make_async_copy(w_hbm.at[rows], w.at[i, pl.ds(c * 144, 144)], wsem.at[i, c])

    for i in range(8):
        for c in range(3):
            w_copy(i, c).start()
    so_copy = pltpu.make_async_copy(so_hbm, so, sosem)
    wo_copy = pltpu.make_async_copy(wo_hbm, wo, wosem)
    order_copy = pltpu.make_async_copy(order_hbm, order, ordsem)
    hat[...] = normalize(x[...])[0].astype(BF)
    pl.semaphore_wait(barrier, NP - 1 + NF - 1)

    def q_copy(fr, s):
        return send(qsend.at[s, fr], qkv.at[fr, p], qss.at[fr, s], qrs.at[fr, s], "pos", pos_peer(p, s, 1))

    @pl.loop(0, 8)
    def _(i):
        for c in range(3):
            w_copy(i, c).wait()
        r = dot(hat[...], w[i], 1, 1)
        pad = jnp.zeros((TOK, 256 - 3 * HD), F32)
        for e in range(2):
            part = [r[:, c * 144 + e * HD : c * 144 + e * HD + HD] for c in range(3)]
            val = jnp.concatenate(part + [pad], axis=1).astype(BF)
            qsend[2 * i + lax.rem(par + e, 2)] = val.reshape(FR, PL, 256)

        @pl.when(i > 0)
        def _():
            q_copy(0, 2 * i).start()

        q_copy(0, 2 * i + 1).start()

    @pl.loop(1, NP)
    def _(s):
        q_copy(1, s).start()

    qkv[:, pl.ds(p, 1)] = qsend[0][:, None]
    for late in (so_copy, wo_copy, order_copy):
        late.start()

    def c_copy(s):
        to = lax.rem(f + s, NF)
        return send(csend.at[to], crecv.at[f], css.at[s], crs.at[s], "frame", to)

    csend[...] = dot(perm[...], cot[...], 1, 0).astype(BF).reshape(NF, SLAB, D)

    @pl.loop(1, NF)
    def _(s):
        c_copy(s).start()

    crecv[pl.ds(f, 1)] = csend[pl.ds(f, 1)]

    def o_copy(fr, s):
        to = lax.rem(p + s, NP)
        return send(osend.at[fr, to], orecv.at[fr, p], oss.at[fr, s], ors.at[fr, s], "pos", to)

    outs = []
    for fr in range(FR):

        @pl.loop(1, NP)
        def _(s):
            q_copy(fr, s).wait_recv()

        out = pltpu.make_async_copy(qkv.at[fr], qkv_out.at[fr], outsem.at[fr])
        out.start()
        outs.append(out)
        rows = qkv[fr].reshape(ALL, 256)
        lane = lax.broadcasted_iota(jnp.int32, (1, 128), 1)
        keep = (lane < HD).astype(F32).astype(BF)
        zeros = jnp.zeros((ALL, 128 - HD), BF)
        qbuf[...] = rows[:, :128] * keep
        kbuf[...] = rows[:, HD : HD + 128]
        vt[...] = jnp.concatenate([rows[:, 2 * HD : 3 * HD], zeros], axis=1).T

        @pl.loop(0, ALL // QT)
        def _(t):
            tile = lax.rem(p // 4 + t, ALL // QT)
            at = pl.ds(pl.multiple_of(tile * QT, QT), QT)
            q = qbuf[at]
            top = jnp.full((8, QT), -jnp.inf, F32)
            for k in range(0, ALL, KC):
                s = dot(kbuf[k : k + KC], q, 1, 1)
                sbuf[k : k + KC] = s
                top = jnp.maximum(top, jnp.max(s.reshape(KC // 8, 8, QT), axis=0))
            top = jnp.max(top, axis=0, keepdims=True) * (SCALE * LOG2E)
            total = jnp.zeros((8, QT), F32)
            for k in range(0, ALL, KC):
                e = jnp.exp2(sbuf[k : k + KC] * (SCALE * LOG2E) - top)
                total = total + jnp.sum(e.reshape(KC // 8, 8, QT), axis=0)
                pbuf[k : k + KC] = e.astype(BF)
            total = jnp.sum(total, axis=0, keepdims=True)
            o = dot(vt[...], pbuf[...], 1, 0) * (1.0 / total)
            stat_out[fr, :, at] = jnp.broadcast_to(top + jnp.log(total) * LOG2E, (8, QT))
            att_out[fr, :, at] = o
            turned = o.T.reshape(4, 3, GRP, 128)
            osend[fr, pl.ds(tile * 4, 4)] = pack([turned[:, g, :, :HD] for g in range(3)])
            for j in range(4):
                to = tile * 4 + j

                @pl.when(to != p)
                def _():
                    o_copy(fr, lax.rem(to - p + NP, NP)).start()

        orecv[fr, pl.ds(p, 1)] = osend[fr, pl.ds(p, 1)]

    so_copy.wait()
    for fr in range(FR):

        @pl.loop(1, NP)
        def _(s):
            o_copy(fr, s).wait_recv()

        got = [orecv[fr, h].astype(F32) for h in range(HEADS)]
        mixed = jnp.concatenate(
            [jnp.concatenate([lanes(v, g) for v in got], axis=1) for g in range(3)], axis=0
        ).astype(BF)
        part = slice(fr * PL, (fr + 1) * PL)
        mixed_out[part] = mixed
        stream[part] = (x[part].astype(F32) + dot(mixed, so[...], 1, 1)).astype(BF)

    def f_copy(s):
        to = lax.rem(f + s, NF)
        return send(fsend.at[to], frecv.at[f], fss.at[s], frs.at[s], "frame", to)

    fsend[...] = dot(perm[...], stream[...], 1, 0).astype(BF).reshape(NF, SLAB, D)

    @pl.loop(1, NF)
    def _(s):
        f_copy(s).start()

    frecv[pl.ds(f, 1)] = fsend[pl.ds(f, 1)]

    @pl.loop(1, NF)
    def _(s):
        c_copy(s).wait_recv()

    cot_out[...] = crecv[...]
    tcot = crecv[...].reshape(TT, D)
    wo_copy.wait()
    back_out[...] = dot(tcot, wo[...], 1, 0).astype(BF)
    order_copy.wait()
    for e in range(2):
        split_out[e] = dot(tcot, order[e], 1, 0).astype(BF)

    @pl.loop(1, NP)
    def _(s):
        for fr in range(FR):
            q_copy(fr, s).wait_send()
            o_copy(fr, s).wait_send()

    for out in outs:
        out.wait()

    @pl.loop(1, NF)
    def _(s):
        f_copy(s).wait_recv()

    stream_out[...] = frecv[...]

    @pl.loop(1, NF)
    def _(s):
        c_copy(s).wait_send()
        f_copy(s).wait_send()


def vmem():
    return pl.BlockSpec(memory_space=pltpu.VMEM)


def anywhere():
    return pl.BlockSpec(memory_space=pl.ANY)


DMA = pltpu.SemaphoreType.DMA


def params(collective_id):
    return pltpu.CompilerParams(
        collective_id=collective_id, has_side_effects=True, vmem_limit_bytes=LIMIT
    )


def space_forward(x, cot, perm, w, so, wo, order):
    V = pltpu.VMEM
    sds = jax.ShapeDtypeStruct
    return pl.pallas_call(
        space_forward_kernel,
        out_shape=(
            sds((FR, NP, PL, 256), BF),
            sds((FR, 8, ALL), F32),
            sds((FR, 128, ALL), F32),
            sds((TOK, D), BF),
            sds((NF, SLAB, D), BF),
            sds((NF, SLAB, D), BF),
            sds((TT, D), BF),
            sds((2, TT, GH), BF),
        ),
        in_specs=[vmem(), vmem(), vmem()] + [anywhere()] * 4,
        out_specs=(anywhere(),) + (vmem(),) * 7,
        scratch_shapes=[
            V((8, 432, D), BF), V((D, D), BF), V((D, D), BF), V((2, D, GH), BF), V((TOK, D), BF), V((NP, FR, PL, 256), BF),
            V((FR, NP, PL, 256), BF), V((ALL, 128), BF), V((ALL, 128), BF), V((128, ALL), BF),
            V((ALL, QT), F32), V((ALL, QT), BF),
            V((FR, NP, GRP, 256), BF), V((FR, NP, GRP, 256), BF), V((TOK, D), BF),
            V((NF, SLAB, D), BF), V((NF, SLAB, D), BF), V((NF, SLAB, D), BF), V((NF, SLAB, D), BF),
            DMA((8, 3)), DMA, DMA, DMA, DMA((FR, NP)), DMA((FR, NP)), DMA((FR, NP)), DMA((FR, NP)),
            DMA((NF,)), DMA((NF,)), DMA((NF,)), DMA((NF,)), DMA((FR,)),
        ],
        compiler_params=params(1),
    )(x, cot, perm, w, so, wo, order)


def rest_kernel(
    stream, cot, back, tasend, mask, unperm, spread, x, mixed, stat, att,
    order_hbm, tw_hbm, qkv_hbm, w_hbm, so_hbm,
    grad_out, sums_out,
    w, so, order, hat, tqkv, tmixed, probs, dqkv, usend, urecv, up,
    tarecv, tmsend, tmrecv, asend, arecv, mrecv,
    qkv, bsend, brecv, gpart, grecv, hsend, hrecv,
    qbuf, kbuf, vbuf, bbuf, kt, pbuf, sbuf, dq, dk, dv, rsend, rrecv,
    wsem, sosem, ordsem, qsem, uss, urs, mss, mrs, bss, brs, gss, grs, hss, hrs, rss, rrs,
):
    p = lax.axis_index("pos")
    f = lax.axis_index("frame")
    par = lax.rem(p, 2)
    chip = p // 2
    y, half = lax.rem(f, 4), f // 4
    place = NK * half + chip
    mate = p + 1 - 2 * par
    barrier = pltpu.get_barrier_semaphore()
    greet(barrier, p, f, True, True)

    @pl.loop(1, NK)
    def _(s):
        other = {"frame": 4 * (1 - half) + y, "pos": 2 * lax.rem(chip + s, NK) + par}
        pl.semaphore_signal(barrier, inc=1, device_id=other)

    tw_copies = [
        pltpu.make_async_copy(tw_hbm.at[pl.ds(c * D, D)], w.at[c], wsem.at[c]) for c in range(3)
    ]
    for c in tw_copies:
        c.start()
    order_copy = pltpu.make_async_copy(order_hbm, order, ordsem)
    so_copy = pltpu.make_async_copy(so_hbm, so, sosem)
    qkv_copy = pltpu.make_async_copy(qkv_hbm, qkv, qsem)

    normed, inv = normalize(stream[...])
    hat[...] = normed
    normed = normed.astype(BF)
    for c in range(3):
        tw_copies[c].wait()
        tqkv[c] = dot(normed, w[c], 1, 1).astype(BF)
    for late in (qkv_copy, so_copy, order_copy):
        late.start()
    tmixed[...] = jnp.zeros_like(tmixed)
    dqkv[...] = jnp.zeros_like(dqkv)

    def window(h):
        off = (h * HD) % 128
        start = h * HD - off
        width = 128 if off + HD <= 128 else 256
        lane = lax.broadcasted_iota(jnp.int32, (1, width), 1)
        keep = ((lane >= off) & (lane < off + HD)).astype(F32).astype(BF)
        return slice(start, start + width), keep

    for h in range(HEADS):
        win, keep = window(h)
        s = dot(tqkv[0, :, win] * keep, tqkv[1, :, win], 1, 1) * SCALE + mask[...]
        e = jnp.exp(s - jnp.max(s, axis=1, keepdims=True))
        prob = e * (1.0 / jnp.sum(e, axis=1, keepdims=True))
        probs[h] = prob
        tmixed[:, win] += dot(prob.astype(BF), tqkv[2, :, win] * keep, 1, 0)
    tmsend[...] = tmixed[...].astype(BF)
    pl.semaphore_wait(barrier, NP - 1 + NF - 1 + NK - 1)
    ta_copy = send(tasend.at[1 - par], tarecv, mss.at[0], mrs.at[0], "pos", mate)
    tm_copy = send(tmsend, tmrecv, mss.at[1], mrs.at[1], "pos", mate)
    m_copy = send(mixed, mrecv, mss.at[2], mrs.at[2], "pos", mate)
    ta_copy.start()
    tm_copy.start()
    m_copy.start()
    for h in range(HEADS):
        win, keep = window(h)
        k, q = tqkv[1, :, win] * keep, tqkv[0, :, win] * keep
        b = back[:, win] * keep
        prob = probs[h]
        gp = dot(b, tqkv[2, :, win], 1, 1)
        gs = prob * (gp - jnp.sum(prob * gp, axis=1, keepdims=True)) * SCALE
        gs = gs.astype(BF)
        dqkv[0, :, win] += dot(gs, k, 1, 0)
        dqkv[1, :, win] += dot(gs, q, 0, 0)
        dqkv[2, :, win] += dot(prob.astype(BF), b, 0, 0)
    grad_hat = dot(dqkv[0].astype(BF), w[0], 1, 0)
    for c in range(1, 3):
        grad_hat += dot(dqkv[c].astype(BF), w[c], 1, 0)
    turned = cot[...].astype(F32) + norm_back(grad_hat, hat[...], inv)
    usend[...] = turned.astype(BF).reshape(NF, SLAB, D)

    def u_copy(s):
        to = lax.rem(f + s, NF)
        return send(usend.at[to], urecv.at[f], uss.at[s], urs.at[s], "frame", to)

    @pl.loop(1, NF)
    def _(s):
        u_copy(s).start()

    urecv[pl.ds(f, 1)] = usend[pl.ds(f, 1)]

    w_copies = [
        pltpu.make_async_copy(w_hbm.at[pl.ds(c * D, D)], w.at[c], wsem.at[c]) for c in range(3)
    ]
    for c in w_copies:
        c.start()

    def g_copy(g, s):
        to = lax.rem(y + s, 4)
        rows = pl.ds(pl.multiple_of(to * 2 * GS, 16), 2 * GS)
        return send(
            gpart.at[g, rows], grecv.at[g, y], gss.at[g, s], grs.at[g, s], "frame", 4 * half + to
        )

    def gradient(g, mine, left, theirs, right):
        for r in range(0, GH, 128):
            part = dot(mine[:, r : r + 128], left[...], 0, 0)
            part += dot(theirs[:, r : r + 128], right[...], 0, 0)
            gpart[g, r : r + 128] = part.astype(BF)

        @pl.loop(1, 4)
        def _(s):
            g_copy(g, s).start()

        grecv[g, pl.ds(y, 1)] = gpart[g, pl.ds(pl.multiple_of(y * 2 * GS, 16), 2 * GS)][None]

    ta_copy.wait()
    tm_copy.wait()
    gradient(0, tasend.at[par], tmsend, tarecv, tmrecv)

    qkv_copy.wait()
    so_copy.wait()
    lane = lax.broadcasted_iota(jnp.int32, (1, 128), 1)
    keep = (lane < HD).astype(F32).astype(BF)
    zeros = jnp.zeros((ALL, 128 - HD), BF)
    for fr in range(FR):
        rows = qkv[fr].reshape(ALL, 256)
        qbuf[fr] = rows[:, :128] * keep
        k = rows[:, HD : HD + 128] * keep
        kbuf[fr] = k
        kt[fr] = k.T
        vbuf[fr] = jnp.concatenate([rows[:, 2 * HD : 3 * HD], zeros], axis=1)

    @pl.loop(1, NF)
    def _(s):
        u_copy(s).wait_recv()

    up[...] = dot(unperm[...], urecv[...].reshape(TT, D), 1, 0).astype(BF)

    sback = dot(up[...], so[...], 1, 0).reshape(FR, 3, GRP, D)
    for h in range(HEADS):
        bsend[:, h] = pack([lanes(sback[:, g], h) for g in range(3)])

    def b_copy(fr, s):
        to, dst = pos_peer(p, s, 1), p
        return send(bsend.at[fr, to], brecv.at[fr, dst], bss.at[fr, s], brs.at[fr, s], "pos", to)

    for fr in range(FR):

        @pl.loop(1, NP)
        def _(s):
            b_copy(fr, s).start()

    brecv[:, pl.ds(p, 1)] = bsend[:, pl.ds(p, 1)]
    order_copy.wait()
    for e in range(2):
        asend[e] = dot(up[...], order[e], 1, 0).astype(BF)
    a_copy = send(asend.at[1 - par], arecv, mss.at[3], mrs.at[3], "pos", mate)
    a_copy.start()
    a_copy.wait()
    m_copy.wait()
    gradient(1, asend.at[par], mixed, arecv, mrecv)

    def r_copy(fr, s):
        to = pos_peer(p, s, 1)
        return send(rsend.at[fr, to], rrecv.at[fr, p], rss.at[fr, s], rrs.at[fr, s], "pos", to)

    def h_copy(g, s):
        to = lax.rem(place + s, NP)
        return pltpu.make_async_remote_copy(
            src_ref=hsend.at[g, to],
            dst_ref=hrecv.at[g, place],
            send_sem=hss.at[g, s],
            recv_sem=hrs.at[g, s],
            device_id={"frame": 4 * (to // NK) + y, "pos": 2 * lax.rem(to, NK) + par},
        )

    def fold(g):
        @pl.loop(1, 4)
        def _(s):
            g_copy(g, s).wait_recv()

        total = grecv[g, 0].astype(F32)
        for s in range(1, 4):
            total += grecv[g, s].astype(F32)
        hsend[g] = dot(spread[...], total.astype(BF), 1, 0).astype(BF).reshape(NP, 16, D)

        @pl.loop(1, NP)
        def _(s):
            h_copy(g, s).start()

        hrecv[g, pl.ds(place, 1)] = hsend[g, pl.ds(place, 1)]

    for fr in range(FR):
        dk[...] = jnp.zeros_like(dk)
        dv[...] = jnp.zeros_like(dv)

        @pl.loop(1, NP)
        def _(s):
            b_copy(fr, s).wait_recv()

        got = brecv[fr]
        zeros = jnp.zeros((NP, GRP, 128 - HD), BF)
        for g in range(3):
            bbuf[:, g * GRP : (g + 1) * GRP] = jnp.concatenate([lanes(got, g), zeros], axis=-1)

        @pl.loop(0, ALL // BT)
        def _(t):
            at = pl.ds(pl.multiple_of(t * BT, BT), BT)
            q = qbuf[fr, at]
            b = bbuf.reshape(ALL, 128)[at]
            total = jnp.sum(b.astype(F32).T * att[fr, :, at], axis=0, keepdims=True)
            lse = stat[fr, 0:1, at]
            for k in range(0, ALL, KC):
                s = dot(kbuf[fr, k : k + KC], q, 1, 1)
                gp = dot(vbuf[fr, k : k + KC], b, 1, 1)
                prob = jnp.exp2(s * (SCALE * LOG2E) - lse)
                pbuf[k : k + KC] = prob.astype(BF)
                sbuf[k : k + KC] = (prob * (gp - total)).astype(BF)
            dv[...] += dot(pbuf[...], b, 1, 0)
            dk[...] += dot(sbuf[...], q, 1, 0)
            dq[at] = dot(kt[fr], sbuf[...], 1, 0).T

        val = pack([dq[:, :HD] * SCALE, dk[:, :HD] * SCALE, dv[:, :HD]])
        rsend[fr] = val.reshape(NP, PL, 256)

        @pl.loop(1, NP)
        def _(s):
            r_copy(fr, s).start()

        rrecv[fr, pl.ds(p, 1)] = rsend[fr, pl.ds(p, 1)]
        if fr == 0:
            fold(0)

    def finish_rows(fr):
        @pl.loop(1, NP)
        def _(s):
            r_copy(fr, s).wait_recv()

        got = [rrecv[fr, h].astype(F32) for h in range(HEADS)]
        grad_hat = jnp.zeros((PL, D), F32)
        for c in range(3):
            part = jnp.concatenate([lanes(v, c) for v in got], axis=1)
            grad_hat += dot(part.astype(BF), w[c], 1, 0)
        here = slice(fr * PL, (fr + 1) * PL)
        normed, inv = normalize(x[here])
        grad_out[here] = (up[here].astype(F32) + norm_back(grad_hat, normed, inv)).astype(BF)

    for c in w_copies:
        c.wait()
    finish_rows(0)
    fold(1)
    finish_rows(1)
    for g in range(2):

        @pl.loop(1, NP)
        def _(s):
            h_copy(g, s).wait_recv()

        total = hrecv[g, 0].astype(F32)
        for s in range(1, NP):
            total += hrecv[g, s].astype(F32)
        sums_out[g] = total

    @pl.loop(1, NP)
    def _(s):
        for fr in range(FR):
            b_copy(fr, s).wait_send()
            r_copy(fr, s).wait_send()
        for g in range(2):
            h_copy(g, s).wait_send()

    @pl.loop(1, NF)
    def _(s):
        u_copy(s).wait_send()

    @pl.loop(1, 4)
    def _(s):
        for g in range(2):
            g_copy(g, s).wait_send()


def rest(stream, cot, back, split, mask, unperm, spread, x, mixed, stat, att, order, tw, qkv, w, so):
    V = pltpu.VMEM
    sds = jax.ShapeDtypeStruct
    return pl.pallas_call(
        rest_kernel,
        out_shape=(sds((TOK, D), BF), sds((2, 16, D), F32)),
        in_specs=[vmem()] * 11 + [anywhere()] * 5,
        out_specs=(vmem(), vmem()),
        scratch_shapes=[
            V((3, D, D), BF), V((D, D), BF), V((2, D, GH), BF), V((TT, D), F32),
            V((3, TT, D), BF), V((TT, D), F32), V((HEADS, TT, TT), F32),
            V((3, TT, D), F32), V((NF, SLAB, D), BF), V((NF, SLAB, D), BF), V((TOK, D), BF),
            V((TT, GH), BF), V((TT, D), BF), V((TT, D), BF),
            V((2, TOK, GH), BF), V((TOK, GH), BF), V((TOK, D), BF),
            V((FR, NP, PL, 256), BF), V((FR, NP, GRP, 256), BF), V((FR, NP, GRP, 256), BF),
            V((2, GH, D), BF), V((2, 4, 2 * GS, D), BF),
            V((2, NP, 16, D), BF), V((2, NP, 16, D), BF),
            V((FR, ALL, 128), BF), V((FR, ALL, 128), BF), V((FR, ALL, 128), BF),
            V((NP, PL, 128), BF), V((FR, 128, ALL), BF),
            V((ALL, BT), BF), V((ALL, BT), BF),
            V((ALL, 128), F32), V((ALL, 128), F32), V((ALL, 128), F32),
            V((FR, NP, PL, 256), BF), V((FR, NP, PL, 256), BF),
            DMA((3,)), DMA, DMA, DMA, DMA((NF,)), DMA((NF,)), DMA((4,)), DMA((4,)),
            DMA((FR, NP)), DMA((FR, NP)), DMA((2, 4)), DMA((2, 4)),
            DMA((2, NP)), DMA((2, NP)), DMA((FR, NP)), DMA((FR, NP)),
        ],
        compiler_params=params(2),
    )(stream, cot, back, split, mask, unperm, spread, x, mixed, stat, att, order, tw, qkv, w, so)


def finish_kernel(grad, sums, grad_out, gs_out, gt_out):
    grad_out[...] = grad[...]
    gt_out[...] = sums[0, :GR]
    gs_out[...] = sums[1, :GR]


def finish(grad, sums):
    sds = jax.ShapeDtypeStruct
    return pl.pallas_call(
        finish_kernel,
        out_shape=(sds((TOK, D), BF), sds((GR, D), F32), sds((GR, D), F32)),
        in_specs=[vmem(), vmem()],
        out_specs=(vmem(), vmem(), vmem()),
    )(grad, sums)


def tables():
    row = np.arange(TT)
    slab, inner = row // SLAB, row % SLAB
    real = inner < FR * TP
    col = (inner // TP) * PL + slab * TP + inner % TP
    perm = (real[:, None] & (col[:, None] == np.arange(TOK)[None])).astype(np.float32)
    place = np.where(real, inner % TP, -1)
    mask = np.where(place[:, None] == place[None], 0.0, -1e30).astype(np.float32)
    row = np.arange(NP * 16)
    source = row // 16 // NK * GS + row // 16 % NK * GR + row % 16
    spread = (row % 16 < GR)[:, None] & (source[:, None] == np.arange(2 * GS)[None])
    col = np.arange(2 * GH)
    core, slab, inner = col // GH, col % GH // GS, col % GS
    frame = slab % 2 * 4 + slab // 2
    source = (frame * NP + 2 * (inner // GR) + core) * GR + inner % GR
    order = (inner < NK * GR)[None] & (np.arange(D)[:, None] == source[None])
    order = order.reshape(D, 2, GH).transpose(1, 0, 2)
    return [jnp.asarray(t.astype(np.float32), BF) for t in (perm, perm.T, spread, order)] + [
        jnp.asarray(mask)
    ]


def shards(inputs, cotangent, space_projection, space_output, time_projection, time_output):
    perm, unperm, spread, order, mask = tables()
    x = inputs.reshape(TOK, D)
    cot = cotangent.reshape(TOK, D)
    qkv, stat, att, mixed, stream_t, cot_t, back, split = space_forward(
        x, cot, perm, space_projection, space_output, time_output, order
    )
    grad, sums = rest(
        stream_t.reshape(TT, D), cot_t.reshape(TT, D), back, split, mask, unperm, spread, x, mixed,
        stat, att, order, time_projection, qkv, space_projection, space_output,
    )
    grad, gs, gt = finish(grad, sums)
    return grad.reshape(FR, PL, D), gs, gt


def solution(mesh):
    return jax.shard_map(
        shards,
        mesh=mesh,
        in_specs=(P("frame", "pos", None), P("frame", "pos", None), P(), P(), P(), P()),
        out_specs=(P("frame", "pos", None), P(("frame", "pos"), None), P(("frame", "pos"), None)),
        check_vma=False,
    )
```

```python
import jax
import jax.numpy as jnp
import numpy as np
from jax import lax
from jax.experimental import pallas as pl
from jax.experimental.pallas import tpu as pltpu
from jax.sharding import PartitionSpec as P

HEADS = 16
EPS = 1e-06
BF = jnp.bfloat16
F32 = jnp.float32
D = 1152
HD = 72
NP = 16
NF = 8
FR = 2
PL = 96
TOK = FR * PL
ALL = NP * PL
TP = PL // NF
SLAB = 32
TT = NF * SLAB
GR = D // NF // NP
NK = NP // 2
GS = 80
GH = NF * GS
GRP = PL // 3
SCALE = HD ** (-0.5)
LOG2E = 1.4426950408889634
QT = 384
BT = 256
KC = 256
LIMIT = 60 * 1024 * 1024


def dot(a, b, ca, cb):
    return lax.dot_general(a, b, (((ca,), (cb,)), ((), ())), preferred_element_type=F32)


def normalize(tokens):
    values = tokens.astype(F32)
    center = values - jnp.mean(values, axis=-1, keepdims=True)
    inv_std = lax.rsqrt(jnp.mean(center * center, axis=-1, keepdims=True) + EPS)
    return center * inv_std, inv_std


def norm_back(grad_hat, normed, inv_std):
    mean_grad = jnp.mean(grad_hat, axis=-1, keepdims=True)
    mean_proj = jnp.mean(grad_hat * normed, axis=-1, keepdims=True)
    return inv_std * (grad_hat - mean_grad - normed * mean_proj)


def pos_peer(p, s, sign):
    v = 7 - (s // 2 + 7) % 8
    x, z = lax.rem(p // 8 + v // 4, 2), lax.rem(lax.rem(p // 2, 4) + sign * (v % 4) + 4, 4)
    return 8 * x + 2 * z + lax.rem(lax.rem(p, 2) + s % 2, 2)


def pack(parts):
    shape = parts[0].shape[:-1] + (256 - 3 * HD,)
    return jnp.concatenate(list(parts) + [jnp.zeros(shape, F32)], axis=-1).astype(BF)


def lanes(value, g):
    return value[..., g * HD : (g + 1) * HD]


def greet(barrier, p, f, pos, frame):
    if pos:

        @pl.loop(1, NP)
        def _(s):
            pl.semaphore_signal(barrier, inc=1, device_id={"pos": lax.rem(p + s, NP)})

    if frame:

        @pl.loop(1, NF)
        def _(s):
            pl.semaphore_signal(barrier, inc=1, device_id={"frame": lax.rem(f + s, NF)})


def send(src, dst, send_sem, recv_sem, axis, dest):
    return pltpu.make_async_remote_copy(
        src_ref=src, dst_ref=dst, send_sem=send_sem, recv_sem=recv_sem, device_id={axis: dest}
    )


def space_forward_kernel(
    x, cot, perm, w_hbm, so_hbm, wo_hbm, order_hbm,
    qkv_out, stat_out, att_out, mixed_out, stream_out, cot_out, back_out, split_out,
    w, so, wo, order, hat, qsend, qkv, kbuf, qbuf, vt, sbuf, pbuf, osend, orecv, stream, fsend, frecv, csend, crecv,
    wsem, sosem, wosem, ordsem, qss, qrs, oss, ors, fss, frs, css, crs, outsem,
):
    p = lax.axis_index("pos")
    f = lax.axis_index("frame")
    par = lax.rem(p, 2)
    barrier = pltpu.get_barrier_semaphore()
    greet(barrier, p, f, True, True)

    def w_copy(i, c):
        pair = pos_peer(p, 2 * i, 1) // 2
        rows = pl.ds(pl.multiple_of(c * D + pair * 144, 16), 144)
        return pltpu.make_async_copy(w_hbm.at[rows], w.at[i, pl.ds(c * 144, 144)], wsem.at[i, c])

    for i in range(8):
        for c in range(3):
            w_copy(i, c).start()
    so_copy = pltpu.make_async_copy(so_hbm, so, sosem)
    wo_copy = pltpu.make_async_copy(wo_hbm, wo, wosem)
    order_copy = pltpu.make_async_copy(order_hbm, order, ordsem)
    hat[...] = normalize(x[...])[0].astype(BF)
    pl.semaphore_wait(barrier, NP - 1 + NF - 1)

    def q_copy(fr, s):
        return send(qsend.at[s, fr], qkv.at[fr, p], qss.at[fr, s], qrs.at[fr, s], "pos", pos_peer(p, s, 1))

    @pl.loop(0, 8)
    def _(i):
        for c in range(3):
            w_copy(i, c).wait()
        r = dot(hat[...], w[i], 1, 1)
        pad = jnp.zeros((TOK, 256 - 3 * HD), F32)
        for e in range(2):
            part = [r[:, c * 144 + e * HD : c * 144 + e * HD + HD] for c in range(3)]
            val = jnp.concatenate(part + [pad], axis=1).astype(BF)
            qsend[2 * i + lax.rem(par + e, 2)] = val.reshape(FR, PL, 256)

        @pl.when(i > 0)
        def _():
            q_copy(0, 2 * i).start()

        q_copy(0, 2 * i + 1).start()

    @pl.loop(1, NP)
    def _(s):
        q_copy(1, s).start()

    qkv[:, pl.ds(p, 1)] = qsend[0][:, None]
    for late in (so_copy, wo_copy, order_copy):
        late.start()

    def c_copy(s):
        to = lax.rem(f + s, NF)
        return send(csend.at[to], crecv.at[f], css.at[s], crs.at[s], "frame", to)

    csend[...] = dot(perm[...], cot[...], 1, 0).astype(BF).reshape(NF, SLAB, D)

    @pl.loop(1, NF)
    def _(s):
        c_copy(s).start()

    crecv[pl.ds(f, 1)] = csend[pl.ds(f, 1)]

    def o_copy(fr, s):
        to = lax.rem(p + s, NP)
        return send(osend.at[fr, to], orecv.at[fr, p], oss.at[fr, s], ors.at[fr, s], "pos", to)

    outs = []
    for fr in range(FR):

        @pl.loop(1, NP)
        def _(s):
            q_copy(fr, s).wait_recv()

        out = pltpu.make_async_copy(qkv.at[fr], qkv_out.at[fr], outsem.at[fr])
        out.start()
        outs.append(out)
        rows = qkv[fr].reshape(ALL, 256)
        lane = lax.broadcasted_iota(jnp.int32, (1, 128), 1)
        keep = (lane < HD).astype(F32).astype(BF)
        zeros = jnp.zeros((ALL, 128 - HD), BF)
        qbuf[...] = rows[:, :128] * keep
        kbuf[...] = rows[:, HD : HD + 128]
        vt[...] = jnp.concatenate([rows[:, 2 * HD : 3 * HD], zeros], axis=1).T

        @pl.loop(0, ALL // QT)
        def _(t):
            tile = lax.rem(p // 4 + ALL // QT - 1 - t, ALL // QT)
            at = pl.ds(pl.multiple_of(tile * QT, QT), QT)
            q = qbuf[at]
            top = jnp.full((8, QT), -jnp.inf, F32)
            for k in range(0, ALL, KC):
                s = dot(kbuf[k : k + KC], q, 1, 1)
                sbuf[k : k + KC] = s
                top = jnp.maximum(top, jnp.max(s.reshape(KC // 8, 8, QT), axis=0))
            top = jnp.max(top, axis=0, keepdims=True) * (SCALE * LOG2E)
            total = jnp.zeros((8, QT), F32)
            for k in range(0, ALL, KC):
                e = jnp.exp2(sbuf[k : k + KC] * (SCALE * LOG2E) - top)
                total = total + jnp.sum(e.reshape(KC // 8, 8, QT), axis=0)
                pbuf[k : k + KC] = e.astype(BF)
            total = jnp.sum(total, axis=0, keepdims=True)
            o = dot(vt[...], pbuf[...], 1, 0) * (1.0 / total)
            stat_out[fr, :, at] = jnp.broadcast_to(top + jnp.log(total) * LOG2E, (8, QT))
            att_out[fr, :, at] = o[:HD]
            turned = o.T.reshape(4, 3, GRP, 128)
            osend[fr, pl.ds(tile * 4, 4)] = pack([turned[:, g, :, :HD] for g in range(3)])
            for j in range(4):
                to = tile * 4 + j

                @pl.when(to != p)
                def _():
                    o_copy(fr, lax.rem(to - p + NP, NP)).start()

        orecv[fr, pl.ds(p, 1)] = osend[fr, pl.ds(p, 1)]

    so_copy.wait()
    for fr in range(FR):

        @pl.loop(1, NP)
        def _(s):
            o_copy(fr, s).wait_recv()

        got = [orecv[fr, h].astype(F32) for h in range(HEADS)]
        mixed = jnp.concatenate(
            [jnp.concatenate([lanes(v, g) for v in got], axis=1) for g in range(3)], axis=0
        ).astype(BF)
        part = slice(fr * PL, (fr + 1) * PL)
        mixed_out[part] = mixed
        stream[part] = (x[part].astype(F32) + dot(mixed, so[...], 1, 1)).astype(BF)

    def f_copy(s):
        to = lax.rem(f + s, NF)
        return send(fsend.at[to], frecv.at[f], fss.at[s], frs.at[s], "frame", to)

    fsend[...] = dot(perm[...], stream[...], 1, 0).astype(BF).reshape(NF, SLAB, D)

    @pl.loop(1, NF)
    def _(s):
        f_copy(s).start()

    frecv[pl.ds(f, 1)] = fsend[pl.ds(f, 1)]

    @pl.loop(1, NF)
    def _(s):
        c_copy(s).wait_recv()

    cot_out[...] = crecv[...]
    tcot = crecv[...].reshape(TT, D)
    wo_copy.wait()
    back_out[...] = dot(tcot, wo[...], 1, 0).astype(BF)
    order_copy.wait()
    for e in range(2):
        split_out[e] = dot(tcot, order[e], 1, 0).astype(BF)

    @pl.loop(1, NP)
    def _(s):
        for fr in range(FR):
            q_copy(fr, s).wait_send()
            o_copy(fr, s).wait_send()

    for out in outs:
        out.wait()

    @pl.loop(1, NF)
    def _(s):
        f_copy(s).wait_recv()

    stream_out[...] = frecv[...]

    @pl.loop(1, NF)
    def _(s):
        c_copy(s).wait_send()
        f_copy(s).wait_send()


def vmem():
    return pl.BlockSpec(memory_space=pltpu.VMEM)


def anywhere():
    return pl.BlockSpec(memory_space=pl.ANY)


DMA = pltpu.SemaphoreType.DMA


def params(collective_id):
    return pltpu.CompilerParams(
        collective_id=collective_id, has_side_effects=True, vmem_limit_bytes=LIMIT
    )


def space_forward(x, cot, perm, w, so, wo, order):
    V = pltpu.VMEM
    sds = jax.ShapeDtypeStruct
    return pl.pallas_call(
        space_forward_kernel,
        out_shape=(
            sds((FR, NP, PL, 256), BF),
            sds((FR, 8, ALL), F32),
            sds((FR, HD, ALL), F32),
            sds((TOK, D), BF),
            sds((NF, SLAB, D), BF),
            sds((NF, SLAB, D), BF),
            sds((TT, D), BF),
            sds((2, TT, GH), BF),
        ),
        in_specs=[vmem(), vmem(), vmem()] + [anywhere()] * 4,
        out_specs=(anywhere(),) + (vmem(),) * 7,
        scratch_shapes=[
            V((8, 432, D), BF), V((D, D), BF), V((D, D), BF), V((2, D, GH), BF), V((TOK, D), BF), V((NP, FR, PL, 256), BF),
            V((FR, NP, PL, 256), BF), V((ALL, 128), BF), V((ALL, 128), BF), V((128, ALL), BF),
            V((ALL, QT), F32), V((ALL, QT), BF),
            V((FR, NP, GRP, 256), BF), V((FR, NP, GRP, 256), BF), V((TOK, D), BF),
            V((NF, SLAB, D), BF), V((NF, SLAB, D), BF), V((NF, SLAB, D), BF), V((NF, SLAB, D), BF),
            DMA((8, 3)), DMA, DMA, DMA, DMA((FR, NP)), DMA((FR, NP)), DMA((FR, NP)), DMA((FR, NP)),
            DMA((NF,)), DMA((NF,)), DMA((NF,)), DMA((NF,)), DMA((FR,)),
        ],
        compiler_params=params(1),
    )(x, cot, perm, w, so, wo, order)


def rest_kernel(
    stream, cot, back, tasend, mask, unperm, spread, x, mixed, stat, att,
    order_hbm, tw_hbm, qkv_hbm, w_hbm, so_hbm,
    grad_out, sums_out,
    w, so, order, hat, tqkv, tmixed, probs, dqkv, usend, urecv, up,
    tarecv, tmsend, tmrecv, asend, arecv, mrecv,
    qkv, bsend, brecv, gpart, grecv, hsend, hrecv,
    qbuf, kbuf, vbuf, bbuf, kt, pbuf, sbuf, dq, dk, dv, rsend, rrecv,
    wsem, sosem, ordsem, qsem, uss, urs, mss, mrs, bss, brs, gss, grs, hss, hrs, rss, rrs,
):
    p = lax.axis_index("pos")
    f = lax.axis_index("frame")
    par = lax.rem(p, 2)
    chip = p // 2
    y, half = lax.rem(f, 4), f // 4
    place = NK * half + chip
    mate = p + 1 - 2 * par
    barrier = pltpu.get_barrier_semaphore()
    greet(barrier, p, f, True, True)

    @pl.loop(1, NK)
    def _(s):
        other = {"frame": 4 * (1 - half) + y, "pos": 2 * lax.rem(chip + s, NK) + par}
        pl.semaphore_signal(barrier, inc=1, device_id=other)

    tw_copies = [
        pltpu.make_async_copy(tw_hbm.at[pl.ds(c * D, D)], w.at[c], wsem.at[c]) for c in range(3)
    ]
    for c in tw_copies:
        c.start()
    order_copy = pltpu.make_async_copy(order_hbm, order, ordsem)
    so_copy = pltpu.make_async_copy(so_hbm, so, sosem)
    qkv_copy = pltpu.make_async_copy(qkv_hbm, qkv, qsem)

    normed, inv = normalize(stream[...])
    hat[...] = normed
    normed = normed.astype(BF)
    for c in range(3):
        tw_copies[c].wait()
        tqkv[c] = dot(normed, w[c], 1, 1).astype(BF)
    for late in (qkv_copy, so_copy, order_copy):
        late.start()
    tmixed[...] = jnp.zeros_like(tmixed)
    dqkv[...] = jnp.zeros_like(dqkv)

    def window(h):
        off = (h * HD) % 128
        start = h * HD - off
        width = 128 if off + HD <= 128 else 256
        lane = lax.broadcasted_iota(jnp.int32, (1, width), 1)
        keep = ((lane >= off) & (lane < off + HD)).astype(F32).astype(BF)
        return slice(start, start + width), keep

    for h in range(HEADS):
        win, keep = window(h)
        s = dot(tqkv[0, :, win] * keep, tqkv[1, :, win], 1, 1) * SCALE + mask[...]
        e = jnp.exp(s - jnp.max(s, axis=1, keepdims=True))
        prob = e * (1.0 / jnp.sum(e, axis=1, keepdims=True))
        probs[h] = prob
        tmixed[:, win] += dot(prob.astype(BF), tqkv[2, :, win] * keep, 1, 0)
    tmsend[...] = tmixed[...].astype(BF)
    pl.semaphore_wait(barrier, NP - 1 + NF - 1 + NK - 1)
    ta_copy = send(tasend.at[1 - par], tarecv, mss.at[0], mrs.at[0], "pos", mate)
    tm_copy = send(tmsend, tmrecv, mss.at[1], mrs.at[1], "pos", mate)
    m_copy = send(mixed, mrecv, mss.at[2], mrs.at[2], "pos", mate)
    ta_copy.start()
    tm_copy.start()
    m_copy.start()
    for h in range(HEADS):
        win, keep = window(h)
        k, q = tqkv[1, :, win] * keep, tqkv[0, :, win] * keep
        b = back[:, win] * keep
        prob = probs[h]
        gp = dot(b, tqkv[2, :, win], 1, 1)
        gs = prob * (gp - jnp.sum(prob * gp, axis=1, keepdims=True)) * SCALE
        gs = gs.astype(BF)
        dqkv[0, :, win] += dot(gs, k, 1, 0)
        dqkv[1, :, win] += dot(gs, q, 0, 0)
        dqkv[2, :, win] += dot(prob.astype(BF), b, 0, 0)
    grad_hat = dot(dqkv[0].astype(BF), w[0], 1, 0)
    for c in range(1, 3):
        grad_hat += dot(dqkv[c].astype(BF), w[c], 1, 0)
    turned = cot[...].astype(F32) + norm_back(grad_hat, hat[...], inv)
    usend[...] = turned.astype(BF).reshape(NF, SLAB, D)

    def u_copy(s):
        to = lax.rem(f + s, NF)
        return send(usend.at[to], urecv.at[f], uss.at[s], urs.at[s], "frame", to)

    @pl.loop(1, NF)
    def _(s):
        u_copy(s).start()

    urecv[pl.ds(f, 1)] = usend[pl.ds(f, 1)]

    w_copies = [
        pltpu.make_async_copy(w_hbm.at[pl.ds(c * D, D)], w.at[c], wsem.at[c]) for c in range(3)
    ]
    for c in w_copies:
        c.start()

    def g_copy(g, s):
        to = lax.rem(y + s, 4)
        rows = pl.ds(pl.multiple_of(to * 2 * GS, 16), 2 * GS)
        return send(
            gpart.at[g, rows], grecv.at[g, y], gss.at[g, s], grs.at[g, s], "frame", 4 * half + to
        )

    def gradient(g, mine, left, theirs, right):
        for r in range(0, GH, 128):
            part = dot(mine[:, r : r + 128], left[...], 0, 0)
            part += dot(theirs[:, r : r + 128], right[...], 0, 0)
            gpart[g, r : r + 128] = part.astype(BF)

        @pl.loop(1, 4)
        def _(s):
            g_copy(g, s).start()

        grecv[g, pl.ds(y, 1)] = gpart[g, pl.ds(pl.multiple_of(y * 2 * GS, 16), 2 * GS)][None]

    ta_copy.wait()
    tm_copy.wait()
    gradient(0, tasend.at[par], tmsend, tarecv, tmrecv)

    qkv_copy.wait()
    so_copy.wait()
    lane = lax.broadcasted_iota(jnp.int32, (1, 128), 1)
    keep = (lane < HD).astype(F32).astype(BF)
    zeros = jnp.zeros((ALL, 128 - HD), BF)
    for fr in range(FR):
        rows = qkv[fr].reshape(ALL, 256)
        qbuf[fr] = rows[:, :128] * keep
        k = rows[:, HD : HD + 128] * keep
        kbuf[fr] = k
        kt[fr] = k.T
        vbuf[fr] = jnp.concatenate([rows[:, 2 * HD : 3 * HD], zeros], axis=1)

    @pl.loop(1, NF)
    def _(s):
        u_copy(s).wait_recv()

    up[...] = dot(unperm[...], urecv[...].reshape(TT, D), 1, 0).astype(BF)

    sback = dot(up[...], so[...], 1, 0).reshape(FR, 3, GRP, D)
    for h in range(HEADS):
        bsend[:, h] = pack([lanes(sback[:, g], h) for g in range(3)])

    def b_copy(fr, s):
        to, dst = pos_peer(p, s, 1), p
        return send(bsend.at[fr, to], brecv.at[fr, dst], bss.at[fr, s], brs.at[fr, s], "pos", to)

    for fr in range(FR):

        @pl.loop(1, NP)
        def _(s):
            b_copy(fr, s).start()

    brecv[:, pl.ds(p, 1)] = bsend[:, pl.ds(p, 1)]
    order_copy.wait()
    for e in range(2):
        asend[e] = dot(up[...], order[e], 1, 0).astype(BF)
    a_copy = send(asend.at[1 - par], arecv, mss.at[3], mrs.at[3], "pos", mate)
    a_copy.start()
    a_copy.wait()
    m_copy.wait()
    gradient(1, asend.at[par], mixed, arecv, mrecv)

    def r_copy(fr, s):
        to = pos_peer(p, s, 1)
        return send(rsend.at[fr, to], rrecv.at[fr, p], rss.at[fr, s], rrs.at[fr, s], "pos", to)

    def h_copy(g, s):
        to = lax.rem(place + s, NP)
        return pltpu.make_async_remote_copy(
            src_ref=hsend.at[g, to],
            dst_ref=hrecv.at[g, place],
            send_sem=hss.at[g, s],
            recv_sem=hrs.at[g, s],
            device_id={"frame": 4 * (to // NK) + y, "pos": 2 * lax.rem(to, NK) + par},
        )

    def fold(g):
        @pl.loop(1, 4)
        def _(s):
            g_copy(g, s).wait_recv()

        total = grecv[g, 0].astype(F32)
        for s in range(1, 4):
            total += grecv[g, s].astype(F32)
        hsend[g] = dot(spread[...], total.astype(BF), 1, 0).astype(BF).reshape(NP, 16, D)

        @pl.loop(1, NP)
        def _(s):
            h_copy(g, s).start()

        hrecv[g, pl.ds(place, 1)] = hsend[g, pl.ds(place, 1)]

    for fr in range(FR):
        dk[...] = jnp.zeros_like(dk)
        dv[...] = jnp.zeros_like(dv)

        @pl.loop(1, NP)
        def _(s):
            b_copy(fr, s).wait_recv()

        got = brecv[fr]
        zeros = jnp.zeros((NP, GRP, 128 - HD), BF)
        for g in range(3):
            bbuf[:, g * GRP : (g + 1) * GRP] = jnp.concatenate([lanes(got, g), zeros], axis=-1)

        @pl.loop(0, ALL // BT)
        def _(t):
            at = pl.ds(pl.multiple_of(t * BT, BT), BT)
            q = qbuf[fr, at]
            b = bbuf.reshape(ALL, 128)[at]
            total = jnp.sum(b.astype(F32).T[:HD] * att[fr, :, at], axis=0, keepdims=True)
            lse = stat[fr, 0:1, at]
            for k in range(0, ALL, KC):
                s = dot(kbuf[fr, k : k + KC], q, 1, 1)
                gp = dot(vbuf[fr, k : k + KC], b, 1, 1)
                prob = jnp.exp2(s * (SCALE * LOG2E) - lse)
                pbuf[k : k + KC] = prob.astype(BF)
                sbuf[k : k + KC] = (prob * (gp - total)).astype(BF)
            dv[...] += dot(pbuf[...], b, 1, 0)
            dk[...] += dot(sbuf[...], q, 1, 0)
            dq[at] = dot(kt[fr], sbuf[...], 1, 0).T

        val = pack([dq[:, :HD] * SCALE, dk[:, :HD] * SCALE, dv[:, :HD]])
        rsend[fr] = val.reshape(NP, PL, 256)

        @pl.loop(1, NP)
        def _(s):
            r_copy(fr, s).start()

        rrecv[fr, pl.ds(p, 1)] = rsend[fr, pl.ds(p, 1)]
        if fr == 0:
            fold(0)

    def finish_rows(fr):
        @pl.loop(1, NP)
        def _(s):
            r_copy(fr, s).wait_recv()

        got = [rrecv[fr, h].astype(F32) for h in range(HEADS)]
        grad_hat = jnp.zeros((PL, D), F32)
        for c in range(3):
            part = jnp.concatenate([lanes(v, c) for v in got], axis=1)
            grad_hat += dot(part.astype(BF), w[c], 1, 0)
        here = slice(fr * PL, (fr + 1) * PL)
        normed, inv = normalize(x[here])
        grad_out[here] = (up[here].astype(F32) + norm_back(grad_hat, normed, inv)).astype(BF)

    for c in w_copies:
        c.wait()
    finish_rows(0)
    fold(1)
    finish_rows(1)
    for g in range(2):

        @pl.loop(1, NP)
        def _(s):
            h_copy(g, s).wait_recv()

        total = hrecv[g, 0].astype(F32)
        for s in range(1, NP):
            total += hrecv[g, s].astype(F32)
        sums_out[g] = total

    @pl.loop(1, NP)
    def _(s):
        for fr in range(FR):
            b_copy(fr, s).wait_send()
            r_copy(fr, s).wait_send()
        for g in range(2):
            h_copy(g, s).wait_send()

    @pl.loop(1, NF)
    def _(s):
        u_copy(s).wait_send()

    @pl.loop(1, 4)
    def _(s):
        for g in range(2):
            g_copy(g, s).wait_send()


def rest(stream, cot, back, split, mask, unperm, spread, x, mixed, stat, att, order, tw, qkv, w, so):
    V = pltpu.VMEM
    sds = jax.ShapeDtypeStruct
    return pl.pallas_call(
        rest_kernel,
        out_shape=(sds((TOK, D), BF), sds((2, 16, D), F32)),
        in_specs=[vmem()] * 11 + [anywhere()] * 5,
        out_specs=(vmem(), vmem()),
        scratch_shapes=[
            V((3, D, D), BF), V((D, D), BF), V((2, D, GH), BF), V((TT, D), F32),
            V((3, TT, D), BF), V((TT, D), F32), V((HEADS, TT, TT), F32),
            V((3, TT, D), F32), V((NF, SLAB, D), BF), V((NF, SLAB, D), BF), V((TOK, D), BF),
            V((TT, GH), BF), V((TT, D), BF), V((TT, D), BF),
            V((2, TOK, GH), BF), V((TOK, GH), BF), V((TOK, D), BF),
            V((FR, NP, PL, 256), BF), V((FR, NP, GRP, 256), BF), V((FR, NP, GRP, 256), BF),
            V((2, GH, D), BF), V((2, 4, 2 * GS, D), BF),
            V((2, NP, 16, D), BF), V((2, NP, 16, D), BF),
            V((FR, ALL, 128), BF), V((FR, ALL, 128), BF), V((FR, ALL, 128), BF),
            V((NP, PL, 128), BF), V((FR, 128, ALL), BF),
            V((ALL, BT), BF), V((ALL, BT), BF),
            V((ALL, 128), F32), V((ALL, 128), F32), V((ALL, 128), F32),
            V((FR, NP, PL, 256), BF), V((FR, NP, PL, 256), BF),
            DMA((3,)), DMA, DMA, DMA, DMA((NF,)), DMA((NF,)), DMA((4,)), DMA((4,)),
            DMA((FR, NP)), DMA((FR, NP)), DMA((2, 4)), DMA((2, 4)),
            DMA((2, NP)), DMA((2, NP)), DMA((FR, NP)), DMA((FR, NP)),
        ],
        compiler_params=params(2),
    )(stream, cot, back, split, mask, unperm, spread, x, mixed, stat, att, order, tw, qkv, w, so)


def finish_kernel(grad, sums, grad_out, gs_out, gt_out):
    grad_out[...] = grad[...]
    gt_out[...] = sums[0, :GR]
    gs_out[...] = sums[1, :GR]


def finish(grad, sums):
    sds = jax.ShapeDtypeStruct
    return pl.pallas_call(
        finish_kernel,
        out_shape=(sds((TOK, D), BF), sds((GR, D), F32), sds((GR, D), F32)),
        in_specs=[vmem(), vmem()],
        out_specs=(vmem(), vmem(), vmem()),
    )(grad, sums)


def tables():
    row = np.arange(TT)
    slab, inner = row // SLAB, row % SLAB
    real = inner < FR * TP
    col = (inner // TP) * PL + slab * TP + inner % TP
    perm = (real[:, None] & (col[:, None] == np.arange(TOK)[None])).astype(np.float32)
    place = np.where(real, inner % TP, -1)
    mask = np.where(place[:, None] == place[None], 0.0, -1e30).astype(np.float32)
    row = np.arange(NP * 16)
    source = row // 16 // NK * GS + row // 16 % NK * GR + row % 16
    spread = (row % 16 < GR)[:, None] & (source[:, None] == np.arange(2 * GS)[None])
    col = np.arange(2 * GH)
    core, slab, inner = col // GH, col % GH // GS, col % GS
    frame = slab % 2 * 4 + slab // 2
    source = (frame * NP + 2 * (inner // GR) + core) * GR + inner % GR
    order = (inner < NK * GR)[None] & (np.arange(D)[:, None] == source[None])
    order = order.reshape(D, 2, GH).transpose(1, 0, 2)
    return [jnp.asarray(t.astype(np.float32), BF) for t in (perm, perm.T, spread, order)] + [
        jnp.asarray(mask)
    ]


def shards(inputs, cotangent, space_projection, space_output, time_projection, time_output):
    perm, unperm, spread, order, mask = tables()
    x = inputs.reshape(TOK, D)
    cot = cotangent.reshape(TOK, D)
    qkv, stat, att, mixed, stream_t, cot_t, back, split = space_forward(
        x, cot, perm, space_projection, space_output, time_output, order
    )
    grad, sums = rest(
        stream_t.reshape(TT, D), cot_t.reshape(TT, D), back, split, mask, unperm, spread, x, mixed,
        stat, att, order, time_projection, qkv, space_projection, space_output,
    )
    grad, gs, gt = finish(grad, sums)
    return grad.reshape(FR, PL, D), gs, gt


def solution(mesh):
    return jax.shard_map(
        shards,
        mesh=mesh,
        in_specs=(P("frame", "pos", None), P("frame", "pos", None), P(), P(), P(), P()),
        out_specs=(P("frame", "pos", None), P(("frame", "pos"), None), P(("frame", "pos"), None)),
        check_vma=False,
    )
```
